128 devices in a mesh: dp: 64 (over z, x_lo, y, core), fsdp: 2 (over x_hi).
Axes of the slice: x: 4 (x_hi: 2, x_lo: 2; x = x_hi * 2 + x_lo), y: 4, z: 4, core: 2. Of those that a mesh axis runs over, the one named last changes fastest.
Arguments:
- latents: bfloat16 [64, 256, 1280], P('dp'), may hold values from -6 to 6
- script_ids: int32 [64], P('dp'), may hold values from 0 to 15
- gain_table: bfloat16 [1280, 16], P(('dp', 'fsdp')), may hold values from 0.099609375 to 1.8984375
- bias_one: bfloat16 [1280], P(('dp', 'fsdp')), may hold values from -2.390625 to 2.390625
- w_qkv: bfloat16 [1280, 3840], P(('dp', 'fsdp')), may hold values from -0.15625 to 0.15625
- w_out: bfloat16 [1280, 1280], P(('dp', 'fsdp')), may hold values from -0.625 to 0.625
- gain_two: bfloat16 [1280], P(('dp', 'fsdp')), may hold values from 0.099609375 to 1.8984375
- bias_two: bfloat16 [1280], P(('dp', 'fsdp')), may hold values from -2.390625 to 2.390625
- w_up: bfloat16 [1280, 1280], P(('dp', 'fsdp')), may hold values from -0.15625 to 0.15625
- w_down: bfloat16 [1280, 1280], P(('dp', 'fsdp')), may hold values from -0.25 to 0.25
- cotangent: bfloat16 [64, 256, 1280], P('dp'), may hold values from -6 to 6
Outputs:
- latents_out: bfloat16 [64, 256, 1280], P('dp')
- input_grad: float32 [64, 256, 1280], P('dp')
- gain_table_grad: float32 [1280, 16], P(('dp', 'fsdp'))
- bias_one_grad: float32 [1280], P(('dp', 'fsdp'))
- w_qkv_grad: float32 [1280, 3840], P(('dp', 'fsdp'))
- w_out_grad: float32 [1280, 1280], P(('dp', 'fsdp'))
- gain_two_grad: float32 [1280], P(('dp', 'fsdp'))
- bias_two_grad: float32 [1280], P(('dp', 'fsdp'))
- w_up_grad: float32 [1280, 1280], P(('dp', 'fsdp'))
- w_down_grad: float32 [1280, 1280], P(('dp', 'fsdp'))
The draws below stay inside these ranges and needn't reach their ends.
All inputs are finite; a program needn't handle non-finite values.
Results may differ from the reference program's by a relative error of at most 0.012.
Values may be sent and summed in bfloat16 or wider, within the bound.
A program may use at most 256 MiB of HBM per device.

```python
import math
import jax
import jax.numpy as jnp
from jax import lax

HEADS = 8
HEAD_DIM = 160
D = 1280
FF = 1280
LAT = 256
SCRIPTS = 16
ITEMS = 64


def touch_ends(entries, stream_key, low, top_value):
    index_at = [jax.random.randint(jax.random.fold_in(stream_key, axis), (), 0, length) for axis, length in enumerate(entries.shape)]
    main_axis = entries.shape.index(max(entries.shape))
    beside = index_at[:main_axis] + [(index_at[main_axis] + 1) % entries.shape[main_axis]] + index_at[main_axis + 1:]
    return entries.at[tuple(index_at)].set(low).at[tuple(beside)].set(top_value)


def block_scale(own_key, extent, cuts, least, high):
    def one(position, blocks):
        draws = jax.random.uniform(jax.random.fold_in(jax.random.fold_in(own_key, 6), position), (blocks,), jnp.float32, least / len(cuts), high / len(cuts))
        return jnp.repeat(jnp.exp(draws), extent[position] // blocks).reshape((-1,) + (1,) * (len(extent) - position - 1))

    level = one(*cuts[0])
    for cut in cuts[1:]:
        level = level * one(*cut)
    return level


def scatter_about(key, dims, spread, most, shards=(), kind=jnp.bfloat16):
    array = spread * jax.random.normal(key, dims, jnp.float32)
    if shards:
        array = array * block_scale(key, dims, shards, -0.22, 0.18)
    return jnp.clip(array, -most, most).astype(kind)


def setup_inputs(seed: int = 0) -> dict:
    seeds = jax.random.split(jax.random.key(seed), 12)
    latents = scatter_about(seeds[0], (ITEMS, LAT, D), 1.0, 6.0, ((0, 64),))
    script_ids = touch_ends(jax.random.randint(seeds[1], (ITEMS,), 0, SCRIPTS), jax.random.fold_in(seeds[1], 1), 0, SCRIPTS - 1).astype(jnp.int32)
    gain_table = jnp.clip(1.0 + 0.18 * jax.random.normal(seeds[2], (D, SCRIPTS), jnp.float32), 0.099609375, 1.8984375).astype(jnp.bfloat16)
    bias_one = scatter_about(seeds[3], (D,), 0.4, 2.390625, ((0, 128),))
    w_qkv = scatter_about(seeds[4], (D, 3 * D), D ** -0.5, 0.15625, ((0, 128),))
    w_out = scatter_about(seeds[5], (D, D), (D // 16) ** -0.5, 0.625, ((0, 128),))
    gain_two = jnp.clip(1.0 + 0.18 * jax.random.normal(seeds[6], (D,), jnp.float32), 0.099609375, 1.8984375).astype(jnp.bfloat16)
    bias_two = scatter_about(seeds[7], (D,), 0.4, 2.390625, ((0, 128),))
    w_up = scatter_about(seeds[8], (D, FF), D ** -0.5, 0.15625, ((0, 128),))
    w_down = scatter_about(seeds[9], (FF, D), (FF // 2) ** -0.5, 0.25, ((0, 128),))
    cotangent = scatter_about(seeds[10], (ITEMS, LAT, D), 1.0, 6.0, ((0, 64),))
    return {"latents": latents, "script_ids": script_ids, "gain_table": gain_table, "bias_one": bias_one, "w_qkv": w_qkv, "w_out": w_out, "gain_two": gain_two, "bias_two": bias_two, "w_up": w_up, "w_down": w_down, "cotangent": cotangent}


EPSILON = 1e-05
PRECISE = lax.Precision.HIGHEST

@jax.custom_vjp
def low(v):
    return lax.optimization_barrier(v.astype(jnp.bfloat16)).astype(jnp.float32)

@jax.custom_vjp
def low_back(v):
    return v

def low_keep(v):
    return (low(v), None)

def low_pass(kept, grad):
    return (grad,)

def back_keep(v):
    return (v, None)

def back_low(kept, grad):
    return (low(grad),)
low.defvjp(low_keep, low_pass)
low_back.defvjp(back_keep, back_low)

def layer_norm(inputs):
    average = lax.optimization_barrier(jnp.mean(inputs, axis=-1, keepdims=True))
    centered = inputs - average
    variance = lax.optimization_barrier(jnp.mean(centered * centered, axis=-1, keepdims=True))
    return centered * lax.rsqrt(variance + EPSILON)

def project(left, right):
    return jnp.einsum('gsd,de->gse', left, right, precision=PRECISE)

def forward(inputs, one_hot, gain_table, bias_one, w_qkv, w_out, gain_two, bias_two, w_up, w_down):
    groups, length, width = inputs.shape
    score_scale = 1.0 / math.sqrt(HEAD_DIM)
    gains = jnp.einsum('gc,dc->gd', one_hot, gain_table, precision=PRECISE)
    first = low(layer_norm(inputs) * gains[:, None, :] + bias_one)
    projected = low(low_back(project(first, w_qkv)))
    split = projected.reshape(groups, length, 3, HEADS, HEAD_DIM)
    queries = split[:, :, 0]
    key_rows = split[:, :, 1]
    values = split[:, :, 2]
    scores = low_back(jnp.einsum('gshe,gthe->ghst', queries, key_rows, precision=PRECISE) * score_scale)
    probs = low(jax.nn.softmax(scores, axis=-1))
    mixed = jnp.einsum('ghst,gthe->gshe', probs, values, precision=PRECISE).reshape(groups, length, width)
    mixed = low(low_back(mixed))
    middle = inputs + low_back(project(mixed, w_out))
    second = low(layer_norm(middle) * gain_two + bias_two)
    upper = low_back(project(second, w_up))
    active = low(jax.nn.gelu(upper))
    return middle + low_back(project(active, w_down))

def reference(latents, script_ids, gain_table, bias_one, w_qkv, w_out, gain_two, bias_two, w_up, w_down, cotangent):
    weights = tuple((item.astype(jnp.float32) for item in (gain_table, bias_one, w_qkv, w_out, gain_two, bias_two, w_up, w_down)))
    group_size = math.gcd(ITEMS, 16)
    count = ITEMS // group_size
    one_hot = (script_ids[:, None] == jnp.arange(SCRIPTS, dtype=jnp.int32)[None, :]).astype(jnp.float32)
    latent_groups = latents.reshape(count, group_size, LAT, D)
    hot_groups = one_hot.reshape(count, group_size, SCRIPTS)
    cot_groups = cotangent.reshape(count, group_size, LAT, D)

    def step(totals, batch):
        latent_block, hot_block, cot_block = batch
        output, back = jax.vjp(lambda inputs, *params: forward(inputs, hot_block, *params), latent_block.astype(jnp.float32), *weights)
        grads = back(cot_block.astype(jnp.float32))
        totals = tuple((total + grad for total, grad in zip(totals, grads[1:])))
        return (totals, (output.astype(jnp.bfloat16), grads[0]))
    zeros = tuple((jnp.zeros(item.shape, jnp.float32) for item in weights))
    totals, (outputs, input_grads) = lax.scan(step, zeros, (latent_groups, hot_groups, cot_groups))
    latents_out = outputs.reshape(ITEMS, LAT, D)
    input_grad = input_grads.reshape(ITEMS, LAT, D)
    return (latents_out, input_grad, totals[0], totals[1], totals[2], totals[3], totals[4], totals[5], totals[6], totals[7])
```

```python
import math

import jax
import jax.numpy as jnp
from jax import lax
from jax.sharding import PartitionSpec as P

from jax.experimental import pallas as pl
from jax.experimental.pallas import tpu as pltpu

HEADS = 8


EPSILON = 1e-05
PRECISE = lax.Precision.HIGHEST


def in_one_piece(arrays, axis, dim, along):
    widths = [a.shape[along] for a in arrays]
    both = jnp.concatenate(arrays, axis=along)
    whole = lax.all_gather(both, axis, axis=dim, tiled=True)
    return tuple(jnp.split(whole, [sum(widths[:k]) for k in range(1, len(widths))], axis=along))


MESH = pl.DeviceIdType.MESH
CW = 640

class Pos:
    def __init__(s):
        dp = lax.axis_index("dp"); s.xh = lax.axis_index("fsdp")
        s.c = dp % 2; s.y = (dp // 2) % 4; s.xl = (dp // 8) % 2; s.z = dp // 16
        s.x = s.xh * 2 + s.xl; s.h = s.y // 2; s.par = s.y % 2
    def dev(s, x=None, y=None, z=None, c=None):
        x = s.x if x is None else x; y = s.y if y is None else y
        z = s.z if z is None else z; c = s.c if c is None else c
        return (((z * 2 + x % 2) * 4 + y) * 2 + c, x // 2)
    def ring(s, ax, d):
        if ax == 0: return s.dev(x=(s.x + d) % 4)
        if ax == 1: return s.dev(y=(s.y + d) % 4)
        return s.dev(z=(s.z + d) % 4)
    def coord(s, ax, d):
        return ((s.x, s.y, s.z)[ax] + d) % 4

class AG:

    def __init__(s, p, W, stg, pieces, ssem, rsem, sib_r, s0s, s0r):
        s.p, s.W, s.stg, s.pieces = p, W, stg, pieces
        s.ssem, s.rsem, s.s0s, s.s0r = ssem, rsem, s0s, s0r
    def partners(s):
        p = s.p
        out = []
        for ax in range(3):
            for d in (1, 2, 3): out.append(p.ring(ax, d))
        for dy in (0, 1):
            for dx in (0, 1):
                for dc in (0, 1):
                    if (dy, dx, dc) == (0, 0, 0): continue
                    if (dy, dx, dc) == (0, 1, 0): continue
                    y = p.y ^ dy if dy else p.y
                    x = (p.x + 2 * dx) % 4
                    out.append(p.dev(x=x, y=y, c=(p.c + dc) % 2))
        return out
    def s0_targets(s):
        p = s.p
        res = []
        for dy in (0, 1):
            for dx in (0, 1):
                y = p.y ^ dy if dy else p.y
                x = (p.x + 2 * dx) % 4
                res.append((dy, dx, y, x))
        return res
    def s0_src(s):
        p = s.p
        return (p.par * 2 + p.c) * 2 + p.xh
    def s0(s, ph, act):
        p = s.p; o = s.s0_src()
        for tc in (0, 1):
            cond = (o <= 4) if tc == 0 else (o >= 4)
            @pl.when(cond)
            def _(tc=tc):
                for i, (dy, dx, y, x) in enumerate(s.s0_targets()):
                    chunk = (x // 2) * 2 + y % 2
                    src = s.pieces.at[ph, chunk]
                    dst = s.stg.at[ph, o - 4 * tc]
                    if dy == 0 and dx == 0:
                        @pl.when(p.c == tc)
                        def _():
                            cp = pltpu.make_async_copy(src, dst, s.s0r.at[ph, o - 4 * tc])
                            if act == 'start': cp.start()
                        @pl.when(p.c != tc)
                        def _():
                            cp = pltpu.make_async_remote_copy(src, dst, s.s0s.at[ph, i * 2 + tc], s.s0r.at[ph, o - 4 * tc], device_id=p.dev(y=y, x=x, c=tc), device_id_type=MESH)
                            if act == 'start': cp.start()
                            else: cp.wait_send()
                    else:
                        cp = pltpu.make_async_remote_copy(src, dst, s.s0s.at[ph, i * 2 + tc], s.s0r.at[ph, o - 4 * tc], device_id=p.dev(y=y, x=x, c=tc), device_id_type=MESH)
                        if act == 'start': cp.start()
                        else: cp.wait_send()
    def s0_recv(s, ph):
        p = s.p
        for k in range(5):
            def w(k=k):
                pltpu.make_async_copy(s.pieces.at[ph, 0], s.stg.at[ph, k], s.s0r.at[ph, k]).wait()
            if k < 4: w()
            else: pl.when(p.c == 0)(w)
    def compact(s, ph):
        p = s.p
        i = lax.broadcasted_iota(jnp.int32, (48, 80), 0)
        k = lax.broadcasted_iota(jnp.int32, (48, 80), 1)
        r = 48 * p.c + i
        q = (r * 205) >> 11
        col = (q - 4 * p.c) * 16 + (r - q * 10)
        P = jnp.where(k == col, 1.0, 0.0).astype(jnp.bfloat16)
        res = jnp.dot(P, s.stg[ph].reshape(80, CW), preferred_element_type=jnp.float32).astype(jnp.bfloat16)
        def put(ts):
            s.W[ph, p.xh, p.par, p.z, p.xl, p.h, 3 * p.c + ts] = res[ts * 16:(ts + 1) * 16]
        put(0); put(1)
        pl.when(p.c == 0)(lambda: put(2))
    def order(s, ph, ts):
        a = (ph + ts) % 3
        return ((a + 1) % 3, (a + 2) % 3, a)
    def region(s, ph, t, full, over=None):
        p = s.p; o = over or {}
        x = o.get(0); y = o.get(1); z = o.get(2)
        xh, xl = (p.xh, p.xl) if x is None else (x // 2, x % 2)
        h, par = (p.h, p.par) if y is None else (y // 2, y % 2)
        zz = p.z if z is None else z
        if 0 in full: xh = xl = slice(None)
        if 1 in full: h = par = slice(None)
        if 2 in full: zz = slice(None)
        return [ph, xh, par, zz, xl, h, t]
    def ref(s, reg): return s.W.at[tuple(reg)]
    def cp(s, reg, slot, k, dev):
        r = s.ref(reg)
        return pltpu.make_async_remote_copy(r, r, s.ssem.at[slot, k], s.rsem.at[slot, k], device_id=dev, device_id_type=MESH)
    def half(s, reg, full, hf):
        reg = list(reg)
        i = 3 if 2 in full else (1 if 0 in full else 2)
        reg[i] = pl.ds(hf * 2, 2) if i == 3 else pl.ds(hf, 1)
        return reg
    def slot(s, ph, ts): return ph * 3 + ts
    def t(s, ts): return 3 * s.p.c + ts
    def g(s, ts, f):
        if ts < 2: f()
        else: pl.when(s.p.c == 0)(f)
    def direct(s, stage, ph, ts, act):
        a = s.order(ph, ts); full = a[:stage]; ax = a[stage]
        for d in (1, 3, 2):
            k = stage * 3 + d - 1
            if act == 'recv':
                s.cp(s.region(ph, s.t(ts), full, {ax: s.p.coord(ax, -d)}), s.slot(ph, ts), k, s.p.ring(ax, d)).wait_recv()
            else:
                c = s.cp(s.region(ph, s.t(ts), full), s.slot(ph, ts), k, s.p.ring(ax, d))
                c.start() if act == 'start' else c.wait_send()
    def s3(s, ph, ts, what, act):
        a = s.order(ph, ts); full = a[:2]; ax = a[2]; sl = s.slot(ph, ts); tt = s.t(ts)
        R, L = s.p.ring(ax, 1), s.p.ring(ax, 3)
        own = s.region(ph, tt, full)
        fl = s.region(ph, tt, full, {ax: s.p.coord(ax, -1)})
        fr = s.region(ph, tt, full, {ax: s.p.coord(ax, 1)})
        op = s.region(ph, tt, full, {ax: s.p.coord(ax, 2)})
        if what == 'own':
            if act == 'recvL': s.cp(fl, sl, 6, R).wait_recv()
            elif act == 'recvR': s.cp(fr, sl, 7, L).wait_recv()
            else:
                for reg, k, dv in ((own, 6, R), (own, 7, L)):
                    c = s.cp(reg, sl, k, dv)
                    c.start() if act == 'start' else c.wait_send()
        elif what == 'fwdR':
            if act == 'recv': s.cp(s.half(op, full, 0), sl, 8, R).wait_recv()
            else:
                c = s.cp(s.half(fl, full, 0), sl, 8, R)
                c.start() if act == 'start' else c.wait_send()
        elif what == 'fwdL':
            if act == 'recv': s.cp(s.half(op, full, 1), sl, 9, L).wait_recv()
            else:
                c = s.cp(s.half(fr, full, 1), sl, 9, L)
                c.start() if act == 'start' else c.wait_send()
    def sib(s, ph, ts, piece, act):
        a = s.order(ph, ts); full = a[:2]; ax = a[2]
        d = (0, -1, 1, 2)[piece]
        dv = s.p.dev(c=1 - s.p.c)
        t = s.t(ts) if act != 'recv' else 3 * (1 - s.p.c) + ts
        c = s.cp(s.region(ph, t, full, {ax: s.p.coord(ax, d)}), s.slot(ph, ts), 10 + piece, dv)
        if act == 'start': c.start()
        elif act == 'recv': c.wait_recv()
        else: c.wait_send()
    def go(s, ts, f, other=False):
        def h():
            f()
        if ts < 2: h()
        else: pl.when(s.p.c == (1 if other else 0))(h)
    def phase_a(s, ph):
        for ts in range(3): s.go(ts, lambda ts=ts: s.direct(0, ph, ts, 'start'))
    def phase_b(s, ph):
        for ts in range(3):
            s.go(ts, lambda ts=ts: (s.direct(0, ph, ts, 'recv'), s.direct(1, ph, ts, 'start')))
    def phase_c(s, ph):
        for ts in range(3):
            s.go(ts, lambda ts=ts: (s.direct(1, ph, ts, 'recv'), s.s3(ph, ts, 'own', 'start'), s.sib(ph, ts, 0, 'start')))
    def phase_d(s, ph):
        for ts in range(3):
            s.go(ts, lambda ts=ts: (
                s.s3(ph, ts, 'own', 'recvL'), s.s3(ph, ts, 'fwdR', 'start'), s.sib(ph, ts, 1, 'start'),
                s.s3(ph, ts, 'own', 'recvR'), s.s3(ph, ts, 'fwdL', 'start'), s.sib(ph, ts, 2, 'start')))
    def phase_e(s, ph):
        for ts in range(3):
            s.go(ts, lambda ts=ts: (s.s3(ph, ts, 'fwdR', 'recv'), s.s3(ph, ts, 'fwdL', 'recv'), s.sib(ph, ts, 3, 'start')))
    def phase_f(s, ph):
        for ts in range(3):
            s.go(ts, lambda ts=ts: [s.sib(ph, ts, k, 'recv') for k in range(4)], other=True)
    def drain(s, ph):
        s.s0(ph, 'wait_send')
        for ts in range(3):
            s.go(ts, lambda ts=ts: (s.direct(0, ph, ts, 'ws'), s.direct(1, ph, ts, 'ws'), s.s3(ph, ts, 'own', 'ws'),
                 s.s3(ph, ts, 'fwdR', 'ws'), s.s3(ph, ts, 'fwdL', 'ws'), [s.sib(ph, ts, k, 'ws') for k in range(4)]))

def barrier(partners):
    b = pltpu.get_barrier_semaphore()
    for d in partners:
        pl.semaphore_signal(b, inc=1, device_id=d, device_id_type=MESH)
    pl.semaphore_wait(b, len(partners))

def ag_scratch():
    return [
        pltpu.VMEM((3, 2, 2, 4, 2, 2, 5, 16, CW), jnp.bfloat16),
        pltpu.VMEM((3, 5, 16, CW), jnp.bfloat16),
        pltpu.VMEM((3, 4, 16, CW), jnp.bfloat16),
        pltpu.SemaphoreType.DMA((9, 14)),
        pltpu.SemaphoreType.DMA((9, 14)),
        pltpu.SemaphoreType.DMA((3, 8)),
        pltpu.SemaphoreType.DMA((3, 5)),
    ]
def fill_pieces(pieces, wqkv, wout, wup, wdown):
    mats = [(wqkv, 0), (wqkv, 1280), (wqkv, 2560), (wout, 0), (wup, 0), (wdown, 0)]
    for ph in range(3):
        for xh in range(2):
            r, off = mats[2 * ph + xh]
            for par in range(2):
                v = r[:, off + par * 640: off + (par + 1) * 640]
                pieces[ph, 2 * xh + par] = jnp.concatenate([v.astype(jnp.float32), jnp.zeros((6, 640), jnp.float32)], axis=0).astype(jnp.bfloat16)


def gather_kernel(wq, wo, wu, wd, out, W, stg, pieces, ssem, rsem, s0s, s0r, osem):
    p = Pos()
    ag = AG(p, W, stg, pieces, ssem, rsem, None, s0s, s0r)
    fill_pieces(pieces, wq, wo, wu, wd)
    stg[...] = jnp.zeros_like(stg)
    barrier(ag.partners())
    for ph in range(3): ag.s0(ph, 'start')
    for ph in range(3):
        ag.s0_recv(ph); ag.compact(ph); ag.phase_a(ph)
    for ph in range(3): ag.phase_b(ph)
    for ph in range(3): ag.phase_c(ph)
    for ph in range(3): ag.phase_d(ph)
    for ph in range(3): ag.phase_e(ph)
    for ph in range(3): ag.phase_f(ph)
    for ph in range(3): ag.drain(ph)
    cp = pltpu.make_async_copy(W, out, osem); cp.start(); cp.wait()


def gather_all(wq, wo, wu, wd):
    out = pl.pallas_call(gather_kernel, out_shape=jax.ShapeDtypeStruct((3,2,2,4,2,2,5,16,CW), jnp.bfloat16),
        in_specs=[pl.BlockSpec(memory_space=pltpu.VMEM)]*4, out_specs=pl.BlockSpec(memory_space=pl.ANY),
        scratch_shapes=ag_scratch()+[pltpu.SemaphoreType.DMA],
        compiler_params=pltpu.CompilerParams(collective_id=0, has_side_effects=True, vmem_limit_bytes=56*2**20), name="gather_all")(wq, wo, wu, wd)
    w = out.reshape(3, 4, 1280, CW)
    panels = [jnp.concatenate([w[m // 2, 2 * (m % 2)], w[m // 2, 2 * (m % 2) + 1]], axis=1) for m in range(6)]
    return jnp.concatenate(panels[:3], axis=1), panels[3], panels[4], panels[5]


def layer_norm(inputs):
    average = jnp.mean(inputs, axis=-1, keepdims=True)
    centered = inputs - average
    variance = jnp.mean(centered * centered, axis=-1, keepdims=True)
    inv_scale = lax.rsqrt(variance + EPSILON)
    return (centered * inv_scale, inv_scale)


def norm_back(grad_normed, normed, inv_scale):
    first_mean = jnp.mean(grad_normed, axis=-1, keepdims=True)
    second_mean = jnp.mean(grad_normed * normed, axis=-1, keepdims=True)
    return inv_scale * (grad_normed - first_mean - normed * second_mean)


def times_t(left, right):
    return lax.dot_general(
        left, right, (((1,), (1,)), ((), ())), preferred_element_type=jnp.float32
    )


def forward_pass(latents, script_ids, gathered):
    full_qkv, full_out, full_up, full_down, full_small = gathered
    items, length, width = latents.shape
    rows_all = items * length
    head_dim = width // HEADS
    scripts = full_small.shape[1] - 3
    small_float = full_small.astype(jnp.float32)
    table = small_float[:, :scripts]
    bias_first = small_float[:, scripts]
    gain_second = small_float[:, scripts + 1]
    bias_second = small_float[:, scripts + 2]
    one_hot = (script_ids[:, None] == jnp.arange(scripts, dtype=jnp.int32)[None, :]).astype(
        jnp.float32
    )
    gains_item = lax.dot_general(
        one_hot,
        table,
        (((1,), (1,)), ((), ())),
        precision=PRECISE,
        preferred_element_type=jnp.float32,
    )
    gains_rows = jnp.broadcast_to(gains_item[:, None, :], (items, length, width)).reshape(
        rows_all, width
    )
    inputs = latents.astype(jnp.float32).reshape(rows_all, width)
    normed_one, inv_one = layer_norm(inputs)
    first = (normed_one * gains_rows + bias_first).astype(jnp.bfloat16)
    projected = jnp.dot(first, full_qkv, preferred_element_type=jnp.float32).astype(jnp.bfloat16)
    split = projected.reshape(items, length, 3, HEADS, head_dim)
    queries = split[:, :, 0]
    key_rows = split[:, :, 1]
    values = split[:, :, 2]
    score_scale = 1.0 / math.sqrt(head_dim)
    scores = (
        jnp.einsum("ashe,athe->ahst", queries, key_rows, preferred_element_type=jnp.float32)
        * score_scale
    )
    row_max = jnp.max(scores, axis=-1, keepdims=True)
    exp_scores = jnp.exp(scores - row_max)
    probs = exp_scores / jnp.sum(exp_scores, axis=-1, keepdims=True)
    probs_low = probs.astype(jnp.bfloat16)
    mixed = jnp.einsum("ahst,athe->ashe", probs_low, values, preferred_element_type=jnp.float32)
    mixed = mixed.reshape(rows_all, width).astype(jnp.bfloat16)
    middle = inputs + jnp.dot(mixed, full_out, preferred_element_type=jnp.float32)
    normed_two, inv_two = layer_norm(middle)
    second = (normed_two * gain_second + bias_second).astype(jnp.bfloat16)
    upper = jnp.dot(second, full_up, preferred_element_type=jnp.float32)
    active = jax.nn.gelu(upper).astype(jnp.bfloat16)
    output = middle + jnp.dot(active, full_down, preferred_element_type=jnp.float32)
    kept = (
        one_hot,
        gains_rows,
        gain_second,
        normed_one,
        inv_one,
        first,
        queries,
        key_rows,
        values,
        probs,
        probs_low,
        mixed,
        normed_two,
        inv_two,
        second,
        upper,
        active,
    )
    return (output, kept)


def per_device(
    latents,
    script_ids,
    gain_table,
    bias_one,
    w_qkv,
    w_out,
    gain_two,
    bias_two,
    w_up,
    w_down,
    cotangent,
):
    small = jnp.concatenate(
        [gain_table, bias_one[:, None], gain_two[:, None], bias_two[:, None]], axis=1
    )
    full_small, = in_one_piece((small,), ("dp", "fsdp"), 0, 1)
    gathered = gather_all(w_qkv, w_out, w_up, w_down) + (full_small,)
    output, kept = forward_pass(latents, script_ids, gathered)
    full_qkv, full_out, full_up, full_down, full_small = gathered
    (
        one_hot,
        gains_rows,
        gain_second,
        normed_one,
        inv_one,
        first,
        queries,
        key_rows,
        values,
        probs,
        probs_low,
        mixed,
        normed_two,
        inv_two,
        second,
        upper,
        active,
    ) = kept
    items, length, width = latents.shape
    rows_all = items * length
    head_dim = width // HEADS
    score_scale = 1.0 / math.sqrt(head_dim)
    scripts = one_hot.shape[1]
    share = rows_all // lax.axis_size("fsdp")
    start = lax.axis_index("fsdp") * share

    def select(values_in):
        return lax.dynamic_slice_in_dim(values_in, start, share, 0)

    def weight_grad(left, right):
        return lax.dot_general(
            select(left),
            select(right),
            (((0,), (0,)), ((), ())),
            preferred_element_type=jnp.float32,
        )

    grad_out = cotangent.astype(jnp.float32).reshape(rows_all, width)
    grad_branch = grad_out.astype(jnp.bfloat16)
    down_grad = weight_grad(active, grad_branch)
    grad_active = times_t(grad_branch, full_down)
    upper_value, gelu_back = jax.vjp(jax.nn.gelu, upper)
    grad_upper = gelu_back(grad_active)[0].astype(jnp.bfloat16)
    up_grad = weight_grad(second, grad_upper)
    grad_second = times_t(grad_upper, full_up)
    grad_middle = grad_out + norm_back(grad_second * gain_second, normed_two, inv_two)
    grad_attn_out = grad_middle.astype(jnp.bfloat16)
    out_grad = weight_grad(mixed, grad_attn_out)
    grad_mixed = (
        times_t(grad_attn_out, full_out)
        .astype(jnp.bfloat16)
        .reshape(items, length, HEADS, head_dim)
    )
    grad_probs = jnp.einsum(
        "ashe,athe->ahst", grad_mixed, values, preferred_element_type=jnp.float32
    )
    grad_values = jnp.einsum(
        "ahst,ashe->athe", probs_low, grad_mixed, preferred_element_type=jnp.float32
    )
    row_total = jnp.sum(grad_probs * probs, axis=-1, keepdims=True)
    grad_scores = (probs * (grad_probs - row_total)).astype(jnp.bfloat16)
    grad_queries = (
        jnp.einsum("ahst,athe->ashe", grad_scores, key_rows, preferred_element_type=jnp.float32)
        * score_scale
    )
    grad_keys = (
        jnp.einsum("ahst,ashe->athe", grad_scores, queries, preferred_element_type=jnp.float32)
        * score_scale
    )
    grad_projected = jnp.concatenate(
        [
            grad_queries.reshape(rows_all, width),
            grad_keys.reshape(rows_all, width),
            grad_values.reshape(rows_all, width),
        ],
        axis=1,
    ).astype(jnp.bfloat16)
    qkv_grad = weight_grad(first, grad_projected)
    grad_first = times_t(grad_projected, full_qkv)
    input_grad = grad_middle + norm_back(grad_first * gains_rows, normed_one, inv_one)
    hot_rows = jnp.broadcast_to(one_hot[:, None, :], (items, length, scripts)).reshape(
        rows_all, scripts
    )
    table_grad = lax.dot_general(
        select(grad_first * normed_one),
        select(hot_rows),
        (((0,), (0,)), ((), ())),
        precision=PRECISE,
        preferred_element_type=jnp.float32,
    )
    bias_first_grad = jnp.sum(select(grad_first), axis=0)
    gain_second_grad = jnp.sum(select(grad_second * normed_two), axis=0)
    bias_second_grad = jnp.sum(select(grad_second), axis=0)
    small_grad = jnp.concatenate(
        [
            table_grad,
            bias_first_grad[:, None],
            gain_second_grad[:, None],
            bias_second_grad[:, None],
        ],
        axis=1,
    )
    owned = (
        lax.psum_scatter(qkv_grad.astype(jnp.bfloat16), ("dp", "fsdp"), scatter_dimension=0, tiled=True),
        lax.psum_scatter(out_grad.astype(jnp.bfloat16), ("dp", "fsdp"), scatter_dimension=0, tiled=True),
        lax.psum_scatter(up_grad.astype(jnp.bfloat16), ("dp", "fsdp"), scatter_dimension=0, tiled=True),
        lax.psum_scatter(down_grad.astype(jnp.bfloat16), ("dp", "fsdp"), scatter_dimension=0, tiled=True),
        lax.psum_scatter(small_grad, ("dp", "fsdp"), scatter_dimension=0, tiled=True),
    )
    qkv_own, out_own, up_own, down_own, small_own = owned
    qkv_own, out_own, up_own, down_own = (o.astype(jnp.float32) for o in (qkv_own, out_own, up_own, down_own))
    latents_out = output.reshape(items, length, width).astype(jnp.bfloat16)
    input_grad = input_grad.reshape(items, length, width)
    return (
        latents_out,
        input_grad,
        small_own[:, :scripts],
        small_own[:, scripts],
        qkv_own,
        out_own,
        small_own[:, scripts + 1],
        small_own[:, scripts + 2],
        up_own,
        down_own,
    )


def solution(mesh):
    return jax.shard_map(
        per_device,
        mesh=mesh,
        in_specs=(
            P("dp", None, None),
            P("dp"),
            P(("dp", "fsdp"), None),
            P(("dp", "fsdp")),
            P(("dp", "fsdp"), None),
            P(("dp", "fsdp"), None),
            P(("dp", "fsdp")),
            P(("dp", "fsdp")),
            P(("dp", "fsdp"), None),
            P(("dp", "fsdp"), None),
            P("dp", None, None),
        ),
        out_specs=(
            P("dp", None, None),
            P("dp", None, None),
            P(("dp", "fsdp"), None),
            P(("dp", "fsdp")),
            P(("dp", "fsdp"), None),
            P(("dp", "fsdp"), None),
            P(("dp", "fsdp")),
            P(("dp", "fsdp")),
            P(("dp", "fsdp"), None),
            P(("dp", "fsdp"), None),
        ),
        check_vma=False,
    )
```

```python
import math

import jax
import jax.numpy as jnp
from jax import lax
from jax.experimental import pallas as pl
from jax.experimental.pallas import tpu as pltpu
from jax.sharding import PartitionSpec as P

HEADS = 8
HD = 160
D = 1280
L = 256
EPS = 1e-5
SCALE = 1.0 / math.sqrt(HD)
BF = jnp.bfloat16
F32 = jnp.float32

MESH = pl.DeviceIdType.MESH
CW = 640

class Pos:
    def __init__(s):
        dp = lax.axis_index("dp"); s.xh = lax.axis_index("fsdp")
        s.c = dp % 2; s.y = (dp // 2) % 4; s.xl = (dp // 8) % 2; s.z = dp // 16
        s.x = s.xh * 2 + s.xl; s.h = s.y // 2; s.par = s.y % 2
    def dev(s, x=None, y=None, z=None, c=None):
        x = s.x if x is None else x; y = s.y if y is None else y
        z = s.z if z is None else z; c = s.c if c is None else c
        return (((z * 2 + x % 2) * 4 + y) * 2 + c, x // 2)
    def ring(s, ax, d):
        if ax == 0: return s.dev(x=(s.x + d) % 4)
        if ax == 1: return s.dev(y=(s.y + d) % 4)
        return s.dev(z=(s.z + d) % 4)
    def coord(s, ax, d):
        return ((s.x, s.y, s.z)[ax] + d) % 4

class AG:
    def __init__(s, p, W, stg, pieces, ssem, rsem, sib_r, s0s, s0r):
        s.p, s.W, s.stg, s.pieces = p, W, stg, pieces
        s.ssem, s.rsem, s.s0s, s.s0r = ssem, rsem, s0s, s0r
    def partners(s):
        p = s.p
        out = []
        for ax in range(3):
            for d in (1, 2, 3): out.append(p.ring(ax, d))
        for dy in (0, 1):
            for dx in (0, 1):
                for dc in (0, 1):
                    if (dy, dx, dc) == (0, 0, 0): continue
                    if (dy, dx, dc) == (0, 1, 0): continue
                    y = p.y ^ dy if dy else p.y
                    x = (p.x + 2 * dx) % 4
                    out.append(p.dev(x=x, y=y, c=(p.c + dc) % 2))
        return out
    def s0_targets(s):
        p = s.p
        res = []
        for dy in (0, 1):
            for dx in (0, 1):
                y = p.y ^ dy if dy else p.y
                x = (p.x + 2 * dx) % 4
                res.append((dy, dx, y, x))
        return res
    def s0_src(s):
        p = s.p
        return (p.par * 2 + p.c) * 2 + p.xh
    def s0(s, ph, act):
        p = s.p; o = s.s0_src()
        for tc in (0, 1):
            cond = (o <= 4) if tc == 0 else (o >= 4)
            @pl.when(cond)
            def _(tc=tc):
                for i, (dy, dx, y, x) in enumerate(s.s0_targets()):
                    chunk = (x // 2) * 2 + y % 2
                    src = s.pieces.at[ph, chunk]
                    dst = s.stg.at[ph, o - 4 * tc]
                    if dy == 0 and dx == 0:
                        @pl.when(p.c == tc)
                        def _():
                            cp = pltpu.make_async_copy(src, dst, s.s0r.at[ph, o - 4 * tc])
                            if act == 'start': cp.start()
                        @pl.when(p.c != tc)
                        def _():
                            cp = pltpu.make_async_remote_copy(src, dst, s.s0s.at[ph, i * 2 + tc], s.s0r.at[ph, o - 4 * tc], device_id=p.dev(y=y, x=x, c=tc), device_id_type=MESH)
                            if act == 'start': cp.start()
                            else: cp.wait_send()
                    else:
                        cp = pltpu.make_async_remote_copy(src, dst, s.s0s.at[ph, i * 2 + tc], s.s0r.at[ph, o - 4 * tc], device_id=p.dev(y=y, x=x, c=tc), device_id_type=MESH)
                        if act == 'start': cp.start()
                        else: cp.wait_send()
    def s0_recv(s, ph):
        p = s.p
        for k in range(5):
            def w(k=k):
                pltpu.make_async_copy(s.pieces.at[ph, 0], s.stg.at[ph, k], s.s0r.at[ph, k]).wait()
            if k < 4: w()
            else: pl.when(p.c == 0)(w)
    def compact(s, ph):
        p = s.p
        i = lax.broadcasted_iota(jnp.int32, (48, 80), 0)
        k = lax.broadcasted_iota(jnp.int32, (48, 80), 1)
        r = 48 * p.c + i
        q = (r * 205) >> 11
        col = (q - 4 * p.c) * 16 + (r - q * 10)
        P = jnp.where(k == col, 1.0, 0.0).astype(jnp.bfloat16)
        res = jnp.dot(P, s.stg[ph].reshape(80, CW), preferred_element_type=jnp.float32).astype(jnp.bfloat16)
        def put(ts):
            s.W[ph, p.xh, p.par, p.z, p.xl, p.h, 3 * p.c + ts] = res[ts * 16:(ts + 1) * 16]
        put(0); put(1)
        pl.when(p.c == 0)(lambda: put(2))
    def order(s, ph, ts):
        a = (ph + ts) % 3
        return ((a + 1) % 3, (a + 2) % 3, a)
    def region(s, ph, t, full, over=None):
        p = s.p; o = over or {}
        x = o.get(0); y = o.get(1); z = o.get(2)
        xh, xl = (p.xh, p.xl) if x is None else (x // 2, x % 2)
        h, par = (p.h, p.par) if y is None else (y // 2, y % 2)
        zz = p.z if z is None else z
        if 0 in full: xh = xl = slice(None)
        if 1 in full: h = par = slice(None)
        if 2 in full: zz = slice(None)
        return [ph, xh, par, zz, xl, h, t]
    def ref(s, reg): return s.W.at[tuple(reg)]
    def cp(s, reg, slot, k, dev):
        r = s.ref(reg)
        return pltpu.make_async_remote_copy(r, r, s.ssem.at[slot, k], s.rsem.at[slot, k], device_id=dev, device_id_type=MESH)
    def half(s, reg, full, hf):
        reg = list(reg)
        i = 3 if 2 in full else (1 if 0 in full else 2)
        reg[i] = pl.ds(hf * 2, 2) if i == 3 else pl.ds(hf, 1)
        return reg
    def slot(s, ph, ts): return ph * 3 + ts
    def t(s, ts): return 3 * s.p.c + ts
    def g(s, ts, f):
        if ts < 2: f()
        else: pl.when(s.p.c == 0)(f)
    def direct(s, stage, ph, ts, act):
        a = s.order(ph, ts); full = a[:stage]; ax = a[stage]
        for d in (1, 3, 2):
            k = stage * 3 + d - 1
            if act == 'recv':
                s.cp(s.region(ph, s.t(ts), full, {ax: s.p.coord(ax, -d)}), s.slot(ph, ts), k, s.p.ring(ax, d)).wait_recv()
            else:
                c = s.cp(s.region(ph, s.t(ts), full), s.slot(ph, ts), k, s.p.ring(ax, d))
                c.start() if act == 'start' else c.wait_send()
    def s3(s, ph, ts, what, act):
        a = s.order(ph, ts); full = a[:2]; ax = a[2]; sl = s.slot(ph, ts); tt = s.t(ts)
        R, L = s.p.ring(ax, 1), s.p.ring(ax, 3)
        own = s.region(ph, tt, full)
        fl = s.region(ph, tt, full, {ax: s.p.coord(ax, -1)})
        fr = s.region(ph, tt, full, {ax: s.p.coord(ax, 1)})
        op = s.region(ph, tt, full, {ax: s.p.coord(ax, 2)})
        if what == 'own':
            if act == 'recvL': s.cp(fl, sl, 6, R).wait_recv()
            elif act == 'recvR': s.cp(fr, sl, 7, L).wait_recv()
            else:
                for reg, k, dv in ((own, 6, R), (own, 7, L)):
                    c = s.cp(reg, sl, k, dv)
                    c.start() if act == 'start' else c.wait_send()
        elif what == 'fwdR':
            if act == 'recv': s.cp(s.half(op, full, 0), sl, 8, R).wait_recv()
            else:
                c = s.cp(s.half(fl, full, 0), sl, 8, R)
                c.start() if act == 'start' else c.wait_send()
        elif what == 'fwdL':
            if act == 'recv': s.cp(s.half(op, full, 1), sl, 9, L).wait_recv()
            else:
                c = s.cp(s.half(fr, full, 1), sl, 9, L)
                c.start() if act == 'start' else c.wait_send()
    def sib(s, ph, ts, piece, act):
        a = s.order(ph, ts); full = a[:2]; ax = a[2]
        d = (0, -1, 1, 2)[piece]
        dv = s.p.dev(c=1 - s.p.c)
        t = s.t(ts) if act != 'recv' else 3 * (1 - s.p.c) + ts
        c = s.cp(s.region(ph, t, full, {ax: s.p.coord(ax, d)}), s.slot(ph, ts), 10 + piece, dv)
        if act == 'start': c.start()
        elif act == 'recv': c.wait_recv()
        else: c.wait_send()
    def go(s, ts, f, other=False):
        def h():
            f()
        if ts < 2: h()
        else: pl.when(s.p.c == (1 if other else 0))(h)
    def phase_a(s, ph):
        for ts in range(3): s.go(ts, lambda ts=ts: s.direct(0, ph, ts, 'start'))
    def phase_b(s, ph):
        for ts in range(3):
            s.go(ts, lambda ts=ts: (s.direct(0, ph, ts, 'recv'), s.direct(1, ph, ts, 'start')))
    def phase_c(s, ph):
        for ts in range(3):
            s.go(ts, lambda ts=ts: (s.direct(1, ph, ts, 'recv'), s.s3(ph, ts, 'own', 'start'), s.sib(ph, ts, 0, 'start')))
    def phase_d(s, ph):
        for ts in range(3):
            s.go(ts, lambda ts=ts: (
                s.s3(ph, ts, 'own', 'recvL'), s.s3(ph, ts, 'fwdR', 'start'), s.sib(ph, ts, 1, 'start'),
                s.s3(ph, ts, 'own', 'recvR'), s.s3(ph, ts, 'fwdL', 'start'), s.sib(ph, ts, 2, 'start')))
    def phase_e(s, ph):
        for ts in range(3):
            s.go(ts, lambda ts=ts: (s.s3(ph, ts, 'fwdR', 'recv'), s.s3(ph, ts, 'fwdL', 'recv'), s.sib(ph, ts, 3, 'start')))
    def phase_f(s, ph):
        for ts in range(3):
            s.go(ts, lambda ts=ts: [s.sib(ph, ts, k, 'recv') for k in range(4)], other=True)
    def drain(s, ph):
        s.s0(ph, 'wait_send')
        for ts in range(3):
            s.go(ts, lambda ts=ts: (s.direct(0, ph, ts, 'ws'), s.direct(1, ph, ts, 'ws'), s.s3(ph, ts, 'own', 'ws'),
                 s.s3(ph, ts, 'fwdR', 'ws'), s.s3(ph, ts, 'fwdL', 'ws'), [s.sib(ph, ts, k, 'ws') for k in range(4)]))

def barrier(partners):
    b = pltpu.get_barrier_semaphore()
    for d in partners:
        pl.semaphore_signal(b, inc=1, device_id=d, device_id_type=MESH)
    pl.semaphore_wait(b, len(partners))

def fill_pieces(pieces, wqkv, wout, wup, wdown):
    mats = [(wqkv, 0), (wqkv, 1280), (wqkv, 2560), (wout, 0), (wup, 0), (wdown, 0)]
    for ph in range(3):
        for xh in range(2):
            r, off = mats[2 * ph + xh]
            for par in range(2):
                v = r[:, off + par * 640: off + (par + 1) * 640]
                pieces[ph, 2 * xh + par] = jnp.concatenate([v.astype(jnp.float32), jnp.zeros((6, 640), jnp.float32)], axis=0).astype(jnp.bfloat16)


def dot(a, b):
    return jnp.dot(a, b, preferred_element_type=F32)


def dot_nt(a, b):
    return lax.dot_general(a, b, (((1,), (1,)), ((), ())), preferred_element_type=F32)


def dot_tn(a, b):
    return lax.dot_general(a, b, (((0,), (0,)), ((), ())), preferred_element_type=F32)


class Small:
    def __init__(s, p, buf, recv, ssem, rsem, rings):
        s.p, s.buf, s.recv, s.ssem, s.rsem, s.rings = p, buf, recv, ssem, rsem, rings

    def cps(s, k):
        p = s.p
        n = len(s.rings)
        if k == 0 or k == n + 1:
            src = s.buf.at[1 - p.c] if k == 0 else s.buf.at[p.c]
            dst = s.recv.at[0, 0] if k == 0 else s.recv.at[0, 1]
            return [pltpu.make_async_remote_copy(src, dst, s.ssem.at[k, 0], s.rsem.at[k, 0], device_id=p.dev(c=1 - p.c), device_id_type=MESH)]
        return [pltpu.make_async_remote_copy(s.buf.at[p.c], s.recv.at[k, i], s.ssem.at[k, i], s.rsem.at[k, i], device_id=dv, device_id_type=MESH)
                for i, dv in enumerate(s.rings[k - 1])]

    def start(s, k):
        for c in s.cps(k): c.start()

    def finish(s, k):
        p = s.p
        n = len(s.rings)
        cs = s.cps(k)
        if k == n + 1:
            cs[0].wait_recv()
            cs[0].wait_send()
            s.buf[1 - p.c] = s.recv[0, 1]
            return
        for c in cs: c.wait_recv()
        for c in cs: c.wait_send()
        acc = s.buf[p.c].astype(F32)
        for i in range(len(cs)):
            acc = acc + s.recv[k, i].astype(F32)
        s.buf[p.c] = acc.astype(s.buf.dtype)


class RS:
    def __init__(s, p, G, RD, bufs, FR, EX, FIN, dss, drs, ss, rs, fs, fr):
        s.p, s.G, s.RD, s.bufs, s.FR, s.EX, s.FIN = p, G, RD, bufs, FR, EX, FIN
        s.dss, s.drs, s.ss, s.rs, s.fs, s.fr = dss, drs, ss, rs, fs, fr

    def gref(s, ph):
        return s.G[ph]

    def go(s, ts, f, other=False):
        def h():
            f()
        if ts < 2: h()
        else: pl.when(s.p.c == (1 if other else 0))(h)

    def d2d(s, ph, ts, act):
        p = s.p
        g = s.gref(ph)
        t = 3 * (1 - p.c) + ts if act != 'recv' else 3 * p.c + ts
        for par in range(2):
            cp = pltpu.make_async_remote_copy(g.at[par, :, :, :, t], s.RD.at[ph, ts, par], s.dss.at[ph * 3 + ts, par], s.drs.at[ph * 3 + ts, par], device_id=p.dev(c=1 - p.c), device_id_type=MESH)
            if act == 'start': cp.start()
            elif act == 'ws': cp.wait_send()
            else: cp.wait_recv()

    def d2d_start(s, ph):
        for ts in range(3): s.go(ts, lambda ts=ts: s.d2d(ph, ts, 'start'), other=True)

    def d2d_add(s, ph, ts):
        g = s.gref(ph)
        t = 3 * s.p.c + ts
        s.d2d(ph, ts, 'recv')
        for par in range(2):
            def body(z, _):
                g[par, z, :, :, t] = (g[par, z, :, :, t].astype(F32) + s.RD[ph, ts, par, z].astype(F32)).astype(BF)
                return 0
            lax.fori_loop(0, 4, body, 0)

    def order(s, ph, ts):
        f = (ph + ts) % 3
        return ((0, 1, 2), (1, 2, 0), (2, 1, 0))[f]

    def fidx(s, ph, ts):
        return (ph + ts) % 3

    def piece(s, ph, ts, st, k):
        p = s.p
        o = s.order(ph, ts)
        ax = o[st]
        done = o[:st]
        par = h = zz = xl = slice(None)
        if 0 in done: xl = p.xl
        if 1 in done: h, par = p.h, p.par
        if 2 in done: zz = p.z
        if ax == 0: xl = k
        if ax == 1: h, par = k // 2, k % 2
        if ax == 2: zz = k
        return s.gref(ph).at[par, zz, xl, h, 3 * p.c + ts]

    def half(s, ph, ts, st, k, hf):
        p = s.p
        o = s.order(ph, ts)
        ax = o[st]
        assert st == 0
        t = 3 * p.c + ts
        if ax == 1: return s.gref(ph).at[k % 2, pl.ds(2 * hf, 2), :, k // 2, t]
        return s.gref(ph).at[hf, k, :, :, t]

    def bhalf(s, ph, ts, hf):
        f = s.fidx(ph, ts)
        b = s.bufs[f][0]
        if f == 1: return b.at[ph, 2, pl.ds(2 * hf, 2)]
        return b.at[ph, 2, hf]

    def cp(s, src, dst, sl, k, dev):
        return pltpu.make_async_remote_copy(src, dst, s.ss.at[sl, k], s.rs.at[sl, k], device_id=dev, device_id_type=MESH)

    def add(s, dst, srcs):
        lead = dst.shape[:-2]
        if len(lead) >= 1 and lead[0] > 1:
            def body(i, _):
                acc = dst[i].astype(F32)
                for r in srcs: acc = acc + r[i].astype(F32)
                dst[i] = acc.astype(BF)
                return 0
            lax.fori_loop(0, lead[0], body, 0)
        else:
            acc = dst[...].astype(F32)
            for r in srcs: acc = acc + r[...].astype(F32)
            dst[...] = acc.astype(BF)

    def sem(s, st, i):
        return (0, 4, 7)[st] + i

    def ring_cps(s, ph, ts, st):
        p = s.p
        o = s.order(ph, ts)
        ax = o[st]
        f = s.fidx(ph, ts)
        sl = ph * 3 + ts
        b = s.bufs[f][st]
        if ax == 0:
            k = 1 - p.xl
            return [s.cp(s.piece(ph, ts, st, k), b.at[ph, 0], sl, s.sem(st, 0), p.dev(x=p.xh * 2 + k))]
        res = []
        for i, d in enumerate((1, 3, 2)):
            res.append(s.cp(s.piece(ph, ts, st, p.coord(ax, d)), b.at[ph, i], sl, s.sem(st, i), p.ring(ax, d)))
        return res

    def first_a(s, ph, ts):
        if s.order(ph, ts)[0] == 0:
            for c in s.ring_cps(ph, ts, 0): c.start()
            return
        for c in s.sf_half(ph, ts): c.start()

    def sf_half(s, ph, ts):
        p = s.p
        ax = s.order(ph, ts)[0]
        sl = ph * 3 + ts
        k = p.coord(ax, 2)
        return [s.cp(s.half(ph, ts, 0, k, 1), s.bhalf(ph, ts, 1), sl, 2, p.ring(ax, 1)),
                s.cp(s.half(ph, ts, 0, k, 0), s.bhalf(ph, ts, 0), sl, 3, p.ring(ax, 3))]

    def sf_full(s, ph, ts):
        p = s.p
        ax = s.order(ph, ts)[0]
        sl = ph * 3 + ts
        b = s.bufs[s.fidx(ph, ts)][0]
        return [s.cp(s.piece(ph, ts, 0, p.coord(ax, 1)), b.at[ph, 0], sl, 0, p.ring(ax, 1)),
                s.cp(s.piece(ph, ts, 0, p.coord(ax, 3)), b.at[ph, 1], sl, 1, p.ring(ax, 3))]

    def first_b(s, ph, ts):
        p = s.p
        o = s.order(ph, ts)
        ax = o[0]
        if ax == 0: return
        hb = s.sf_half(ph, ts)
        full = s.sf_full(ph, ts)
        hb[0].wait_recv()
        s.add(s.half(ph, ts, 0, p.coord(ax, 1), 1), [s.bhalf(ph, ts, 1)])
        full[0].start()
        hb[1].wait_recv()
        s.add(s.half(ph, ts, 0, p.coord(ax, 3), 0), [s.bhalf(ph, ts, 0)])
        full[1].start()

    def first_c(s, ph, ts):
        p = s.p
        o = s.order(ph, ts)
        ax = o[0]
        me = (p.xl, p.y, p.z)[ax]
        b = s.bufs[s.fidx(ph, ts)][0]
        cs = s.ring_cps(ph, ts, 0) if ax == 0 else s.sf_full(ph, ts)
        for c in cs: c.wait_recv()
        s.add(s.piece(ph, ts, 0, me), [b.at[ph, i] for i in range(len(cs))])

    def next_start(s, ph, ts, st):
        for c in s.ring_cps(ph, ts, st): c.start()

    def next_finish(s, ph, ts, st):
        p = s.p
        ax = s.order(ph, ts)[st]
        me = (p.xl, p.y, p.z)[ax]
        b = s.bufs[s.fidx(ph, ts)][st]
        cs = s.ring_cps(ph, ts, st)
        for c in cs: c.wait_recv()
        s.add(s.piece(ph, ts, st, me), [b.at[ph, i] for i in range(len(cs))])

    def each(s, f):
        for ts in range(3): s.go(ts, lambda ts=ts: f(ts))

    def step(s, ph, k):
        if k == 0: s.d2d_start(ph)
        elif k == 1: s.each(lambda ts: (s.d2d_add(ph, ts), s.first_a(ph, ts)))
        elif k == 2: s.each(lambda ts: s.first_b(ph, ts))
        elif k == 3: s.each(lambda ts: (s.first_c(ph, ts), s.next_start(ph, ts, 1)))
        elif k == 4: s.each(lambda ts: (s.next_finish(ph, ts, 1), s.next_start(ph, ts, 2)))
        elif k == 5:
            s.each(lambda ts: s.next_finish(ph, ts, 2))
            s.final_start(ph)

    def fin_cps(s, ph, k):
        p = s.p
        o = 4 * p.c + k
        chunk = 2 * p.xh + p.par
        dev = p.dev(x=(o % 2) * 2 + p.xl, y=2 * p.h + o // 4, c=(o // 2) % 2)
        return pltpu.make_async_remote_copy(s.EX.at[ph, k], s.FIN.at[ph, chunk, p.c], s.fs.at[ph, k], s.fr.at[ph, chunk * 2 + p.c], device_id=dev, device_id_type=MESH)

    def myo(s):
        p = s.p
        return (p.par * 2 + p.c) * 2 + p.xh

    def final_start(s, ph):
        p = s.p
        g = s.gref(ph)
        def put(ts):
            s.FR[ts] = g[p.par, p.z, p.xl, p.h, 3 * p.c + ts]
        put(0); put(1)
        pl.when(p.c == 0)(lambda: put(2))
        i = lax.broadcasted_iota(jnp.int32, (80, 48), 1)
        k = lax.broadcasted_iota(jnp.int32, (80, 48), 0)
        r = 48 * p.c + i
        q = (r * 205) >> 11
        col = (q - 4 * p.c) * 16 + (r - q * 10)
        pt = jnp.where(k == col, 1.0, 0.0).astype(BF)
        s.EX[ph] = dot(pt, s.FR[...].reshape(48, CW)).astype(BF).reshape(5, 16, CW)
        for k in range(5):
            def send(k=k):
                me = 4 * p.c + k == s.myo()
                @pl.when(me)
                def _():
                    s.FIN[ph, 2 * p.xh + p.par, p.c] = s.EX[ph, k]
                @pl.when(jnp.logical_not(me))
                def _():
                    s.fin_cps(ph, k).start()
            if k < 4: send()
            else: pl.when(p.c == 0)(send)

    def final_wait(s, ph):
        p = s.p
        o = s.myo()
        for chunk in range(4):
            for sc in range(2):
                c1 = (o <= 4) if sc == 0 else (o >= 4)
                mine = jnp.logical_and(chunk == 2 * p.xh + p.par, sc == p.c)
                @pl.when(jnp.logical_and(c1, jnp.logical_not(mine)))
                def _(chunk=chunk, sc=sc):
                    pltpu.make_async_remote_copy(s.EX.at[ph, 0], s.FIN.at[ph, chunk, sc], s.fs.at[ph, 0], s.fr.at[ph, chunk * 2 + sc], device_id=p.dev(c=1 - p.c), device_id_type=MESH).wait_recv()

    def drain(s, ph):
        p = s.p
        for ts in range(3):
            s.go(ts, lambda ts=ts: s.d2d(ph, ts, 'ws'), other=True)
            def ws(ts=ts):
                if s.order(ph, ts)[0] == 0:
                    for c in s.ring_cps(ph, ts, 0): c.wait_send()
                else:
                    for c in s.sf_half(ph, ts) + s.sf_full(ph, ts): c.wait_send()
                for st in (1, 2):
                    for c in s.ring_cps(ph, ts, st): c.wait_send()
            s.go(ts, ws)
        for k in range(5):
            def w(k=k):
                pl.when(4 * p.c + k != s.myo())(lambda: s.fin_cps(ph, k).wait_send())
            if k < 4: w()
            else: pl.when(p.c == 0)(w)


FIRST, Q, K, V, MIXED, SECOND, ACTIVE, GU, GAO, GMX, GQ, GK, GV = range(13)
RB = 32


def block_kernel(lat, cot, sid, small, wq, wo, wu, wd, o_lat, o_in, o_small, o_qkv, o_out, o_up, o_down,
                 W, stg, pieces, A, N1, N2, MID, DG, PR, I1, I2, VEC, CS, G2, RD, b00, b01, b02, b10, b11, b12, b20, b21, b22,
                 FR, EX, FIN, SB, SBR, SG, SGR,
                 ssem, rsem, s0s, s0r, dss, drs, gss, grs, fs, fr, sbs, sbr, sgs, sgr):
    p = Pos()
    ag = AG(p, W, stg, pieces, ssem, rsem, None, s0s, s0r)
    G = [W.at[2, 0], W.at[2, 1], G2]
    rs = RS(p, G, RD, [[b00, b01, b02], [b10, b11, b12], [b20, b21, b22]], FR, EX, FIN, dss, drs, gss, grs, fs, fr)
    ring3 = lambda ax: [p.ring(ax, d) for d in (1, 3, 2)]
    sb = Small(p, SB, SBR, sbs, sbr, [ring3(0), ring3(1), ring3(2)])
    sg = Small(p, SG, SGR, sgs, sgr, [ring3(1), ring3(2), [p.dev(x=p.xh * 2 + 1 - p.xl)]])
    idx = lax.axis_index("dp") * 2 + p.xh

    parts = ag.partners()
    bar = pltpu.get_barrier_semaphore()
    fill_pieces(pieces, wq, wo, wu, wd)
    stg[...] = jnp.zeros_like(stg)
    FIN[...] = jnp.zeros_like(FIN)
    FR[...] = jnp.zeros_like(FR)
    for d in parts:
        pl.semaphore_signal(bar, inc=1, device_id=d, device_id_type=MESH)
    j = lax.broadcasted_iota(jnp.int32, (16, D), 0)
    lane = lax.broadcasted_iota(jnp.int32, (16, D), 1)
    own = jnp.where(jnp.logical_and(lane == idx * 10 + j, j < 10), 1.0, 0.0)
    spread = dot_tn(small[...], own.astype(BF)).astype(BF)
    for k in range(2): SB[k] = spread[:, k * 640:(k + 1) * 640]
    pl.semaphore_wait(bar, len(parts))

    for ph in range(3): ag.s0(ph, 'start')
    sb.start(0)

    def ln1(r, _):
        rows = pl.ds(pl.multiple_of(r * RB, RB), RB)
        x = lat[rows, :].astype(F32)
        mu = jnp.mean(x, axis=-1, keepdims=True)
        xc = x - mu
        inv = lax.rsqrt(jnp.mean(xc * xc, axis=-1, keepdims=True) + EPS)
        N1[rows, :] = xc * inv
        I1[rows, :] = jnp.broadcast_to(inv, (RB, 128))
        return 0
    lax.fori_loop(0, L // RB, ln1, 0)
    A[MIXED] = jnp.zeros((L, D), BF)
    for k in (GQ, GK, GV): A[k] = jnp.zeros((L, D), BF)
    CS[...] = jnp.zeros_like(CS)

    sb.finish(0); sb.start(1)
    for ph in range(3):
        ag.s0_recv(ph); ag.compact(ph); ag.phase_a(ph)
        sb.finish(ph + 1); sb.start(ph + 2)
    ag.phase_b(0); ag.phase_c(0)
    ag.phase_b(1)
    ag.phase_b(2)
    ag.phase_c(1)
    sb.finish(4)
    lane32 = lax.broadcasted_iota(jnp.int32, (8, 32), 1)
    sub8 = lax.broadcasted_iota(jnp.int32, (8, 32), 0)
    tgt = jnp.where(sub8 == 0, sid[0], jnp.where(sub8 < 4, 15 + sub8, -1))
    pick = jnp.where(lane32 == tgt, 1.0, 0.0).astype(BF)
    for k in range(2): VEC[:, k * 640:(k + 1) * 640] = dot(pick, SB[k])

    def mk_first(r, _):
        rows = pl.ds(pl.multiple_of(r * RB, RB), RB)
        A[FIRST, rows, :] = (N1[rows, :] * VEC[0:1, :] + VEC[1:2, :]).astype(BF)
        return 0
    lax.fori_loop(0, L // RB, mk_first, 0)
    ag.phase_d(0)
    ag.phase_c(2)
    ag.phase_e(0)
    ag.phase_f(0)

    def wpan(ph, xh, par): return W[ph, xh, par].reshape(D, CW)
    def cols(par): return pl.ds(par * CW, CW)

    for xh, dst in ((0, Q), (1, K)):
        for par in range(2):
            A[dst, :, cols(par)] = dot(A[FIRST], wpan(0, xh, par)).astype(BF)
    ag.phase_d(1)
    ag.phase_e(1)
    ag.phase_f(1)
    for par in range(2):
        A[V, :, cols(par)] = dot(A[FIRST], wpan(1, 0, par)).astype(BF)
    ag.phase_d(2)

    lane256 = lax.broadcasted_iota(jnp.int32, (1, 256), 1)
    def masks(w):
        m = jnp.where(jnp.logical_and(lane256 >= 32 * w, lane256 < 32 * w + HD), 1.0, 0.0)
        return m, m.astype(BF)
    def win(pn, w):
        return pl.ds(pl.multiple_of(pn * CW + w * 128, 128), 256)

    for w in range(4):
        m32, m16 = masks(w)
        def att(pn, _, w=w, m32=m32, m16=m16):
            cw = win(pn, w)
            sc = dot_nt(A[Q, :, cw] * m16, A[K, :, cw]) * SCALE
            e = jnp.exp(sc - jnp.max(sc, axis=-1, keepdims=True))
            pr = e / jnp.sum(e, axis=-1, keepdims=True)
            PR[pn * 4 + w] = pr
            mx = dot(pr.astype(BF), A[V, :, cw]) * m32
            A[MIXED, :, cw] = A[MIXED, :, cw] + mx.astype(BF)
            return 0
        lax.fori_loop(0, 2, att, 0)
    ag.phase_e(2)
    for par in range(2):
        MID[:, cols(par)] = lat[:, cols(par)].astype(F32) + dot(A[MIXED], wpan(1, 1, par))

    def ln2(r, _):
        rows = pl.ds(pl.multiple_of(r * RB, RB), RB)
        x = MID[rows, :]
        mu = jnp.mean(x, axis=-1, keepdims=True)
        xc = x - mu
        inv = lax.rsqrt(jnp.mean(xc * xc, axis=-1, keepdims=True) + EPS)
        n = xc * inv
        N2[rows, :] = n
        I2[rows, :] = jnp.broadcast_to(inv, (RB, 128))
        A[SECOND, rows, :] = (n * VEC[2:3, :] + VEC[3:4, :]).astype(BF)
        return 0
    lax.fori_loop(0, L // RB, ln2, 0)
    ag.phase_f(2)
    for par in range(2):
        DG[:, cols(par)] = dot(A[SECOND], wpan(2, 0, par))

    def gelu(r, _):
        rows = pl.ds(pl.multiple_of(r * RB, RB), RB)
        u = DG[rows, :]
        c0 = math.sqrt(2.0 / math.pi)
        u2 = u * u
        th = jnp.tanh(c0 * (u + 0.044715 * u2 * u))
        hp = 0.5 * (1.0 + th)
        A[ACTIVE, rows, :] = (u * hp).astype(BF)
        DG[rows, :] = hp + 0.5 * u * (1.0 - th * th) * (c0 * (1.0 + 3 * 0.044715 * u2))
        return 0
    lax.fori_loop(0, L // RB, gelu, 0)

    def back(src, ph, xh, n):
        acc = None
        for par in range(2):
            t = dot_nt(src(par), W[ph, xh, par, 2 * n:2 * n + 2].reshape(CW, CW))
            acc = t if acc is None else acc + t
        return acc

    for n in range(2):
        A[GU, :, cols(n)] = (back(lambda par: cot[:, cols(par)], 2, 1, n) * DG[:, cols(n)]).astype(BF)

    def wgrad(ph, l0, l1, r0, r1):
        li = jnp.where(p.xh == 0, l0, l1)
        ri = jnp.where(p.xh == 0, r0, r1) if r1 is not None else None
        g = G[ph]
        for n in range(2):
            for par in range(2):
                if ri is None:
                    v = dot_tn(A[li, :, cols(n)], GR[:, cols(par)])
                else:
                    v = dot_tn(A[li, :, cols(n)], A[ri, :, cols(par)])
                g[par, 2 * n:2 * n + 2] = v.astype(BF).reshape(2, 2, 2, 5, 16, CW)

    for par in range(2):
        o_lat[:, cols(par)] = (MID[:, cols(par)] + dot(A[ACTIVE], wpan(2, 1, par))).astype(BF)
    A[GAO] = cot[...]
    wgrad(2, SECOND, ACTIVE, GU, GAO)
    rs.step(2, 0)

    for n in range(2):
        MID[:, cols(n)] = back(lambda par: A[GU, :, cols(par)], 2, 0, n)
    rs.step(2, 1)

    def ln2b(r, _):
        rows = pl.ds(pl.multiple_of(r * RB, RB), RB)
        gs = MID[rows, :]
        n = N2[rows, :]
        CS[1] += jnp.sum((gs * n).reshape(RB // 8, 8, D), axis=0)
        CS[2] += jnp.sum(gs.reshape(RB // 8, 8, D), axis=0)
        dn = gs * VEC[2:3, :]
        m1 = jnp.mean(dn, axis=-1, keepdims=True)
        m2 = jnp.mean(dn * n, axis=-1, keepdims=True)
        gm = cot[rows, :].astype(F32) + I2[rows, 0:1] * (dn - m1 - n * m2)
        N2[rows, :] = gm
        A[GAO, rows, :] = gm.astype(BF)
        return 0
    lax.fori_loop(0, L // RB, ln2b, 0)
    for n in range(2):
        A[GMX, :, cols(n)] = back(lambda par: A[GAO, :, cols(par)], 1, 1, n).astype(BF)
    rs.step(2, 2)

    for w in range(4):
        m32, m16 = masks(w)
        def attb(pn, _, w=w, m32=m32, m16=m16):
            cw = win(pn, w)
            gm = A[GMX, :, cw] * m16
            qm = A[Q, :, cw] * m16
            pr = PR[pn * 4 + w]
            gp = dot_nt(gm, A[V, :, cw])
            rt = jnp.sum(gp * pr, axis=-1, keepdims=True)
            gsc = (pr * (gp - rt)).astype(BF)
            A[GV, :, cw] = A[GV, :, cw] + dot_tn(pr.astype(BF), gm).astype(BF)
            A[GQ, :, cw] = A[GQ, :, cw] + (dot(gsc, A[K, :, cw]) * SCALE * m32).astype(BF)
            A[GK, :, cw] = A[GK, :, cw] + (dot_tn(gsc, qm) * SCALE).astype(BF)
            return 0
        lax.fori_loop(0, 2, attb, 0)
        if w == 1: rs.step(2, 3)
    ag.drain(0); ag.drain(1); ag.drain(2)
    wgrad(1, FIRST, MIXED, GV, GAO)
    rs.step(1, 0)
    wgrad(0, FIRST, FIRST, GQ, GK)
    rs.step(2, 4)
    rs.step(1, 1)
    rs.step(0, 0)
    rs.step(2, 5)
    rs.step(1, 2)
    rs.step(0, 1)

    for n in range(2):
        acc = None
        for g, (ph, xh) in ((GQ, (0, 0)), (GK, (0, 1)), (GV, (1, 0))):
            t = back(lambda par: A[g, :, cols(par)], ph, xh, n)
            acc = t if acc is None else acc + t
        MID[:, cols(n)] = acc
    rs.step(1, 3)
    rs.step(0, 2)

    def ln1b(r, _):
        rows = pl.ds(pl.multiple_of(r * RB, RB), RB)
        gf = MID[rows, :]
        n = N1[rows, :]
        CS[3] += jnp.sum((gf * n).reshape(RB // 8, 8, D), axis=0)
        CS[0] += jnp.sum(gf.reshape(RB // 8, 8, D), axis=0)
        dn = gf * VEC[0:1, :]
        m1 = jnp.mean(dn, axis=-1, keepdims=True)
        m2 = jnp.mean(dn * n, axis=-1, keepdims=True)
        o_in[rows, :] = N2[rows, :] + I1[rows, 0:1] * (dn - m1 - n * m2)
        return 0
    lax.fori_loop(0, L // RB, ln1b, 0)
    sub24 = lax.broadcasted_iota(jnp.int32, (24, 640), 0)
    for k in range(2):
        v = [jnp.sum(CS[i, :, k * 640:(k + 1) * 640], axis=0, keepdims=True) for i in range(4)]
        SG[k] = (jnp.where(sub24 == sid[0], v[3], 0.0) + jnp.where(sub24 == 16, v[0], 0.0)
                 + jnp.where(sub24 == 17, v[1], 0.0) + jnp.where(sub24 == 18, v[2], 0.0))
    sg.start(0)
    rs.step(1, 4)
    rs.step(0, 3)
    sg.finish(0); sg.start(1)
    rs.step(1, 5)
    rs.step(0, 4)
    sg.finish(1); sg.start(2)
    rs.step(0, 5)
    sg.finish(2); sg.start(3)

    outs = [(o_qkv, 0), (o_qkv, 1280), (o_qkv, 2560), (o_out, 0), (o_up, 0), (o_down, 0)]
    def emit(ph):
        rs.final_wait(ph)
        for xh in range(2):
            o, off = outs[2 * ph + xh]
            for par in range(2):
                v = FIN[ph, 2 * xh + par, 0].astype(F32) + FIN[ph, 2 * xh + par, 1].astype(F32)
                o[:, off + par * 640: off + (par + 1) * 640] = v[0:10]
    emit(2)
    sg.finish(3); sg.start(4)
    emit(1)
    sg.finish(4)
    acc = None
    for k in range(2):
        t = lax.dot_general(own[:, k * 640:(k + 1) * 640], SG[k], (((1,), (1,)), ((), ())), precision=lax.Precision.HIGHEST, preferred_element_type=F32)
        acc = t if acc is None else acc + t
    o_small[...] = acc[0:10]
    emit(0)
    for ph in range(3): rs.drain(ph)


def per_device(latents, script_ids, gain_table, bias_one, w_qkv, w_out, gain_two, bias_two, w_up, w_down, cotangent):
    small = jnp.concatenate([gain_table, bias_one[:, None], gain_two[:, None], bias_two[:, None]], axis=1)
    small = jnp.pad(small, ((0, 6), (0, 13)))
    V_ = pltpu.VMEM
    dma = pltpu.SemaphoreType.DMA
    blk = (16, CW)
    scratch = [
        V_((3, 2, 2, 4, 2, 2, 5, 16, CW), BF), V_((3, 5) + blk, BF), V_((3, 4) + blk, BF),
        V_((13, L, D), BF), V_((L, D), F32), V_((L, D), F32), V_((L, D), F32), V_((L, D), F32),
        V_((8, 256, 256), F32), V_((L, 128), F32), V_((L, 128), F32), V_((8, D), F32), V_((4, 8, D), F32),
        V_((2, 4, 2, 2, 5) + blk, BF), V_((3, 3, 2, 4, 2, 2) + blk, BF),
        V_((3, 1, 2, 4, 2) + blk, BF), V_((3, 3, 4) + blk, BF), V_((3, 3) + blk, BF),
        V_((3, 3, 4, 2) + blk, BF), V_((3, 3, 2) + blk, BF), V_((3, 1) + blk, BF),
        V_((3, 3, 2, 2, 2) + blk, BF), V_((3, 3, 2) + blk, BF), V_((3, 1) + blk, BF),
        V_((3,) + blk, BF), V_((3, 5) + blk, BF), V_((3, 4, 2) + blk, BF),
        V_((2, 32, 640), BF), V_((4, 3, 32, 640), BF), V_((2, 24, 640), F32), V_((4, 3, 24, 640), F32),
        dma((9, 14)), dma((9, 14)), dma((3, 8)), dma((3, 5)),
        dma((9, 2)), dma((9, 2)), dma((9, 10)), dma((9, 10)), dma((3, 5)), dma((3, 8)),
        dma((5, 3)), dma((5, 3)), dma((5, 3)), dma((5, 3)),
    ]
    vm = pl.BlockSpec(memory_space=pltpu.VMEM)
    sm = pl.BlockSpec(memory_space=pltpu.SMEM)
    res = pl.pallas_call(
        block_kernel,
        out_shape=[jax.ShapeDtypeStruct((L, D), BF), jax.ShapeDtypeStruct((L, D), F32), jax.ShapeDtypeStruct((10, 24), F32),
                   jax.ShapeDtypeStruct((10, 3 * D), F32)] + [jax.ShapeDtypeStruct((10, D), F32)] * 3,
        in_specs=[vm, vm, sm, vm, vm, vm, vm, vm],
        out_specs=[vm] * 7,
        scratch_shapes=scratch,
        compiler_params=pltpu.CompilerParams(collective_id=0, has_side_effects=True, vmem_limit_bytes=62 * 2**20),
        name="block",
    )(latents.reshape(L, D), cotangent.reshape(L, D), script_ids, small, w_qkv, w_out, w_up, w_down)
    o_lat, o_in, o_small, o_qkv, o_out, o_up, o_down = res
    return (o_lat.reshape(1, L, D), o_in.reshape(1, L, D), o_small[:, :16], o_small[:, 16], o_qkv, o_out,
            o_small[:, 17], o_small[:, 18], o_up, o_down)


def solution(mesh):
    row = P(("dp", "fsdp"), None)
    vec = P(("dp", "fsdp"))
    item = P("dp", None, None)
    return jax.shard_map(
        per_device,
        mesh=mesh,
        in_specs=(item, P("dp"), row, vec, row, row, vec, vec, row, row, item),
        out_specs=(item, item, row, vec, row, row, vec, vec, row, row),
        check_vma=False,
    )
```

```python
import math

import jax
import jax.numpy as jnp
from jax import lax
from jax.experimental import pallas as pl
from jax.experimental.pallas import tpu as pltpu
from jax.sharding import PartitionSpec as P

HEADS = 8
HD = 160
D = 1280
L = 256
EPS = 1e-5
SCALE = 1.0 / math.sqrt(HD)
BF = jnp.bfloat16
F32 = jnp.float32

MESH = pl.DeviceIdType.MESH
CW = 640

class Pos:
    def __init__(s):
        dp = lax.axis_index("dp"); s.xh = lax.axis_index("fsdp")
        s.c = dp % 2; s.y = (dp // 2) % 4; s.xl = (dp // 8) % 2; s.z = dp // 16
        s.x = s.xh * 2 + s.xl; s.h = s.y // 2; s.par = s.y % 2
    def dev(s, x=None, y=None, z=None, c=None):
        x = s.x if x is None else x; y = s.y if y is None else y
        z = s.z if z is None else z; c = s.c if c is None else c
        return (((z * 2 + x % 2) * 4 + y) * 2 + c, x // 2)
    def ring(s, ax, d):
        if ax == 0: return s.dev(x=(s.x + d) % 4)
        if ax == 1: return s.dev(y=(s.y + d) % 4)
        return s.dev(z=(s.z + d) % 4)
    def coord(s, ax, d):
        return ((s.x, s.y, s.z)[ax] + d) % 4

class AG:
    def __init__(s, p, W, stg, pieces, ssem, rsem, sib_r, s0s, s0r):
        s.p, s.W, s.stg, s.pieces = p, W, stg, pieces
        s.ssem, s.rsem, s.s0s, s.s0r = ssem, rsem, s0s, s0r
    def partners(s):
        p = s.p
        out = []
        for ax in range(3):
            for d in (1, 2, 3): out.append(p.ring(ax, d))
        for dy in (0, 1):
            for dx in (0, 1):
                for dc in (0, 1):
                    if (dy, dx, dc) == (0, 0, 0): continue
                    if (dy, dx, dc) == (0, 1, 0): continue
                    y = p.y ^ dy if dy else p.y
                    x = (p.x + 2 * dx) % 4
                    out.append(p.dev(x=x, y=y, c=(p.c + dc) % 2))
        return out
    def s0_targets(s):
        p = s.p
        res = []
        for dy in (0, 1):
            for dx in (0, 1):
                y = p.y ^ dy if dy else p.y
                x = (p.x + 2 * dx) % 4
                res.append((dy, dx, y, x))
        return res
    def s0_src(s):
        p = s.p
        return (p.par * 2 + p.c) * 2 + p.xh
    def s0(s, ph, act):
        p = s.p; o = s.s0_src()
        for tc in (0, 1):
            cond = (o <= 4) if tc == 0 else (o >= 4)
            @pl.when(cond)
            def _(tc=tc):
                for i, (dy, dx, y, x) in enumerate(s.s0_targets()):
                    chunk = (x // 2) * 2 + y % 2
                    src = s.pieces.at[ph, chunk]
                    dst = s.stg.at[ph, o - 4 * tc]
                    if dy == 0 and dx == 0:
                        @pl.when(p.c == tc)
                        def _():
                            cp = pltpu.make_async_copy(src, dst, s.s0r.at[ph, o - 4 * tc])
                            if act == 'start': cp.start()
                        @pl.when(p.c != tc)
                        def _():
                            cp = pltpu.make_async_remote_copy(src, dst, s.s0s.at[ph, i * 2 + tc], s.s0r.at[ph, o - 4 * tc], device_id=p.dev(y=y, x=x, c=tc), device_id_type=MESH)
                            if act == 'start': cp.start()
                            else: cp.wait_send()
                    else:
                        cp = pltpu.make_async_remote_copy(src, dst, s.s0s.at[ph, i * 2 + tc], s.s0r.at[ph, o - 4 * tc], device_id=p.dev(y=y, x=x, c=tc), device_id_type=MESH)
                        if act == 'start': cp.start()
                        else: cp.wait_send()
    def s0_recv(s, ph):
        p = s.p
        for k in range(5):
            def w(k=k):
                pltpu.make_async_copy(s.pieces.at[ph, 0], s.stg.at[ph, k], s.s0r.at[ph, k]).wait()
            if k < 4: w()
            else: pl.when(p.c == 0)(w)
    def compact(s, ph):
        p = s.p
        i = lax.broadcasted_iota(jnp.int32, (48, 80), 0)
        k = lax.broadcasted_iota(jnp.int32, (48, 80), 1)
        r = 48 * p.c + i
        q = (r * 205) >> 11
        col = (q - 4 * p.c) * 16 + (r - q * 10)
        P = jnp.where(k == col, 1.0, 0.0).astype(jnp.bfloat16)
        res = jnp.dot(P, s.stg[ph].reshape(80, CW), preferred_element_type=jnp.float32).astype(jnp.bfloat16)
        def put(ts):
            s.W[ph, p.xh, p.par, p.z, p.xl, p.h, 3 * p.c + ts] = res[ts * 16:(ts + 1) * 16]
        put(0); put(1)
        pl.when(p.c == 0)(lambda: put(2))
    def order(s, ph, ts):
        a = (ph + ts) % 3
        return ((a + 1) % 3, (a + 2) % 3, a)
    def region(s, ph, t, full, over=None):
        p = s.p; o = over or {}
        x = o.get(0); y = o.get(1); z = o.get(2)
        xh, xl = (p.xh, p.xl) if x is None else (x // 2, x % 2)
        h, par = (p.h, p.par) if y is None else (y // 2, y % 2)
        zz = p.z if z is None else z
        if 0 in full: xh = xl = slice(None)
        if 1 in full: h = par = slice(None)
        if 2 in full: zz = slice(None)
        return [ph, xh, par, zz, xl, h, t]
    def ref(s, reg): return s.W.at[tuple(reg)]
    def cp(s, reg, slot, k, dev):
        r = s.ref(reg)
        return pltpu.make_async_remote_copy(r, r, s.ssem.at[slot, k], s.rsem.at[slot, k], device_id=dev, device_id_type=MESH)
    def half(s, reg, full, hf):
        reg = list(reg)
        i = 3 if 2 in full else (1 if 0 in full else 2)
        reg[i] = pl.ds(hf * 2, 2) if i == 3 else pl.ds(hf, 1)
        return reg
    def slot(s, ph, ts): return ph * 3 + ts
    def t(s, ts): return 3 * s.p.c + ts
    def g(s, ts, f):
        if ts < 2: f()
        else: pl.when(s.p.c == 0)(f)
    def direct(s, stage, ph, ts, act):
        a = s.order(ph, ts); full = a[:stage]; ax = a[stage]
        for d in (1, 3, 2):
            k = stage * 3 + d - 1
            if act == 'recv':
                s.cp(s.region(ph, s.t(ts), full, {ax: s.p.coord(ax, -d)}), s.slot(ph, ts), k, s.p.ring(ax, d)).wait_recv()
            else:
                c = s.cp(s.region(ph, s.t(ts), full), s.slot(ph, ts), k, s.p.ring(ax, d))
                c.start() if act == 'start' else c.wait_send()
    def s3(s, ph, ts, what, act):
        a = s.order(ph, ts); full = a[:2]; ax = a[2]; sl = s.slot(ph, ts); tt = s.t(ts)
        R, L = s.p.ring(ax, 1), s.p.ring(ax, 3)
        own = s.region(ph, tt, full)
        fl = s.region(ph, tt, full, {ax: s.p.coord(ax, -1)})
        fr = s.region(ph, tt, full, {ax: s.p.coord(ax, 1)})
        op = s.region(ph, tt, full, {ax: s.p.coord(ax, 2)})
        if what == 'own':
            if act == 'recvL': s.cp(fl, sl, 6, R).wait_recv()
            elif act == 'recvR': s.cp(fr, sl, 7, L).wait_recv()
            else:
                for reg, k, dv in ((own, 6, R), (own, 7, L)):
                    c = s.cp(reg, sl, k, dv)
                    c.start() if act == 'start' else c.wait_send()
        elif what == 'fwdR':
            if act == 'recv': s.cp(s.half(op, full, 0), sl, 8, R).wait_recv()
            else:
                c = s.cp(s.half(fl, full, 0), sl, 8, R)
                c.start() if act == 'start' else c.wait_send()
        elif what == 'fwdL':
            if act == 'recv': s.cp(s.half(op, full, 1), sl, 9, L).wait_recv()
            else:
                c = s.cp(s.half(fr, full, 1), sl, 9, L)
                c.start() if act == 'start' else c.wait_send()
    def sib(s, ph, ts, piece, act):
        a = s.order(ph, ts); full = a[:2]; ax = a[2]
        d = (0, -1, 1, 2)[piece]
        dv = s.p.dev(c=1 - s.p.c)
        t = s.t(ts) if act != 'recv' else 3 * (1 - s.p.c) + ts
        c = s.cp(s.region(ph, t, full, {ax: s.p.coord(ax, d)}), s.slot(ph, ts), 10 + piece, dv)
        if act == 'start': c.start()
        elif act == 'recv': c.wait_recv()
        else: c.wait_send()
    def go(s, ts, f, other=False):
        def h():
            f()
        if ts < 2: h()
        else: pl.when(s.p.c == (1 if other else 0))(h)
    def phase_a(s, ph):
        for ts in range(3): s.go(ts, lambda ts=ts: s.direct(0, ph, ts, 'start'))
    def phase_b(s, ph):
        for ts in range(3):
            s.go(ts, lambda ts=ts: (s.direct(0, ph, ts, 'recv'), s.direct(1, ph, ts, 'start')))
    def phase_c(s, ph):
        for ts in range(3):
            s.go(ts, lambda ts=ts: (s.direct(1, ph, ts, 'recv'), s.s3(ph, ts, 'own', 'start'), s.sib(ph, ts, 0, 'start')))
    def phase_d(s, ph):
        for ts in range(3):
            s.go(ts, lambda ts=ts: (
                s.s3(ph, ts, 'own', 'recvL'), s.s3(ph, ts, 'fwdR', 'start'), s.sib(ph, ts, 1, 'start'),
                s.s3(ph, ts, 'own', 'recvR'), s.s3(ph, ts, 'fwdL', 'start'), s.sib(ph, ts, 2, 'start')))
    def phase_e(s, ph):
        for ts in range(3):
            s.go(ts, lambda ts=ts: (s.s3(ph, ts, 'fwdR', 'recv'), s.s3(ph, ts, 'fwdL', 'recv'), s.sib(ph, ts, 3, 'start')))
    def phase_f(s, ph):
        for ts in range(3):
            s.go(ts, lambda ts=ts: [s.sib(ph, ts, k, 'recv') for k in range(4)], other=True)
    def drain(s, ph):
        s.s0(ph, 'wait_send')
        for ts in range(3):
            s.go(ts, lambda ts=ts: (s.direct(0, ph, ts, 'ws'), s.direct(1, ph, ts, 'ws'), s.s3(ph, ts, 'own', 'ws'),
                 s.s3(ph, ts, 'fwdR', 'ws'), s.s3(ph, ts, 'fwdL', 'ws'), [s.sib(ph, ts, k, 'ws') for k in range(4)]))

def barrier(partners):
    b = pltpu.get_barrier_semaphore()
    for d in partners:
        pl.semaphore_signal(b, inc=1, device_id=d, device_id_type=MESH)
    pl.semaphore_wait(b, len(partners))

def fill_pieces(pieces, wqkv, wout, wup, wdown):
    mats = [(wqkv, 0), (wqkv, 1280), (wqkv, 2560), (wout, 0), (wup, 0), (wdown, 0)]
    for ph in range(3):
        for xh in range(2):
            r, off = mats[2 * ph + xh]
            for par in range(2):
                v = r[:, off + par * 640: off + (par + 1) * 640]
                pieces[ph, 2 * xh + par] = jnp.concatenate([v.astype(jnp.float32), jnp.zeros((6, 640), jnp.float32)], axis=0).astype(jnp.bfloat16)


def dot(a, b):
    return jnp.dot(a, b, preferred_element_type=F32)


def dot_nt(a, b):
    return lax.dot_general(a, b, (((1,), (1,)), ((), ())), preferred_element_type=F32)


def dot_tn(a, b):
    return lax.dot_general(a, b, (((0,), (0,)), ((), ())), preferred_element_type=F32)


class Small:
    def __init__(s, p, buf, recv, ssem, rsem, rings):
        s.p, s.buf, s.recv, s.ssem, s.rsem, s.rings = p, buf, recv, ssem, rsem, rings

    def cps(s, k):
        p = s.p
        n = len(s.rings)
        if k == 0 or k == n + 1:
            src = s.buf.at[1 - p.c] if k == 0 else s.buf.at[p.c]
            dst = s.recv.at[0, 0] if k == 0 else s.recv.at[0, 1]
            return [pltpu.make_async_remote_copy(src, dst, s.ssem.at[k, 0], s.rsem.at[k, 0], device_id=p.dev(c=1 - p.c), device_id_type=MESH)]
        return [pltpu.make_async_remote_copy(s.buf.at[p.c], s.recv.at[k, i], s.ssem.at[k, i], s.rsem.at[k, i], device_id=dv, device_id_type=MESH)
                for i, dv in enumerate(s.rings[k - 1])]

    def start(s, k):
        for c in s.cps(k): c.start()

    def finish(s, k):
        p = s.p
        n = len(s.rings)
        cs = s.cps(k)
        if k == n + 1:
            cs[0].wait_recv()
            cs[0].wait_send()
            s.buf[1 - p.c] = s.recv[0, 1]
            return
        for c in cs: c.wait_recv()
        for c in cs: c.wait_send()
        acc = s.buf[p.c].astype(F32)
        for i in range(len(cs)):
            acc = acc + s.recv[k, i].astype(F32)
        s.buf[p.c] = acc.astype(s.buf.dtype)


class RS:
    def __init__(s, p, G, RD, bufs, FR, EX, FIN, dss, drs, ss, rs, fs, fr):
        s.p, s.G, s.RD, s.bufs, s.FR, s.EX, s.FIN = p, G, RD, bufs, FR, EX, FIN
        s.dss, s.drs, s.ss, s.rs, s.fs, s.fr = dss, drs, ss, rs, fs, fr

    def gref(s, ph):
        return s.G[ph]

    def go(s, ts, f, other=False):
        def h():
            f()
        if ts < 2: h()
        else: pl.when(s.p.c == (1 if other else 0))(h)

    def d2d(s, ph, ts, act, par):
        p = s.p
        g = s.gref(ph)
        t = 3 * (1 - p.c) + ts if act != 'recv' else 3 * p.c + ts
        if True:
            cp = pltpu.make_async_remote_copy(g.at[par, :, :, :, t], s.RD.at[ph, ts, par], s.dss.at[ph * 3 + ts, par], s.drs.at[ph * 3 + ts, par], device_id=p.dev(c=1 - p.c), device_id_type=MESH)
            if act == 'start': cp.start()
            elif act == 'ws': cp.wait_send()
            else: cp.wait_recv()

    def d2d_start(s, ph, par):
        for ts in range(3): s.go(ts, lambda ts=ts: s.d2d(ph, ts, 'start', par), other=True)

    def d2d_add(s, ph, ts, par):
        g = s.gref(ph)
        t = 3 * s.p.c + ts
        s.d2d(ph, ts, 'recv', par)
        def body(z, _):
            g[par, z, :, :, t] = (g[par, z, :, :, t].astype(F32) + s.RD[ph, ts, par, z].astype(F32)).astype(BF)
            return 0
        lax.fori_loop(0, 4, body, 0)

    def order(s, ph, ts):
        return ((1, 0, 2), (2, 0, 1), (0, 1, 2))[ts]

    def fidx(s, ph, ts):
        return (1, 2, 0)[ts]

    def piece(s, ph, ts, st, k):
        p = s.p
        o = s.order(ph, ts)
        ax = o[st]
        done = o[:st]
        par = h = zz = xl = slice(None)
        if 0 in done: xl = p.xl
        if 1 in done: h, par = p.h, p.par
        if 2 in done: zz = p.z
        if ax == 0: xl = k
        if ax == 1: h, par = k // 2, k % 2
        if ax == 2: zz = k
        return s.gref(ph).at[par, zz, xl, h, 3 * p.c + ts]

    def half(s, ph, ts, st, k, hf):
        p = s.p
        o = s.order(ph, ts)
        ax = o[st]
        assert st == 0
        t = 3 * p.c + ts
        if ax == 1: return s.gref(ph).at[k % 2, pl.ds(2 * hf, 2), :, k // 2, t]
        return s.gref(ph).at[hf, k, :, :, t]

    def bhalf(s, ph, ts, hf):
        f = s.fidx(ph, ts)
        b = s.bufs[f][0]
        if f == 1: return b.at[ph, 2, pl.ds(2 * hf, 2)]
        return b.at[ph, 2, hf]

    def cp(s, src, dst, sl, k, dev):
        return pltpu.make_async_remote_copy(src, dst, s.ss.at[sl, k], s.rs.at[sl, k], device_id=dev, device_id_type=MESH)

    def add(s, dst, srcs):
        lead = dst.shape[:-2]
        if len(lead) >= 1 and lead[0] > 1:
            def body(i, _):
                acc = dst[i].astype(F32)
                for r in srcs: acc = acc + r[i].astype(F32)
                dst[i] = acc.astype(BF)
                return 0
            lax.fori_loop(0, lead[0], body, 0)
        else:
            acc = dst[...].astype(F32)
            for r in srcs: acc = acc + r[...].astype(F32)
            dst[...] = acc.astype(BF)

    def sem(s, st, i):
        return (0, 4, 7)[st] + i

    def ring_cps(s, ph, ts, st):
        p = s.p
        o = s.order(ph, ts)
        ax = o[st]
        f = s.fidx(ph, ts)
        sl = ph * 3 + ts
        b = s.bufs[f][st]
        if ax == 0:
            k = 1 - p.xl
            src, dv = s.piece(ph, ts, st, k), p.dev(x=p.xh * 2 + k)
            if st == 0: return [s.cp(src.at[par], b.at[ph, 0, par], sl, par, dv) for par in range(2)]
            return [s.cp(src, b.at[ph, 0], sl, s.sem(st, 0), dv)]
        res = []
        for i, d in enumerate((1, 3, 2)):
            res.append(s.cp(s.piece(ph, ts, st, p.coord(ax, d)), b.at[ph, i], sl, s.sem(st, i), p.ring(ax, d)))
        return res

    def first_a(s, ph, ts, par):
        ax = s.order(ph, ts)[0]
        if ax == 0:
            s.ring_cps(ph, ts, 0)[par].start()
        elif ax == 2:
            s.sf_half(ph, ts)[1 - par].start()
        else:
            @pl.when(s.p.par == par)
            def _():
                for c in s.sf_half(ph, ts): c.start()

    def sf_half(s, ph, ts):
        p = s.p
        ax = s.order(ph, ts)[0]
        sl = ph * 3 + ts
        k = p.coord(ax, 2)
        return [s.cp(s.half(ph, ts, 0, k, 1), s.bhalf(ph, ts, 1), sl, 2, p.ring(ax, 1)),
                s.cp(s.half(ph, ts, 0, k, 0), s.bhalf(ph, ts, 0), sl, 3, p.ring(ax, 3))]

    def sf_full(s, ph, ts):
        p = s.p
        ax = s.order(ph, ts)[0]
        sl = ph * 3 + ts
        b = s.bufs[s.fidx(ph, ts)][0]
        return [s.cp(s.piece(ph, ts, 0, p.coord(ax, 1)), b.at[ph, 0], sl, 0, p.ring(ax, 1)),
                s.cp(s.piece(ph, ts, 0, p.coord(ax, 3)), b.at[ph, 1], sl, 1, p.ring(ax, 3))]

    def first_b(s, ph, ts):
        p = s.p
        o = s.order(ph, ts)
        ax = o[0]
        if ax == 0: return
        hb = s.sf_half(ph, ts)
        full = s.sf_full(ph, ts)
        hb[0].wait_recv()
        s.add(s.half(ph, ts, 0, p.coord(ax, 1), 1), [s.bhalf(ph, ts, 1)])
        full[0].start()
        hb[1].wait_recv()
        s.add(s.half(ph, ts, 0, p.coord(ax, 3), 0), [s.bhalf(ph, ts, 0)])
        full[1].start()

    def first_c(s, ph, ts):
        p = s.p
        o = s.order(ph, ts)
        ax = o[0]
        me = (p.xl, p.y, p.z)[ax]
        b = s.bufs[s.fidx(ph, ts)][0]
        if ax == 0:
            for par, c in enumerate(s.ring_cps(ph, ts, 0)):
                c.wait_recv()
                s.add(s.piece(ph, ts, 0, me).at[par], [b.at[ph, 0, par]])
            return
        cs = s.sf_full(ph, ts)
        for c in cs: c.wait_recv()
        s.add(s.piece(ph, ts, 0, me), [b.at[ph, i] for i in range(len(cs))])

    def next_start(s, ph, ts, st):
        for c in s.ring_cps(ph, ts, st): c.start()

    def next_finish(s, ph, ts, st):
        p = s.p
        ax = s.order(ph, ts)[st]
        me = (p.xl, p.y, p.z)[ax]
        b = s.bufs[s.fidx(ph, ts)][st]
        cs = s.ring_cps(ph, ts, st)
        for c in cs: c.wait_recv()
        s.add(s.piece(ph, ts, st, me), [b.at[ph, i] for i in range(len(cs))])

    def each(s, f):
        for ts in range(3): s.go(ts, lambda ts=ts: f(ts))

    def first(s, ph, par):
        s.each(lambda ts: (s.d2d_add(ph, ts, par), s.first_a(ph, ts, par)))

    def step(s, ph, k):
        if k == 2: s.each(lambda ts: s.first_b(ph, ts))
        elif k == 3: s.each(lambda ts: (s.first_c(ph, ts), s.next_start(ph, ts, 1)))
        elif k == 4: s.each(lambda ts: (s.next_finish(ph, ts, 1), s.next_start(ph, ts, 2)))
        elif k == 5:
            s.each(lambda ts: s.next_finish(ph, ts, 2))
            s.final_start(ph)

    def fin_cps(s, ph, k):
        p = s.p
        o = 4 * p.c + k
        chunk = 2 * p.xh + p.par
        dev = p.dev(x=(o % 2) * 2 + p.xl, y=2 * p.h + o // 4, c=(o // 2) % 2)
        return pltpu.make_async_remote_copy(s.EX.at[ph, k], s.FIN.at[ph, chunk, p.c], s.fs.at[ph, k], s.fr.at[ph, chunk * 2 + p.c], device_id=dev, device_id_type=MESH)

    def myo(s):
        p = s.p
        return (p.par * 2 + p.c) * 2 + p.xh

    def final_start(s, ph):
        p = s.p
        g = s.gref(ph)
        def put(ts):
            s.FR[ts] = g[p.par, p.z, p.xl, p.h, 3 * p.c + ts]
        put(0); put(1)
        pl.when(p.c == 0)(lambda: put(2))
        i = lax.broadcasted_iota(jnp.int32, (80, 48), 1)
        k = lax.broadcasted_iota(jnp.int32, (80, 48), 0)
        r = 48 * p.c + i
        q = (r * 205) >> 11
        col = (q - 4 * p.c) * 16 + (r - q * 10)
        pt = jnp.where(k == col, 1.0, 0.0).astype(BF)
        s.EX[ph] = dot(pt, s.FR[...].reshape(48, CW)).astype(BF).reshape(5, 16, CW)
        for k in range(5):
            def send(k=k):
                me = 4 * p.c + k == s.myo()
                @pl.when(me)
                def _():
                    s.FIN[ph, 2 * p.xh + p.par, p.c] = s.EX[ph, k]
                @pl.when(jnp.logical_not(me))
                def _():
                    s.fin_cps(ph, k).start()
            if k < 4: send()
            else: pl.when(p.c == 0)(send)

    def final_wait(s, ph):
        p = s.p
        o = s.myo()
        for chunk in range(4):
            for sc in range(2):
                c1 = (o <= 4) if sc == 0 else (o >= 4)
                mine = jnp.logical_and(chunk == 2 * p.xh + p.par, sc == p.c)
                @pl.when(jnp.logical_and(c1, jnp.logical_not(mine)))
                def _(chunk=chunk, sc=sc):
                    pltpu.make_async_remote_copy(s.EX.at[ph, 0], s.FIN.at[ph, chunk, sc], s.fs.at[ph, 0], s.fr.at[ph, chunk * 2 + sc], device_id=p.dev(c=1 - p.c), device_id_type=MESH).wait_recv()

    def drain(s, ph):
        p = s.p
        for ts in range(3):
            for par in range(2): s.go(ts, lambda ts=ts: s.d2d(ph, ts, 'ws', par), other=True)
            def ws(ts=ts):
                if s.order(ph, ts)[0] == 0:
                    for c in s.ring_cps(ph, ts, 0): c.wait_send()
                else:
                    for c in s.sf_half(ph, ts) + s.sf_full(ph, ts): c.wait_send()
                for st in (1, 2):
                    for c in s.ring_cps(ph, ts, st): c.wait_send()
            s.go(ts, ws)
        for k in range(5):
            def w(k=k):
                pl.when(4 * p.c + k != s.myo())(lambda: s.fin_cps(ph, k).wait_send())
            if k < 4: w()
            else: pl.when(p.c == 0)(w)


def clear_last(stg, FR):
    stg[:, 4] = jnp.zeros((3, 16, CW), BF)
    FR[2] = jnp.zeros((16, CW), BF)


FIRST, Q, K, V, MIXED, SECOND, ACTIVE, GU, GAO, GMX, GQ, GK, GV = range(13)
RB = 32


def block_kernel(lat_in, cot_in, sid, *refs):
    small_in, (o_lat, o_in), small_out = refs[0:8], refs[8:10], refs[10:16]
    block_body(lat_in, cot_in, sid, small_in, o_lat, o_in, small_out, *refs[16:])


def block_body(lat_in, cot_in, sid, small_in, o_lat, o_in, small_out,
                 W, stg, pieces, A, N1, N2, MID, DG, PR, I1, I2, VEC, CS, G2, RD, b00, b01, b02, b10, b11, b12, b20, b21, b22,
                 FR, EX, FIN, SB, SBR, SG, SGR,
                 lat, cot, gt, b1, g2, b2, wq, wo, wu, wd, o_tab, o_vec, o_qkv, o_out, o_up, o_down, ssem, rsem, s0s, s0r, dss, drs, gss, grs, fs, fr, sbs, sbr, sgs, sgr, io):
    p = Pos()
    ag = AG(p, W, stg, pieces, ssem, rsem, None, s0s, s0r)
    G = [W.at[2, 0], W.at[2, 1], G2]
    rs = RS(p, G, RD, [[b00, b01, b02], [b10, b11, b12], [b20, b21, b22]], FR, EX, FIN, dss, drs, gss, grs, fs, fr)
    ring3 = lambda ax: [p.ring(ax, d) for d in (1, 3, 2)]
    sb = Small(p, SB, SBR, sbs, sbr, [ring3(0), ring3(1), ring3(2)])
    sg = Small(p, SG, SGR, sgs, sgr, [ring3(1), ring3(2), [p.dev(x=p.xh * 2 + 1 - p.xl)]])
    idx = lax.axis_index("dp") * 2 + p.xh

    parts = ag.partners()
    bar = pltpu.get_barrier_semaphore()
    for d in parts:
        pl.semaphore_signal(bar, inc=1, device_id=d, device_id_type=MESH)
    in_lat = pltpu.make_async_copy(lat_in, lat, io.at[0])
    in_cot = pltpu.make_async_copy(cot_in, cot, io.at[1])
    ins = [pltpu.make_async_copy(a, v, io.at[4 + i]) for i, (a, v) in enumerate(zip(small_in, (gt, b1, g2, b2, wq, wo, wu, wd)))]
    for c in ins: c.start()
    in_lat.start(); in_cot.start()
    for c in ins: c.wait()
    fill_pieces(pieces, wq, wo, wu, wd)
    pl.when(p.c == 1)(lambda: clear_last(stg, FR))
    j = lax.broadcasted_iota(jnp.int32, (16, D), 0)
    lane = lax.broadcasted_iota(jnp.int32, (16, D), 1)
    own = jnp.where(jnp.logical_and(lane == idx * 10 + j, j < 10), 1.0, 0.0)
    own16 = own[0:10].astype(BF)
    spread = [dot_tn(gt[...], own16)] + [dot(jnp.broadcast_to(b[...].reshape(1, 10), (8, 10)), own16)[0:1] for b in (b1, g2, b2)] + [jnp.zeros((13, D), F32)]
    spread = jnp.concatenate(spread, axis=0).astype(BF)
    for k in range(2): SB[k] = spread[:, k * 640:(k + 1) * 640]
    pl.semaphore_wait(bar, len(parts))

    sb.start(0)
    for ph in range(3): ag.s0(ph, 'start')

    def ln1(r, _):
        rows = pl.ds(pl.multiple_of(r * RB, RB), RB)
        x = lat[rows, :].astype(F32)
        mu = jnp.mean(x, axis=-1, keepdims=True)
        xc = x - mu
        inv = lax.rsqrt(jnp.mean(xc * xc, axis=-1, keepdims=True) + EPS)
        N1[rows, :] = xc * inv
        I1[rows, :] = jnp.broadcast_to(inv, (RB, 128))
        return 0
    in_lat.wait(); in_cot.wait()
    lax.fori_loop(0, L // RB, ln1, 0)
    ag.s0_recv(0); ag.compact(0); ag.phase_a(0)
    sb.finish(0); sb.start(1)
    ag.s0_recv(1); ag.compact(1); ag.phase_a(1)
    ag.phase_b(0)
    sb.finish(1); sb.start(2)
    ag.s0_recv(2); ag.compact(2); ag.phase_a(2)
    ag.phase_b(1)
    ag.phase_c(0)
    sb.finish(2); sb.start(3)
    ag.phase_b(2)
    ag.phase_c(1)
    sb.finish(3); sb.start(4)
    A[MIXED] = jnp.zeros((L, D), BF)
    for k in (GQ, GK, GV): A[k] = jnp.zeros((L, D), BF)
    CS[...] = jnp.zeros_like(CS)
    ag.phase_d(0)
    ag.phase_c(2)
    sb.finish(4)
    lane32 = lax.broadcasted_iota(jnp.int32, (8, 32), 1)
    sub8 = lax.broadcasted_iota(jnp.int32, (8, 32), 0)
    tgt = jnp.where(sub8 == 0, sid[0], jnp.where(sub8 < 4, 15 + sub8, -1))
    pick = jnp.where(lane32 == tgt, 1.0, 0.0).astype(BF)
    for k in range(2): VEC[:, k * 640:(k + 1) * 640] = dot(pick, SB[k])

    def mk_first(r, _):
        rows = pl.ds(pl.multiple_of(r * RB, RB), RB)
        A[FIRST, rows, :] = (N1[rows, :] * VEC[0:1, :] + VEC[1:2, :]).astype(BF)
        return 0
    lax.fori_loop(0, L // RB, mk_first, 0)
    ag.phase_d(1)
    ag.phase_e(0)
    ag.phase_f(0)

    def wpan(ph, xh, par): return W[ph, xh, par].reshape(D, CW)
    def cols(par): return pl.ds(par * CW, CW)

    for par in range(2):
        A[Q, :, cols(par)] = dot(A[FIRST], wpan(0, 0, par)).astype(BF)
    ag.phase_d(2)
    for par in range(2):
        A[K, :, cols(par)] = dot(A[FIRST], wpan(0, 1, par)).astype(BF)
    ag.phase_e(1)
    ag.phase_f(1)
    for par in range(2):
        A[V, :, cols(par)] = dot(A[FIRST], wpan(1, 0, par)).astype(BF)

    lane256 = lax.broadcasted_iota(jnp.int32, (1, 256), 1)
    def masks(w):
        m = jnp.where(jnp.logical_and(lane256 >= 32 * w, lane256 < 32 * w + HD), 1.0, 0.0)
        return m, m.astype(BF)
    def win(pn, w):
        return pl.ds(pl.multiple_of(pn * CW + w * 128, 128), 256)

    for pn in range(2):
        def att(w, _, pn=pn):
            cw = win(pn, w)
            m32, m16 = masks(w)
            sc = dot_nt(A[Q, :, cw] * m16, A[K, :, cw]) * SCALE
            e = jnp.exp(sc - jnp.max(sc, axis=-1, keepdims=True))
            pr = e * (1.0 / jnp.sum(e, axis=-1, keepdims=True))
            PR[pn * 4 + w] = pr
            mx = dot(pr.astype(BF), A[V, :, cw]) * m32
            A[MIXED, :, cw] = A[MIXED, :, cw] + mx.astype(BF)
            return 0
        lax.fori_loop(0, 4, att, 0, unroll=True)
    ag.phase_e(2)
    for par in range(2):
        MID[:, cols(par)] = lat[:, cols(par)].astype(F32) + dot(A[MIXED], wpan(1, 1, par))

    def ln2(r, _):
        rows = pl.ds(pl.multiple_of(r * RB, RB), RB)
        x = MID[rows, :]
        mu = jnp.mean(x, axis=-1, keepdims=True)
        xc = x - mu
        inv = lax.rsqrt(jnp.mean(xc * xc, axis=-1, keepdims=True) + EPS)
        n = xc * inv
        N2[rows, :] = n
        I2[rows, :] = jnp.broadcast_to(inv, (RB, 128))
        A[SECOND, rows, :] = (n * VEC[2:3, :] + VEC[3:4, :]).astype(BF)
        return 0
    lax.fori_loop(0, L // RB, ln2, 0)
    ag.phase_f(2)
    for par in range(2):
        DG[:, cols(par)] = dot(A[SECOND], wpan(2, 0, par))

    def gelu(r, _):
        rows = pl.ds(pl.multiple_of(r * RB, RB), RB)
        u = DG[rows, :]
        c0 = math.sqrt(2.0 / math.pi)
        u2 = u * u
        th = jnp.tanh(c0 * (u + 0.044715 * u2 * u))
        hp = 0.5 * (1.0 + th)
        A[ACTIVE, rows, :] = (u * hp).astype(BF)
        DG[rows, :] = hp + 0.5 * u * (1.0 - th * th) * (c0 * (1.0 + 3 * 0.044715 * u2))
        return 0
    lax.fori_loop(0, L // RB, gelu, 0)

    def back(src, ph, xh, n):
        acc = None
        for par in range(2):
            t = dot_nt(src(par), W[ph, xh, par, 2 * n:2 * n + 2].reshape(CW, CW))
            acc = t if acc is None else acc + t
        return acc

    for n in range(2):
        A[GU, :, cols(n)] = (back(lambda par: cot[:, cols(par)], 2, 1, n) * DG[:, cols(n)]).astype(BF)

    def wgrad(ph, l0, l1, r0, r1, par):
        li = jnp.where(p.xh == 0, l0, l1)
        ri = jnp.where(p.xh == 0, r0, r1)
        for n in range(2):
            v = dot_tn(A[li, :, cols(n)], A[ri, :, cols(par)])
            G[ph][par, 2 * n:2 * n + 2] = v.astype(BF).reshape(2, 2, 2, 5, 16, CW)
        rs.d2d_start(ph, par)

    A[GAO] = cot[...]
    wgrad(2, SECOND, ACTIVE, GU, GAO, 0)
    wgrad(2, SECOND, ACTIVE, GU, GAO, 1)
    for n in range(2):
        DG[:, cols(n)] = back(lambda par: A[GU, :, cols(par)], 2, 0, n)
        rs.first(2, n)
    for par in range(2):
        A[SECOND, :, cols(par)] = (MID[:, cols(par)] + dot(A[ACTIVE], wpan(2, 1, par))).astype(BF)
    out_lat = pltpu.make_async_copy(A.at[SECOND], o_lat, io.at[2])
    out_lat.start()

    def ln2b(r, _):
        rows = pl.ds(pl.multiple_of(r * RB, RB), RB)
        gs = DG[rows, :]
        n = N2[rows, :]
        CS[1] += jnp.sum((gs * n).reshape(RB // 8, 8, D), axis=0)
        CS[2] += jnp.sum(gs.reshape(RB // 8, 8, D), axis=0)
        dn = gs * VEC[2:3, :]
        m1 = jnp.mean(dn, axis=-1, keepdims=True)
        m2 = jnp.mean(dn * n, axis=-1, keepdims=True)
        gm = cot[rows, :].astype(F32) + I2[rows, 0:1] * (dn - m1 - n * m2)
        N2[rows, :] = gm
        A[GAO, rows, :] = gm.astype(BF)
        return 0
    lax.fori_loop(0, L // RB, ln2b, 0)
    for n in range(2):
        A[GMX, :, cols(n)] = back(lambda par: A[GAO, :, cols(par)], 1, 1, n).astype(BF)
        if n == 0: rs.step(2, 2)

    for pn in range(2):
        def attb(w, _, pn=pn):
            cw = win(pn, w)
            m32, m16 = masks(w)
            gm = A[GMX, :, cw] * m16
            qm = A[Q, :, cw] * m16
            pr = PR[pn * 4 + w]
            gp = dot_nt(gm, A[V, :, cw])
            rt = jnp.sum(gp * pr, axis=-1, keepdims=True)
            gsc = (pr * (gp - rt)).astype(BF)
            A[GV, :, cw] = A[GV, :, cw] + dot_tn(pr.astype(BF), gm).astype(BF)
            A[GQ, :, cw] = A[GQ, :, cw] + (dot(gsc, A[K, :, cw]) * SCALE * m32).astype(BF)
            A[GK, :, cw] = A[GK, :, cw] + (dot_tn(gsc, qm) * SCALE).astype(BF)
            return 0
        if pn == 0:
            lax.fori_loop(0, 4, attb, 0, unroll=True)
            ag.drain(2)
        else:
            lax.fori_loop(0, 2, attb, 0, unroll=True)
            rs.first(1, 0)
            rs.first(0, 0)
            lax.fori_loop(2, 4, attb, 0, unroll=True)
        wgrad(1, FIRST, MIXED, GV, GAO, pn)
        wgrad(0, FIRST, FIRST, GQ, GK, pn)
        rs.step(2, 3 + pn)
    for n in range(2):
        acc = None
        for g, (ph, xh) in ((GQ, (0, 0)), (GK, (0, 1)), (GV, (1, 0))):
            t = back(lambda par: A[g, :, cols(par)], ph, xh, n)
            acc = t if acc is None else acc + t
        MID[:, cols(n)] = acc
        rs.first(1 - n, 1)
    rs.step(1, 2)
    rs.step(0, 2)
    rs.step(2, 5)

    def ln1b(r, _):
        rows = pl.ds(pl.multiple_of(r * RB, RB), RB)
        gf = MID[rows, :]
        n = N1[rows, :]
        CS[3] += jnp.sum((gf * n).reshape(RB // 8, 8, D), axis=0)
        CS[0] += jnp.sum(gf.reshape(RB // 8, 8, D), axis=0)
        dn = gf * VEC[0:1, :]
        m1 = jnp.mean(dn, axis=-1, keepdims=True)
        m2 = jnp.mean(dn * n, axis=-1, keepdims=True)
        DG[rows, :] = N2[rows, :] + I1[rows, 0:1] * (dn - m1 - n * m2)
        return 0
    lax.fori_loop(0, L // RB, ln1b, 0)
    out_in = pltpu.make_async_copy(DG, o_in, io.at[3])
    out_in.start()
    sub24 = lax.broadcasted_iota(jnp.int32, (24, 640), 0)
    for k in range(2):
        v = [jnp.sum(CS[i, :, k * 640:(k + 1) * 640], axis=0, keepdims=True) for i in range(4)]
        SG[k] = (jnp.where(sub24 == sid[0], v[3], 0.0) + jnp.where(sub24 == 16, v[0], 0.0)
                 + jnp.where(sub24 == 17, v[1], 0.0) + jnp.where(sub24 == 18, v[2], 0.0))
    sg.start(0)
    ag.drain(0); ag.drain(1)
    rs.step(1, 3)
    sg.finish(0); sg.start(1)
    rs.step(0, 3)
    rs.step(1, 4)
    sg.finish(1); sg.start(2)
    rs.step(0, 4)
    rs.step(1, 5)
    sg.finish(2); sg.start(3)
    rs.step(0, 5)

    outs = [(o_qkv, 0), (o_qkv, 1280), (o_qkv, 2560), (o_out, 0), (o_up, 0), (o_down, 0)]
    def emit(ph):
        rs.final_wait(ph)
        o_id = rs.myo()
        sel = jnp.where(o_id > 4, 1, 0)
        @pl.when(o_id == 4)
        def _():
            FIN[ph, :, 0] = FIN[ph, :, 0] + FIN[ph, :, 1]
        for xh in range(2):
            o, off = outs[2 * ph + xh]
            for par in range(2):
                v = FIN[ph, 2 * xh + par, sel].astype(F32)
                o[:, off + par * 640: off + (par + 1) * 640] = v[0:10]
    emit(2)
    sg.finish(3); sg.start(4)
    emit(1)
    sg.finish(4)
    tab = None
    for k in range(2):
        ok = own[:, k * 640:(k + 1) * 640]
        t = lax.dot_general(ok, SG[k], (((1,), (1,)), ((), ())), precision=lax.Precision.HIGHEST, preferred_element_type=F32)
        u = lax.dot_general(SG[k, 16:24], ok, (((1,), (1,)), ((), ())), precision=lax.Precision.HIGHEST, preferred_element_type=F32)
        tab, vec = (t, u) if tab is None else (tab + t, vec + u)
    o_tab[...] = tab[0:10, 0:16]
    o_vec[...] = vec[:, 0:10]
    emit(0)
    outs = [pltpu.make_async_copy(v, o, io.at[4 + i]) for i, (v, o) in enumerate(zip((o_tab, o_vec, o_qkv, o_out, o_up, o_down), small_out))]
    for c in outs: c.start()
    for ph in range(3): rs.drain(ph)
    out_lat.wait(); out_in.wait()
    for c in outs: c.wait()


def results_kernel(lat, inp, tab, vec, qkv, out, up, down, o_lat, o_in, o_tab, o_b1, o_g2, o_b2, o_qkv, o_out, o_up, o_down, sem):
    cps = [pltpu.make_async_copy(a, o, sem.at[i]) for i, (a, o) in enumerate(((lat, o_lat), (inp, o_in), (qkv, o_qkv), (out, o_out), (up, o_up), (down, o_down)))]
    for c in cps: c.start()
    o_tab[...] = tab[...]
    for i, o in enumerate((o_b1, o_g2, o_b2)): o[...] = vec[i]
    for c in cps: c.wait()


def per_device(latents, script_ids, gain_table, bias_one, w_qkv, w_out, gain_two, bias_two, w_up, w_down, cotangent):
    V_ = pltpu.VMEM
    dma = pltpu.SemaphoreType.DMA
    blk = (16, CW)
    scratch = [
        V_((3, 2, 2, 4, 2, 2, 5, 16, CW), BF), V_((3, 5) + blk, BF), V_((3, 4) + blk, BF),
        V_((13, L, D), BF), V_((L, D), F32), V_((L, D), F32), V_((L, D), F32), V_((L, D), F32),
        V_((8, 256, 256), F32), V_((L, 128), F32), V_((L, 128), F32), V_((8, D), F32), V_((4, 8, D), F32),
        V_((2, 4, 2, 2, 5) + blk, BF), V_((3, 3, 2, 4, 2, 2) + blk, BF),
        V_((3, 1, 2, 4, 2) + blk, BF), V_((3, 3, 4) + blk, BF), V_((3, 3) + blk, BF),
        V_((3, 3, 4, 2) + blk, BF), V_((3, 1, 4) + blk, BF), V_((3, 3) + blk, BF),
        V_((3, 3, 2, 2, 2) + blk, BF), V_((3, 1, 2, 2) + blk, BF), V_((3, 3) + blk, BF),
        V_((3,) + blk, BF), V_((3, 5) + blk, BF), V_((3, 4, 2) + blk, BF),
        V_((2, 32, 640), BF), V_((4, 3, 32, 640), BF), V_((2, 24, 640), F32), V_((4, 3, 24, 640), F32), V_((L, D), BF), V_((L, D), BF),
        V_((10, 16), BF), V_((10,), BF), V_((10,), BF), V_((10,), BF), V_((10, 3 * D), BF), V_((10, D), BF), V_((10, D), BF), V_((10, D), BF),
        V_((10, 16), F32), V_((8, 10), F32), V_((10, 3 * D), F32), V_((10, D), F32), V_((10, D), F32), V_((10, D), F32),
        dma((9, 14)), dma((9, 14)), dma((3, 8)), dma((3, 5)),
        dma((9, 2)), dma((9, 2)), dma((9, 10)), dma((9, 10)), dma((3, 5)), dma((3, 8)),
        dma((5, 3)), dma((5, 3)), dma((5, 3)), dma((5, 3)), dma((12,)),
    ]
    vm = pl.BlockSpec(memory_space=pltpu.VMEM)
    sm = pl.BlockSpec(memory_space=pltpu.SMEM)
    hbm = pl.BlockSpec(memory_space=pl.ANY)
    f32 = lambda *d: jax.ShapeDtypeStruct(d, F32)
    res = pl.pallas_call(
        block_kernel,
        out_shape=[jax.ShapeDtypeStruct((L, D), BF), f32(L, D), f32(10, 16), f32(8, 10), f32(10, 3 * D), f32(10, D), f32(10, D), f32(10, D)],
        in_specs=[hbm, hbm, sm] + [hbm] * 8,
        out_specs=[hbm] * 8,
        scratch_shapes=scratch,
        compiler_params=pltpu.CompilerParams(collective_id=0, has_side_effects=True, vmem_limit_bytes=62 * 2**20),
        name="block",
    )(latents.reshape(L, D), cotangent.reshape(L, D), script_ids, gain_table, bias_one, gain_two, bias_two, w_qkv, w_out, w_up, w_down)
    o_lat, o_in, o_tab, o_b1, o_g2, o_b2, o_qkv, o_out, o_up, o_down = pl.pallas_call(
        results_kernel,
        out_shape=[jax.ShapeDtypeStruct((L, D), BF), f32(L, D), f32(10, 16), f32(10), f32(10), f32(10), f32(10, 3 * D), f32(10, D), f32(10, D), f32(10, D)],
        in_specs=[vm] * 8,
        out_specs=[hbm, hbm] + [vm] * 4 + [hbm] * 4,
        scratch_shapes=[dma((6,))],
        name="results",
    )(*res)
    return (o_lat.reshape(1, L, D), o_in.reshape(1, L, D), o_tab, o_b1, o_qkv, o_out, o_g2, o_b2, o_up, o_down)


def solution(mesh):
    row = P(("dp", "fsdp"), None)
    vec = P(("dp", "fsdp"))
    item = P("dp", None, None)
    return jax.shard_map(
        per_device,
        mesh=mesh,
        in_specs=(item, P("dp"), row, vec, row, row, vec, vec, row, row, item),
        out_specs=(item, item, row, vec, row, row, vec, vec, row, row),
        check_vma=False,
    )
```

```python
import math

import jax
import jax.numpy as jnp
from jax import lax
from jax.experimental import pallas as pl
from jax.experimental.pallas import tpu as pltpu
from jax.sharding import PartitionSpec as P

HEADS = 8
HD = 160
D = 1280
L = 256
EPS = 1e-5
SCALE = 1.0 / math.sqrt(HD)
BF = jnp.bfloat16
F32 = jnp.float32

MESH = pl.DeviceIdType.MESH
CW = 640

class Pos:
    def __init__(s):
        dp = lax.axis_index("dp"); s.xh = lax.axis_index("fsdp")
        s.c = dp % 2; s.y = (dp // 2) % 4; s.xl = (dp // 8) % 2; s.z = dp // 16
        s.x = s.xh * 2 + s.xl; s.h = s.y // 2; s.par = s.y % 2
    def dev(s, x=None, y=None, z=None, c=None):
        x = s.x if x is None else x; y = s.y if y is None else y
        z = s.z if z is None else z; c = s.c if c is None else c
        return (((z * 2 + x % 2) * 4 + y) * 2 + c, x // 2)
    def ring(s, ax, d):
        if ax == 0: return s.dev(x=(s.x + d) % 4)
        if ax == 1: return s.dev(y=(s.y + d) % 4)
        return s.dev(z=(s.z + d) % 4)
    def coord(s, ax, d):
        return ((s.x, s.y, s.z)[ax] + d) % 4

def wait(ref, sem):
    pltpu.make_async_copy(ref, ref, sem).wait()

class AG:
    def __init__(s, p, W, stg, pieces, ssem, rsem, sib_r, s0s, s0r):
        s.p, s.W, s.stg, s.pieces = p, W, stg, pieces
        s.ssem, s.rsem, s.s0s, s.s0r = ssem, rsem, s0s, s0r
    def partners(s):
        p = s.p
        out = []
        for ax in range(3):
            for d in (1, 2, 3): out.append(p.ring(ax, d))
        for dy in (0, 1):
            for dx in (0, 1):
                for dc in (0, 1):
                    if (dy, dx, dc) == (0, 0, 0): continue
                    if (dy, dx, dc) == (0, 1, 0): continue
                    y = p.y ^ dy if dy else p.y
                    x = (p.x + 2 * dx) % 4
                    out.append(p.dev(x=x, y=y, c=(p.c + dc) % 2))
        return out
    def s0_targets(s):
        p = s.p
        res = []
        for dy in (0, 1):
            for dx in (0, 1):
                y = p.y ^ dy if dy else p.y
                x = (p.x + 2 * dx) % 4
                res.append((dy, dx, y, x))
        return res
    def s0_src(s):
        p = s.p
        return (p.par * 2 + p.c) * 2 + p.xh
    def s0(s, ph):
        p = s.p; o = s.s0_src()
        for tc in (0, 1):
            cond = (o <= 4) if tc == 0 else (o >= 4)
            @pl.when(cond)
            def _(tc=tc):
                for dy, dx, y, x in s.s0_targets():
                    src = s.pieces.at[ph, (x // 2) * 2 + y % 2]
                    dst = s.stg.at[ph, o - 4 * tc]
                    def send(sem):
                        pltpu.make_async_remote_copy(src, dst, s.s0s.at[sem], s.s0r.at[ph], device_id=p.dev(y=y, x=x, c=tc), device_id_type=MESH).start()
                    if dy == 0 and dx == 0:
                        @pl.when(p.c == tc)
                        def _():
                            pltpu.make_async_copy(src, dst, s.s0r.at[ph]).start()
                        @pl.when(p.c != tc)
                        def _():
                            send(2)
                    else:
                        send(tc)
    def s0_recv(s, ph):
        pl.when(s.p.c == 0)(lambda: wait(s.stg.at[ph], s.s0r.at[ph]))
        pl.when(s.p.c == 1)(lambda: wait(s.stg.at[ph, 0:4], s.s0r.at[ph]))
    def compact(s, ph):
        p = s.p
        i = lax.broadcasted_iota(jnp.int32, (48, 80), 0)
        k = lax.broadcasted_iota(jnp.int32, (48, 80), 1)
        r = 48 * p.c + i
        q = (r * 205) >> 11
        col = (q - 4 * p.c) * 16 + (r - q * 10)
        P = jnp.where(k == col, 1.0, 0.0).astype(jnp.bfloat16)
        res = jnp.dot(P, s.stg[ph].reshape(80, CW), preferred_element_type=jnp.float32).astype(jnp.bfloat16)
        def put(ts):
            s.W[ph, p.xh, p.par, p.z, p.xl, p.h, 3 * p.c + ts] = res[ts * 16:(ts + 1) * 16]
        put(0); put(1)
        pl.when(p.c == 0)(lambda: put(2))
    def order(s, ph, ts):
        a = (ph + ts) % 3
        return ((a + 1) % 3, (a + 2) % 3, a)
    def region(s, ph, t, full, over=None):
        p = s.p; o = over or {}
        x = o.get(0); y = o.get(1); z = o.get(2)
        xh, xl = (p.xh, p.xl) if x is None else (x // 2, x % 2)
        h, par = (p.h, p.par) if y is None else (y // 2, y % 2)
        zz = p.z if z is None else z
        if 0 in full: xh = xl = slice(None)
        if 1 in full: h = par = slice(None)
        if 2 in full: zz = slice(None)
        return [ph, xh, par, zz, xl, h, t]
    def ref(s, reg): return s.W.at[tuple(reg)]
    def cp(s, reg, ph, ts, kind, k, dev):
        r = s.ref(reg)
        return pltpu.make_async_remote_copy(r, r, s.ssem.at[kind + (4 if ts == 2 else 0)], s.rsem.at[ph * 3 + ts, k], device_id=dev, device_id_type=MESH)
    def half(s, reg, full, hf):
        reg = list(reg)
        i = 3 if 2 in full else (1 if 0 in full else 2)
        reg[i] = pl.ds(hf * 2, 2) if i == 3 else pl.ds(hf, 1)
        return reg
    def t(s, ts): return 3 * s.p.c + ts
    def direct(s, stage, ph, ts):
        a = s.order(ph, ts); full = a[:stage]; ax = a[stage]
        for d in (1, 3, 2):
            s.cp(s.region(ph, s.t(ts), full), ph, ts, stage, stage, s.p.ring(ax, d)).start()
    def got(s, ph, ts, k):
        r = s.W.at[ph]
        ref = (lambda: r.at[0, 0, 0:3, 0, 0, 0], lambda: r.at[0, 0, 0:3, :, :, 0], lambda: r.at[0, 0, :, :, :, 0],
               lambda: r.at[0, 0, :, :, :, 0], lambda: r.at[0, 0, :, :, :, 0], lambda: r.at[:, :, :, :, :, 0])[k]()
        wait(ref, s.rsem.at[ph * 3 + ts, k])
    def s3(s, ph, ts, what):
        a = s.order(ph, ts); full = a[:2]; ax = a[2]; tt = s.t(ts)
        R, L = s.p.ring(ax, 1), s.p.ring(ax, 3)
        reg = lambda d: s.region(ph, tt, full, {ax: s.p.coord(ax, d)})
        if what == 'own':
            s.cp(reg(0), ph, ts, 2, 2, R).start()
            s.cp(reg(0), ph, ts, 2, 3, L).start()
        elif what == 'fwdR': s.cp(s.half(reg(-1), full, 0), ph, ts, 2, 4, R).start()
        else: s.cp(s.half(reg(1), full, 1), ph, ts, 2, 4, L).start()
    def sib(s, ph, ts, piece):
        a = s.order(ph, ts); full = a[:2]; ax = a[2]
        d = (0, -1, 1, 2)[piece]
        s.cp(s.region(ph, s.t(ts), full, {ax: s.p.coord(ax, d)}), ph, ts, 3, 5, s.p.dev(c=1 - s.p.c)).start()
    def go(s, ts, f, other=False):
        def h():
            f()
        if ts < 2: h()
        else: pl.when(s.p.c == (1 if other else 0))(h)
    def each(s, f, other=False):
        for ts in range(3): s.go(ts, lambda ts=ts: f(ts), other)
    def phase_a(s, ph):
        s.each(lambda ts: s.direct(0, ph, ts))
    def phase_b(s, ph):
        s.each(lambda ts: (s.got(ph, ts, 0), s.direct(1, ph, ts)))
    def phase_c(s, ph):
        s.each(lambda ts: (s.got(ph, ts, 1), s.s3(ph, ts, 'own'), s.sib(ph, ts, 0)))
    def phase_d(s, ph):
        s.each(lambda ts: (s.got(ph, ts, 2), s.s3(ph, ts, 'fwdR'), s.sib(ph, ts, 1), s.got(ph, ts, 3), s.s3(ph, ts, 'fwdL'), s.sib(ph, ts, 2)))
    def phase_e(s, ph):
        s.each(lambda ts: (s.got(ph, ts, 4), s.sib(ph, ts, 3)))
    def phase_f(s, ph):
        s.each(lambda ts: s.got(ph, ts, 5), other=True)
    def drain(s):
        W = s.W
        for ts, t in ((0, slice(0, 2)), (2, 0)):
            def w(ts=ts, t=t):
                k = 4 if ts == 2 else 0
                wait(W.at[:, 0, 0, 0:3, 0, 0, t], s.ssem.at[k])
                wait(W.at[:, 0, 0, 0:3, :, :, t], s.ssem.at[k + 1])
                wait(W.at[:, :, :, 0:3, :, :, t], s.ssem.at[k + 2])
                wait(W.at[:, :, :, :, :, :, t], s.ssem.at[k + 3])
            if ts == 0: w()
            else: pl.when(s.p.c == 0)(w)
        o = s.s0_src()
        for tc in (0, 1):
            cond = (o <= 4) if tc == 0 else (o >= 4)
            pl.when(cond)(lambda tc=tc: wait(s.pieces.at[:, 0:3], s.s0s.at[tc]))
            pl.when(jnp.logical_and(cond, s.p.c != tc))(lambda: wait(s.pieces.at[:, 0], s.s0s.at[2]))

def barrier(partners):
    b = pltpu.get_barrier_semaphore()
    for d in partners:
        pl.semaphore_signal(b, inc=1, device_id=d, device_id_type=MESH)
    pl.semaphore_wait(b, len(partners))

def fill_pieces(pieces, wqkv, wout, wup, wdown):
    mats = [(wqkv, 0), (wqkv, 1280), (wqkv, 2560), (wout, 0), (wup, 0), (wdown, 0)]
    for ph in range(3):
        for xh in range(2):
            r, off = mats[2 * ph + xh]
            for par in range(2):
                v = r[:, off + par * 640: off + (par + 1) * 640]
                pieces[ph, 2 * xh + par] = jnp.concatenate([v.astype(jnp.float32), jnp.zeros((6, 640), jnp.float32)], axis=0).astype(jnp.bfloat16)


def dot(a, b):
    return jnp.dot(a, b, preferred_element_type=F32)


def dot_nt(a, b):
    return lax.dot_general(a, b, (((1,), (1,)), ((), ())), preferred_element_type=F32)


def dot_tn(a, b):
    return lax.dot_general(a, b, (((0,), (0,)), ((), ())), preferred_element_type=F32)


class Small:
    def __init__(s, p, buf, recv, ssem, rsem, rings):
        s.p, s.buf, s.recv, s.ssem, s.rsem, s.rings = p, buf, recv, ssem, rsem, rings

    def cps(s, k):
        p = s.p
        n = len(s.rings)
        sems = (s.ssem.at[k], s.rsem.at[k])
        if k == 0 or k == n + 1:
            src = s.buf.at[1 - p.c] if k == 0 else s.buf.at[p.c]
            return [pltpu.make_async_remote_copy(src, s.recv.at[0, 0 if k == 0 else 1], *sems, device_id=p.dev(c=1 - p.c), device_id_type=MESH)]
        return [pltpu.make_async_remote_copy(s.buf.at[p.c], s.recv.at[k, i], *sems, device_id=dv, device_id_type=MESH)
                for i, dv in enumerate(s.rings[k - 1])]

    def start(s, k):
        for c in s.cps(k): c.start()

    def finish(s, k):
        p = s.p
        n = len(s.rings)
        m = 1 if k in (0, n + 1) else len(s.rings[k - 1])
        both = s.recv.at[0 if k == n + 1 else k, 0:m]
        wait(both, s.rsem.at[k])
        wait(both, s.ssem.at[k])
        if k == n + 1:
            s.buf[1 - p.c] = s.recv[0, 1]
            return
        acc = s.buf[p.c].astype(F32)
        for i in range(m):
            acc = acc + s.recv[k, i].astype(F32)
        s.buf[p.c] = acc.astype(s.buf.dtype)


class RS:
    def __init__(s, p, G, GW, RD, bufs, FR, EX, FIN, dss, drs, ss, rs, fs, fr):
        s.p, s.G, s.GW, s.RD, s.bufs, s.FR, s.EX, s.FIN = p, G, GW, RD, bufs, FR, EX, FIN
        s.dss, s.drs, s.ss, s.rs, s.fs, s.fr = dss, drs, ss, rs, fs, fr

    def gref(s, ph):
        return s.G[ph]

    def go(s, ts, f, other=False):
        def h():
            f()
        if ts < 2: h()
        else: pl.when(s.p.c == (1 if other else 0))(h)

    def d2d(s, ph, ts, act, par):
        p = s.p
        g = s.gref(ph)
        t = 3 * (1 - p.c) + ts if act != 'recv' else 3 * p.c + ts
        cp = pltpu.make_async_remote_copy(g.at[par, :, :, :, t], s.RD.at[ph, ts, par], s.dss.at[ts // 2], s.drs.at[ph * 3 + ts, par], device_id=p.dev(c=1 - p.c), device_id_type=MESH)
        if act == 'start': cp.start()
        else: cp.wait_recv()

    def d2d_start(s, ph, par):
        for ts in range(3): s.go(ts, lambda ts=ts: s.d2d(ph, ts, 'start', par), other=True)

    def d2d_add(s, ph, ts, par):
        g = s.gref(ph)
        t = 3 * s.p.c + ts
        s.d2d(ph, ts, 'recv', par)
        def body(z, _):
            g[par, z, :, :, t] = (g[par, z, :, :, t].astype(F32) + s.RD[ph, ts, par, z].astype(F32)).astype(BF)
            return 0
        lax.fori_loop(0, 4, body, 0)

    def order(s, ph, ts):
        return ((1, 0, 2), (2, 0, 1), (0, 1, 2))[ts]

    def fidx(s, ph, ts):
        return (1, 2, 0)[ts]

    def piece(s, ph, ts, st, k):
        p = s.p
        o = s.order(ph, ts)
        ax = o[st]
        done = o[:st]
        par = h = zz = xl = slice(None)
        if 0 in done: xl = p.xl
        if 1 in done: h, par = p.h, p.par
        if 2 in done: zz = p.z
        if ax == 0: xl = k
        if ax == 1: h, par = k // 2, k % 2
        if ax == 2: zz = k
        return s.gref(ph).at[par, zz, xl, h, 3 * p.c + ts]

    def half(s, ph, ts, st, k, hf):
        p = s.p
        o = s.order(ph, ts)
        ax = o[st]
        assert st == 0
        t = 3 * p.c + ts
        if ax == 1: return s.gref(ph).at[k % 2, pl.ds(2 * hf, 2), :, k // 2, t]
        return s.gref(ph).at[hf, k, :, :, t]

    def bhalf(s, ph, ts, hf):
        f = s.fidx(ph, ts)
        b = s.bufs[f][0]
        if f == 1: return b.at[ph, 2, pl.ds(2 * hf, 2)]
        return b.at[ph, 2, hf]

    def cp(s, src, dst, sk, sl, k, dev):
        return pltpu.make_async_remote_copy(src, dst, s.ss.at[sk], s.rs.at[sl, k], device_id=dev, device_id_type=MESH)

    def add(s, dst, srcs):
        lead = dst.shape[:-2]
        if len(lead) >= 1 and lead[0] > 1:
            def body(i, _):
                acc = dst[i].astype(F32)
                for r in srcs: acc = acc + r[i].astype(F32)
                dst[i] = acc.astype(BF)
                return 0
            lax.fori_loop(0, lead[0], body, 0)
        else:
            acc = dst[...].astype(F32)
            for r in srcs: acc = acc + r[...].astype(F32)
            dst[...] = acc.astype(BF)

    def ring_cps(s, ph, ts, st):
        p = s.p
        o = s.order(ph, ts)
        ax = o[st]
        f = s.fidx(ph, ts)
        sl = ph * 3 + ts
        b = s.bufs[f][st]
        sk = st + (3 if ts == 2 else 0)
        if ax == 0:
            k = 1 - p.xl
            src, dv = s.piece(ph, ts, st, k), p.dev(x=p.xh * 2 + k)
            if st == 0: return [s.cp(src.at[par], b.at[ph, 0, par], sk, sl, par, dv) for par in range(2)]
            return [s.cp(src, b.at[ph, 0], sk, sl, 2 + st, dv)]
        res = []
        for i, d in enumerate((1, 3, 2)):
            res.append(s.cp(s.piece(ph, ts, st, p.coord(ax, d)), b.at[ph, i], sk, sl, 2 + st, p.ring(ax, d)))
        return res

    def first_a(s, ph, ts, par):
        ax = s.order(ph, ts)[0]
        if ax == 0:
            s.ring_cps(ph, ts, 0)[par].start()
        elif ax == 2:
            s.sf_half(ph, ts)[1 - par].start()
        else:
            @pl.when(s.p.par == par)
            def _():
                for c in s.sf_half(ph, ts): c.start()

    def sf_half(s, ph, ts):
        p = s.p
        ax = s.order(ph, ts)[0]
        sl = ph * 3 + ts
        k = p.coord(ax, 2)
        return [s.cp(s.half(ph, ts, 0, k, 1), s.bhalf(ph, ts, 1), 0, sl, 0, p.ring(ax, 1)),
                s.cp(s.half(ph, ts, 0, k, 0), s.bhalf(ph, ts, 0), 0, sl, 1, p.ring(ax, 3))]

    def sf_full(s, ph, ts):
        p = s.p
        ax = s.order(ph, ts)[0]
        sl = ph * 3 + ts
        b = s.bufs[s.fidx(ph, ts)][0]
        return [s.cp(s.piece(ph, ts, 0, p.coord(ax, 1)), b.at[ph, 0], 0, sl, 2, p.ring(ax, 1)),
                s.cp(s.piece(ph, ts, 0, p.coord(ax, 3)), b.at[ph, 1], 0, sl, 2, p.ring(ax, 3))]

    def first_b(s, ph, ts):
        p = s.p
        o = s.order(ph, ts)
        ax = o[0]
        if ax == 0: return
        hb = s.sf_half(ph, ts)
        full = s.sf_full(ph, ts)
        hb[0].wait_recv()
        s.add(s.half(ph, ts, 0, p.coord(ax, 1), 1), [s.bhalf(ph, ts, 1)])
        full[0].start()
        hb[1].wait_recv()
        s.add(s.half(ph, ts, 0, p.coord(ax, 3), 0), [s.bhalf(ph, ts, 0)])
        full[1].start()

    def first_c(s, ph, ts):
        p = s.p
        o = s.order(ph, ts)
        ax = o[0]
        me = (p.xl, p.y, p.z)[ax]
        b = s.bufs[s.fidx(ph, ts)][0]
        if ax == 0:
            for par, c in enumerate(s.ring_cps(ph, ts, 0)):
                c.wait_recv()
                s.add(s.piece(ph, ts, 0, me).at[par], [b.at[ph, 0, par]])
            return
        wait(b.at[ph, 0:2], s.rs.at[ph * 3 + ts, 2])
        s.add(s.piece(ph, ts, 0, me), [b.at[ph, i] for i in range(2)])

    def next_start(s, ph, ts, st):
        for c in s.ring_cps(ph, ts, st): c.start()

    def next_finish(s, ph, ts, st):
        p = s.p
        ax = s.order(ph, ts)[st]
        me = (p.xl, p.y, p.z)[ax]
        b = s.bufs[s.fidx(ph, ts)][st]
        wait(b.at[ph], s.rs.at[ph * 3 + ts, 2 + st])
        s.add(s.piece(ph, ts, st, me), [b.at[ph, i] for i in range(1 if ax == 0 else 3)])

    def each(s, f):
        for ts in range(3): s.go(ts, lambda ts=ts: f(ts))

    def first(s, ph, par):
        s.each(lambda ts: (s.d2d_add(ph, ts, par), s.first_a(ph, ts, par)))

    def step(s, ph, k):
        if k == 2: s.each(lambda ts: s.first_b(ph, ts))
        elif k == 3: s.each(lambda ts: (s.first_c(ph, ts), s.next_start(ph, ts, 1)))
        elif k == 4: s.each(lambda ts: (s.next_finish(ph, ts, 1), s.next_start(ph, ts, 2)))
        elif k == 5:
            s.each(lambda ts: s.next_finish(ph, ts, 2))
            s.final_start(ph)

    def fin_cps(s, ph, k):
        p = s.p
        o = 4 * p.c + k
        chunk = 2 * p.xh + p.par
        dev = p.dev(x=(o % 2) * 2 + p.xl, y=2 * p.h + o // 4, c=(o // 2) % 2)
        return pltpu.make_async_remote_copy(s.EX.at[ph, k], s.FIN.at[ph, chunk, p.c], s.fs.at[0], s.fr.at[ph, p.c], device_id=dev, device_id_type=MESH)

    def myo(s):
        p = s.p
        return (p.par * 2 + p.c) * 2 + p.xh

    def final_start(s, ph):
        p = s.p
        g = s.gref(ph)
        def put(ts):
            s.FR[ts] = g[p.par, p.z, p.xl, p.h, 3 * p.c + ts]
        put(0); put(1)
        pl.when(p.c == 0)(lambda: put(2))
        i = lax.broadcasted_iota(jnp.int32, (80, 48), 1)
        k = lax.broadcasted_iota(jnp.int32, (80, 48), 0)
        r = 48 * p.c + i
        q = (r * 205) >> 11
        col = (q - 4 * p.c) * 16 + (r - q * 10)
        pt = jnp.where(k == col, 1.0, 0.0).astype(BF)
        s.EX[ph] = dot(pt, s.FR[...].reshape(48, CW)).astype(BF).reshape(5, 16, CW)
        for k in range(5):
            def send(k=k):
                me = 4 * p.c + k == s.myo()
                @pl.when(me)
                def _():
                    s.FIN[ph, 2 * p.xh + p.par, p.c] = s.EX[ph, k]
                @pl.when(jnp.logical_not(me))
                def _():
                    s.fin_cps(ph, k).start()
            if k < 4: send()
            else: pl.when(p.c == 0)(send)

    def final_wait(s, ph):
        p = s.p
        o = s.myo()
        for sc in range(2):
            used = (o <= 4) if sc == 0 else (o >= 4)
            pl.when(jnp.logical_and(used, p.c == sc))(lambda: wait(s.FIN.at[ph, 0:3, 0], s.fr.at[ph, sc]))
            pl.when(jnp.logical_and(used, p.c != sc))(lambda: wait(s.FIN.at[ph, :, 0], s.fr.at[ph, sc]))

    def drain(s):
        p = s.p
        G = s.GW
        wait(G.at[:, :, :, :, :, 0:2], s.dss.at[0])
        pl.when(p.c == 1)(lambda: wait(G.at[:, :, :, :, :, 0], s.dss.at[1]))
        wait(G.at[:, :, 0:3, :, :, 0:2], s.ss.at[0])
        wait(G.at[:, 0, :, 0, 0, 0:2], s.ss.at[1])
        wait(G.at[:, 0, 0:3, 0, 0, 0:2], s.ss.at[2])
        @pl.when(p.c == 0)
        def _():
            wait(G.at[:, :, :, :, 0, 0], s.ss.at[3])
            wait(G.at[:, 0, 0:3, :, :, 0], s.ss.at[4])
            wait(G.at[:, 0, 0:3, 0, 0, 0], s.ss.at[5])
        o = s.myo()
        n = jnp.where(p.c == 0, jnp.where(o <= 4, 4, 5), jnp.where(o >= 4, 3, 4))
        for k in (3, 4, 5):
            pl.when(n == k)(lambda k=k: wait(s.EX.at[:, 0:k], s.fs.at[0]))


def clear_last(stg, FR):
    stg[:, 4] = jnp.zeros((3, 16, CW), BF)
    FR[2] = jnp.zeros((16, CW), BF)


FIRST, Q, K, V, MIXED, SECOND, ACTIVE, GU, GAO, GMX, GQ, GK, GV = range(13)
RB = 32


def block_kernel(lat_in, cot_in, sid, *refs):
    small_in, (o_lat, o_in), small_out = refs[0:8], refs[8:10], refs[10:16]
    block_body(lat_in, cot_in, sid, small_in, o_lat, o_in, small_out, *refs[16:])


def block_body(lat_in, cot_in, sid, small_in, o_lat, o_in, small_out,
                 W, stg, pieces, A, N1, N2, MID, DG, PR, I1, I2, VEC, CS, GW, RD, b00, b01, b02, b10, b11, b12, b20, b21, b22,
                 FR, EX, FIN, SB, SBR, SG, SGR,
                 lat, cot, gt, b1, g2, b2, wq, wo, wu, wd, o_tab, o_vec, o_qkv, o_out, o_up, o_down, ssem, rsem, s0s, s0r, dss, drs, gss, grs, fs, fr, sbs, sbr, sgs, sgr, io):
    p = Pos()
    ag = AG(p, W, stg, pieces, ssem, rsem, None, s0s, s0r)
    G = [GW.at[0], GW.at[1], GW.at[2]]
    rs = RS(p, G, GW, RD, [[b00, b01, b02], [b10, b11, b12], [b20, b21, b22]], FR, EX, FIN, dss, drs, gss, grs, fs, fr)
    ring3 = lambda ax: [p.ring(ax, d) for d in (1, 3, 2)]
    sb = Small(p, SB, SBR, sbs, sbr, [ring3(0), ring3(1), ring3(2)])
    sg = Small(p, SG, SGR, sgs, sgr, [ring3(1), ring3(2), [p.dev(x=p.xh * 2 + 1 - p.xl)]])
    idx = lax.axis_index("dp") * 2 + p.xh

    parts = ag.partners()
    bar = pltpu.get_barrier_semaphore()
    for d in parts:
        pl.semaphore_signal(bar, inc=1, device_id=d, device_id_type=MESH)
    in_lat = pltpu.make_async_copy(lat_in, lat, io.at[0])
    in_cot = pltpu.make_async_copy(cot_in, cot, io.at[1])
    ins = [pltpu.make_async_copy(a, v, io.at[4 + i]) for i, (a, v) in enumerate(zip(small_in, (gt, b1, g2, b2, wq, wo, wu, wd)))]
    for c in ins: c.start()
    in_lat.start(); in_cot.start()
    for c in ins: c.wait()
    fill_pieces(pieces, wq, wo, wu, wd)
    pl.when(p.c == 1)(lambda: clear_last(stg, FR))
    j = lax.broadcasted_iota(jnp.int32, (16, D), 0)
    lane = lax.broadcasted_iota(jnp.int32, (16, D), 1)
    own = jnp.where(jnp.logical_and(lane == idx * 10 + j, j < 10), 1.0, 0.0)
    own16 = own[0:10].astype(BF)
    spread = [dot_tn(gt[...], own16)] + [dot(jnp.broadcast_to(b[...].reshape(1, 10), (8, 10)), own16)[0:1] for b in (b1, g2, b2)] + [jnp.zeros((13, D), F32)]
    spread = jnp.concatenate(spread, axis=0).astype(BF)
    for k in range(2): SB[k] = spread[:, k * 640:(k + 1) * 640]
    pl.semaphore_wait(bar, len(parts))

    sb.start(0)
    for ph in range(3): ag.s0(ph)

    def ln1(r, _):
        rows = pl.ds(pl.multiple_of(r * RB, RB), RB)
        x = lat[rows, :].astype(F32)
        mu = jnp.mean(x, axis=-1, keepdims=True)
        xc = x - mu
        inv = lax.rsqrt(jnp.mean(xc * xc, axis=-1, keepdims=True) + EPS)
        N1[rows, :] = xc * inv
        I1[rows, :] = jnp.broadcast_to(inv, (RB, 128))
        return 0
    in_lat.wait(); in_cot.wait()
    lax.fori_loop(0, L // RB, ln1, 0)
    ag.s0_recv(0); ag.compact(0); ag.phase_a(0)
    sb.finish(0); sb.start(1)
    ag.s0_recv(1); ag.compact(1); ag.phase_a(1)
    ag.phase_b(0)
    sb.finish(1); sb.start(2)
    ag.s0_recv(2); ag.compact(2); ag.phase_a(2)
    ag.phase_b(1)
    ag.phase_c(0)
    sb.finish(2); sb.start(3)
    ag.phase_b(2)
    ag.phase_c(1)
    sb.finish(3); sb.start(4)
    A[MIXED] = jnp.zeros((L, D), BF)
    for k in (GQ, GK, GV): A[k] = jnp.zeros((L, D), BF)
    CS[...] = jnp.zeros_like(CS)
    ag.phase_d(0)
    ag.phase_c(2)
    sb.finish(4)
    lane32 = lax.broadcasted_iota(jnp.int32, (8, 32), 1)
    sub8 = lax.broadcasted_iota(jnp.int32, (8, 32), 0)
    tgt = jnp.where(sub8 == 0, sid[0], jnp.where(sub8 < 4, 15 + sub8, -1))
    pick = jnp.where(lane32 == tgt, 1.0, 0.0).astype(BF)
    for k in range(2): VEC[:, k * 640:(k + 1) * 640] = dot(pick, SB[k])

    def mk_first(r, _):
        rows = pl.ds(pl.multiple_of(r * RB, RB), RB)
        A[FIRST, rows, :] = (N1[rows, :] * VEC[0:1, :] + VEC[1:2, :]).astype(BF)
        return 0
    lax.fori_loop(0, L // RB, mk_first, 0)
    ag.phase_d(1)
    ag.phase_e(0)
    ag.phase_f(0)

    def wpan(ph, xh, par): return W[ph, xh, par].reshape(D, CW)
    def cols(par): return pl.ds(par * CW, CW)

    for par in range(2):
        A[Q, :, cols(par)] = dot(A[FIRST], wpan(0, 0, par)).astype(BF)
    ag.phase_d(2)
    for par in range(2):
        A[K, :, cols(par)] = dot(A[FIRST], wpan(0, 1, par)).astype(BF)
    ag.phase_e(1)
    ag.phase_f(1)
    for par in range(2):
        A[V, :, cols(par)] = dot(A[FIRST], wpan(1, 0, par)).astype(BF)

    lane256 = lax.broadcasted_iota(jnp.int32, (1, 256), 1)
    def masks(w):
        m = jnp.where(jnp.logical_and(lane256 >= 32 * w, lane256 < 32 * w + HD), 1.0, 0.0)
        return m, m.astype(BF)
    def win(pn, w):
        return pl.ds(pl.multiple_of(pn * CW + w * 128, 128), 256)

    for pn in range(2):
        def att(w, _, pn=pn):
            cw = win(pn, w)
            m32, m16 = masks(w)
            sc = dot_nt(A[Q, :, cw] * m16, A[K, :, cw]) * SCALE
            e = jnp.exp(sc - jnp.max(sc, axis=-1, keepdims=True))
            pr = e * (1.0 / jnp.sum(e, axis=-1, keepdims=True))
            PR[pn * 4 + w] = pr
            mx = dot(pr.astype(BF), A[V, :, cw]) * m32
            A[MIXED, :, cw] = A[MIXED, :, cw] + mx.astype(BF)
            return 0
        lax.fori_loop(0, 4, att, 0, unroll=True)
    ag.phase_e(2)
    for par in range(2):
        MID[:, cols(par)] = lat[:, cols(par)].astype(F32) + dot(A[MIXED], wpan(1, 1, par))

    def ln2(r, _):
        rows = pl.ds(pl.multiple_of(r * RB, RB), RB)
        x = MID[rows, :]
        mu = jnp.mean(x, axis=-1, keepdims=True)
        xc = x - mu
        inv = lax.rsqrt(jnp.mean(xc * xc, axis=-1, keepdims=True) + EPS)
        n = xc * inv
        N2[rows, :] = n
        I2[rows, :] = jnp.broadcast_to(inv, (RB, 128))
        A[SECOND, rows, :] = (n * VEC[2:3, :] + VEC[3:4, :]).astype(BF)
        return 0
    lax.fori_loop(0, L // RB, ln2, 0)
    ag.phase_f(2)
    for par in range(2):
        DG[:, cols(par)] = dot(A[SECOND], wpan(2, 0, par))

    def gelu(r, _):
        rows = pl.ds(pl.multiple_of(r * RB, RB), RB)
        u = DG[rows, :]
        c0 = math.sqrt(2.0 / math.pi)
        u2 = u * u
        th = jnp.tanh(c0 * (u + 0.044715 * u2 * u))
        hp = 0.5 * (1.0 + th)
        A[ACTIVE, rows, :] = (u * hp).astype(BF)
        DG[rows, :] = hp + 0.5 * u * (1.0 - th * th) * (c0 * (1.0 + 3 * 0.044715 * u2))
        return 0
    lax.fori_loop(0, L // RB, gelu, 0)

    def back(src, ph, xh, n):
        acc = None
        for par in range(2):
            t = dot_nt(src(par), W[ph, xh, par, 2 * n:2 * n + 2].reshape(CW, CW))
            acc = t if acc is None else acc + t
        return acc

    half = pl.ds(pl.multiple_of(p.xh * CW, 128), CW)

    def wgrad(ph, par, left, right):
        for n in range(2):
            v = dot_tn(A[left, :, cols(n)], right[:, half])
            G[ph][par, 2 * n:2 * n + 2] = v.astype(BF).reshape(2, 2, 2, 5, 16, CW)
        rs.d2d_start(ph, par)

    wgrad(2, 1, ACTIVE, cot)
    for n in range(2):
        A[GU, :, cols(n)] = (back(lambda par: cot[:, cols(par)], 2, 1, n) * DG[:, cols(n)]).astype(BF)
    wgrad(2, 0, SECOND, A.at[GU])
    for n in range(2):
        DG[:, cols(n)] = back(lambda par: A[GU, :, cols(par)], 2, 0, n)
        rs.first(2, 1 - n)

    def ln2b(r, _):
        rows = pl.ds(pl.multiple_of(r * RB, RB), RB)
        gs = DG[rows, :]
        n = N2[rows, :]
        CS[1] += jnp.sum((gs * n).reshape(RB // 8, 8, D), axis=0)
        CS[2] += jnp.sum(gs.reshape(RB // 8, 8, D), axis=0)
        dn = gs * VEC[2:3, :]
        m1 = jnp.mean(dn, axis=-1, keepdims=True)
        m2 = jnp.mean(dn * n, axis=-1, keepdims=True)
        gm = cot[rows, :].astype(F32) + I2[rows, 0:1] * (dn - m1 - n * m2)
        N2[rows, :] = gm
        A[GAO, rows, :] = gm.astype(BF)
        return 0
    lax.fori_loop(0, L // RB, ln2b, 0)
    wgrad(1, 1, MIXED, A.at[GAO])
    for n in range(2):
        A[GMX, :, cols(n)] = back(lambda par: A[GAO, :, cols(par)], 1, 1, n).astype(BF)
    rs.step(2, 2)
    rs.first(1, 1)

    for i in range(2):
        pn = p.xh if i == 0 else 1 - p.xh
        def attb(w, _, pn=pn):
            cw = win(pn, w)
            m32, m16 = masks(w)
            gm = A[GMX, :, cw] * m16
            qm = A[Q, :, cw] * m16
            pr = PR[pn * 4 + w]
            gp = dot_nt(gm, A[V, :, cw])
            rt = jnp.sum(gp * pr, axis=-1, keepdims=True)
            gsc = (pr * (gp - rt)).astype(BF)
            A[GV, :, cw] = A[GV, :, cw] + dot_tn(pr.astype(BF), gm).astype(BF)
            A[GQ, :, cw] = A[GQ, :, cw] + (dot(gsc, A[K, :, cw]) * SCALE * m32).astype(BF)
            A[GK, :, cw] = A[GK, :, cw] + (dot_tn(gsc, qm) * SCALE).astype(BF)
            return 0
        lax.fori_loop(0, 4, attb, 0, unroll=True)
        if i == 0:
            wgrad(1, 0, FIRST, A.at[GV])
            wgrad(0, 0, FIRST, A.at[GQ])
            wgrad(0, 1, FIRST, A.at[GK])
            rs.step(2, 3)
            rs.first(1, 0)
            rs.first(0, 0)
            rs.first(0, 1)
    rs.step(1, 2)
    for n in range(2):
        acc = None
        for g, (ph, xh) in ((GQ, (0, 0)), (GK, (0, 1)), (GV, (1, 0))):
            t = back(lambda par: A[g, :, cols(par)], ph, xh, n)
            acc = t if acc is None else acc + t
        DG[:, cols(n)] = acc
        if n == 0: rs.step(2, 4)
    rs.step(0, 2)

    def ln1b(r, _):
        rows = pl.ds(pl.multiple_of(r * RB, RB), RB)
        gf = DG[rows, :]
        n = N1[rows, :]
        CS[3] += jnp.sum((gf * n).reshape(RB // 8, 8, D), axis=0)
        CS[0] += jnp.sum(gf.reshape(RB // 8, 8, D), axis=0)
        dn = gf * VEC[0:1, :]
        m1 = jnp.mean(dn, axis=-1, keepdims=True)
        m2 = jnp.mean(dn * n, axis=-1, keepdims=True)
        DG[rows, :] = N2[rows, :] + I1[rows, 0:1] * (dn - m1 - n * m2)
        return 0
    lax.fori_loop(0, L // RB, ln1b, 0)
    out_in = pltpu.make_async_copy(DG, o_in, io.at[3])
    out_in.start()
    sub24 = lax.broadcasted_iota(jnp.int32, (24, 640), 0)
    for k in range(2):
        v = [jnp.sum(CS[i, :, k * 640:(k + 1) * 640], axis=0, keepdims=True) for i in range(4)]
        SG[k] = (jnp.where(sub24 == sid[0], v[3], 0.0) + jnp.where(sub24 == 16, v[0], 0.0)
                 + jnp.where(sub24 == 17, v[1], 0.0) + jnp.where(sub24 == 18, v[2], 0.0))
    sg.start(0)
    rs.step(1, 3)
    rs.step(2, 5)
    for par in range(2):
        A[SECOND, :, cols(par)] = (MID[:, cols(par)] + dot(A[ACTIVE], wpan(2, 1, par))).astype(BF)
    out_lat = pltpu.make_async_copy(A.at[SECOND], o_lat, io.at[2])
    out_lat.start()
    sg.finish(0); sg.start(1)
    ag.drain()
    rs.step(0, 3)
    rs.step(1, 4)
    sg.finish(1); sg.start(2)
    rs.step(0, 4)
    rs.step(1, 5)
    sg.finish(2); sg.start(3)
    rs.step(0, 5)

    outs = [(o_qkv, 0), (o_qkv, 1280), (o_qkv, 2560), (o_out, 0), (o_up, 0), (o_down, 0)]
    def emit(ph):
        rs.final_wait(ph)
        o_id = rs.myo()
        sel = jnp.where(o_id > 4, 1, 0)
        @pl.when(o_id == 4)
        def _():
            FIN[ph, :, 0] = FIN[ph, :, 0] + FIN[ph, :, 1]
        for xh in range(2):
            for par in range(2):
                o, off = outs[2 * ph + par]
                v = FIN[ph, 2 * xh + par, sel].astype(F32)
                o[:, off + xh * 640: off + (xh + 1) * 640] = v[0:10]
    emit(2)
    sg.finish(3); sg.start(4)
    emit(1)
    sg.finish(4)
    tab = None
    for k in range(2):
        ok = own[:, k * 640:(k + 1) * 640]
        t = lax.dot_general(ok, SG[k], (((1,), (1,)), ((), ())), precision=lax.Precision.HIGHEST, preferred_element_type=F32)
        u = lax.dot_general(SG[k, 16:24], ok, (((1,), (1,)), ((), ())), precision=lax.Precision.HIGHEST, preferred_element_type=F32)
        tab, vec = (t, u) if tab is None else (tab + t, vec + u)
    o_tab[...] = tab[0:10, 0:16]
    o_vec[...] = vec[:, 0:10]
    emit(0)
    outs = [pltpu.make_async_copy(v, o, io.at[4 + i]) for i, (v, o) in enumerate(zip((o_tab, o_vec, o_qkv, o_out, o_up, o_down), small_out))]
    for c in outs: c.start()
    rs.drain()
    out_lat.wait(); out_in.wait()
    for c in outs: c.wait()


def results_kernel(lat, inp, tab, vec, qkv, out, up, down, o_lat, o_in, o_tab, o_b1, o_g2, o_b2, o_qkv, o_out, o_up, o_down, sem):
    cps = [pltpu.make_async_copy(a, o, sem.at[i]) for i, (a, o) in enumerate(((lat, o_lat), (inp, o_in), (qkv, o_qkv), (out, o_out), (up, o_up), (down, o_down)))]
    for c in cps: c.start()
    o_tab[...] = tab[...]
    for i, o in enumerate((o_b1, o_g2, o_b2)): o[...] = vec[i]
    for c in cps: c.wait()


def per_device(latents, script_ids, gain_table, bias_one, w_qkv, w_out, gain_two, bias_two, w_up, w_down, cotangent):
    V_ = pltpu.VMEM
    dma = pltpu.SemaphoreType.DMA
    blk = (16, CW)
    scratch = [
        V_((3, 2, 2, 4, 2, 2, 5, 16, CW), BF), V_((3, 5) + blk, BF), V_((3, 4) + blk, BF),
        V_((13, L, D), BF), V_((L, D), F32), V_((L, D), F32), V_((L, D), F32), V_((L, D), F32),
        V_((8, 256, 256), F32), V_((L, 128), F32), V_((L, 128), F32), V_((8, D), F32), V_((4, 8, D), F32),
        V_((3, 2, 4, 2, 2, 5) + blk, BF), V_((3, 3, 2, 4, 2, 2) + blk, BF),
        V_((3, 1, 2, 4, 2) + blk, BF), V_((3, 3, 4) + blk, BF), V_((3, 3) + blk, BF),
        V_((3, 3, 4, 2) + blk, BF), V_((3, 1, 4) + blk, BF), V_((3, 3) + blk, BF),
        V_((3, 3, 2, 2, 2) + blk, BF), V_((3, 1, 2, 2) + blk, BF), V_((3, 3) + blk, BF),
        V_((3,) + blk, BF), V_((3, 5) + blk, BF), V_((3, 4, 2) + blk, BF),
        V_((2, 32, 640), BF), V_((4, 3, 32, 640), BF), V_((2, 24, 640), F32), V_((4, 3, 24, 640), F32), V_((L, D), BF), V_((L, D), BF),
        V_((10, 16), BF), V_((10,), BF), V_((10,), BF), V_((10,), BF), V_((10, 3 * D), BF), V_((10, D), BF), V_((10, D), BF), V_((10, D), BF),
        V_((10, 16), F32), V_((8, 10), F32), V_((10, 3 * D), F32), V_((10, D), F32), V_((10, D), F32), V_((10, D), F32),
        dma((8,)), dma((9, 6)), dma((3,)), dma((3,)),
        dma((2,)), dma((9, 2)), dma((6,)), dma((9, 5)), dma((1,)), dma((3, 2)),
        dma((5,)), dma((5,)), dma((5,)), dma((5,)), dma((12,)),
    ]
    vm = pl.BlockSpec(memory_space=pltpu.VMEM)
    sm = pl.BlockSpec(memory_space=pltpu.SMEM)
    hbm = pl.BlockSpec(memory_space=pl.ANY)
    f32 = lambda *d: jax.ShapeDtypeStruct(d, F32)
    res = pl.pallas_call(
        block_kernel,
        out_shape=[jax.ShapeDtypeStruct((L, D), BF), f32(L, D), f32(10, 16), f32(8, 10), f32(10, 3 * D), f32(10, D), f32(10, D), f32(10, D)],
        in_specs=[hbm, hbm, sm] + [hbm] * 8,
        out_specs=[hbm] * 8,
        scratch_shapes=scratch,
        compiler_params=pltpu.CompilerParams(collective_id=0, has_side_effects=True, vmem_limit_bytes=62 * 2**20),
        name="block",
    )(latents.reshape(L, D), cotangent.reshape(L, D), script_ids, gain_table, bias_one, gain_two, bias_two, w_qkv, w_out, w_up, w_down)
    o_lat, o_in, o_tab, o_b1, o_g2, o_b2, o_qkv, o_out, o_up, o_down = pl.pallas_call(
        results_kernel,
        out_shape=[jax.ShapeDtypeStruct((L, D), BF), f32(L, D), f32(10, 16), f32(10), f32(10), f32(10), f32(10, 3 * D), f32(10, D), f32(10, D), f32(10, D)],
        in_specs=[vm] * 8,
        out_specs=[hbm, hbm] + [vm] * 4 + [hbm] * 4,
        scratch_shapes=[dma((6,))],
        name="results",
    )(*res)
    return (o_lat.reshape(1, L, D), o_in.reshape(1, L, D), o_tab, o_b1, o_qkv, o_out, o_g2, o_b2, o_up, o_down)


def solution(mesh):
    row = P(("dp", "fsdp"), None)
    vec = P(("dp", "fsdp"))
    item = P("dp", None, None)
    return jax.shard_map(
        per_device,
        mesh=mesh,
        in_specs=(item, P("dp"), row, vec, row, row, vec, vec, row, row, item),
        out_specs=(item, item, row, vec, row, row, vec, vec, row, row),
        check_vma=False,
    )
```

```python
import math

import jax
import jax.numpy as jnp
from jax import lax
from jax.experimental import pallas as pl
from jax.experimental.pallas import tpu as pltpu
from jax.sharding import PartitionSpec as P

HEADS = 8
HD = 160
D = 1280
L = 256
EPS = 1e-5
SCALE = 1.0 / math.sqrt(HD)
BF = jnp.bfloat16
F32 = jnp.float32

MESH = pl.DeviceIdType.MESH
CW = 640

class Pos:
    def __init__(s):
        dp = lax.axis_index("dp"); s.xh = lax.axis_index("fsdp")
        s.c = dp % 2; s.y = (dp // 2) % 4; s.xl = (dp // 8) % 2; s.z = dp // 16
        s.x = s.xh * 2 + s.xl; s.h = s.y // 2; s.par = s.y % 2
    def dev(s, x=None, y=None, z=None, c=None):
        x = s.x if x is None else x; y = s.y if y is None else y
        z = s.z if z is None else z; c = s.c if c is None else c
        return (((z * 2 + x % 2) * 4 + y) * 2 + c, x // 2)
    def ring(s, ax, d):
        if ax == 0: return s.dev(x=(s.x + d) % 4)
        if ax == 1: return s.dev(y=(s.y + d) % 4)
        return s.dev(z=(s.z + d) % 4)
    def coord(s, ax, d):
        return ((s.x, s.y, s.z)[ax] + d) % 4

def wait(ref, sem):
    pltpu.make_async_copy(ref, ref, sem).wait()

class AG:
    def __init__(s, p, W, stg, pieces, ssem, rsem, sib_r, s0s, s0r):
        s.p, s.W, s.stg, s.pieces = p, W, stg, pieces
        s.ssem, s.rsem, s.s0s, s.s0r = ssem, rsem, s0s, s0r
    def partners(s):
        p = s.p
        out = []
        for ax in range(3):
            for d in (1, 2, 3): out.append(p.ring(ax, d))
        for dy in (0, 1):
            for dx in (0, 1):
                for dc in (0, 1):
                    if (dy, dx, dc) == (0, 0, 0): continue
                    if (dy, dx, dc) == (0, 1, 0): continue
                    y = p.y ^ dy if dy else p.y
                    x = (p.x + 2 * dx) % 4
                    out.append(p.dev(x=x, y=y, c=(p.c + dc) % 2))
        return out
    def s0_targets(s):
        p = s.p
        res = []
        for dy in (0, 1):
            for dx in (0, 1):
                y = p.y ^ dy if dy else p.y
                x = (p.x + 2 * dx) % 4
                res.append((dy, dx, y, x))
        return res
    def s0_src(s):
        p = s.p
        return (p.par * 2 + p.c) * 2 + p.xh
    def s0(s, ph):
        p = s.p; o = s.s0_src()
        for tc in (0, 1):
            cond = (o <= 4) if tc == 0 else (o >= 4)
            @pl.when(cond)
            def _(tc=tc):
                for dy, dx, y, x in s.s0_targets():
                    src = s.pieces.at[ph, (x // 2) * 2 + y % 2]
                    dst = s.stg.at[ph, o - 4 * tc]
                    def send(sem):
                        pltpu.make_async_remote_copy(src, dst, s.s0s.at[sem], s.s0r.at[ph], device_id=p.dev(y=y, x=x, c=tc), device_id_type=MESH).start()
                    if dy == 0 and dx == 0:
                        @pl.when(p.c == tc)
                        def _():
                            pltpu.make_async_copy(src, dst, s.s0r.at[ph]).start()
                        @pl.when(p.c != tc)
                        def _():
                            send(2)
                    else:
                        send(tc)
    def s0_recv(s, ph):
        pl.when(s.p.c == 0)(lambda: wait(s.stg.at[ph], s.s0r.at[ph]))
        pl.when(s.p.c == 1)(lambda: wait(s.stg.at[ph, 0:4], s.s0r.at[ph]))
    def compact(s, ph):
        p = s.p
        i = lax.broadcasted_iota(jnp.int32, (48, 80), 0)
        k = lax.broadcasted_iota(jnp.int32, (48, 80), 1)
        r = 48 * p.c + i
        q = (r * 205) >> 11
        col = (q - 4 * p.c) * 16 + (r - q * 10)
        P = jnp.where(k == col, 1.0, 0.0).astype(jnp.bfloat16)
        res = jnp.dot(P, s.stg[ph].reshape(80, CW), preferred_element_type=jnp.float32).astype(jnp.bfloat16)
        def put(ts):
            s.W[ph, p.xh, p.par, p.z, p.xl, p.h, 3 * p.c + ts] = res[ts * 16:(ts + 1) * 16]
        put(0); put(1)
        pl.when(p.c == 0)(lambda: put(2))
    def order(s, ph, ts):
        a = (ph + ts) % 3
        return ((a + 1) % 3, (a + 2) % 3, a)
    def region(s, ph, t, full, over=None):
        p = s.p; o = over or {}
        x = o.get(0); y = o.get(1); z = o.get(2)
        xh, xl = (p.xh, p.xl) if x is None else (x // 2, x % 2)
        h, par = (p.h, p.par) if y is None else (y // 2, y % 2)
        zz = p.z if z is None else z
        if 0 in full: xh = xl = slice(None)
        if 1 in full: h = par = slice(None)
        if 2 in full: zz = slice(None)
        return [ph, xh, par, zz, xl, h, t]
    def ref(s, reg): return s.W.at[tuple(reg)]
    def cp(s, reg, ph, ts, kind, k, dev):
        r = s.ref(reg)
        return pltpu.make_async_remote_copy(r, r, s.ssem.at[kind + (4 if ts == 2 else 0)], s.rsem.at[ph * 3 + ts, k], device_id=dev, device_id_type=MESH)
    def half(s, reg, full, hf):
        reg = list(reg)
        i = 3 if 2 in full else (1 if 0 in full else 2)
        reg[i] = pl.ds(hf * 2, 2) if i == 3 else pl.ds(hf, 1)
        return reg
    def t(s, ts): return 3 * s.p.c + ts
    def direct(s, stage, ph, ts):
        a = s.order(ph, ts); full = a[:stage]; ax = a[stage]
        for d in (1, 3, 2):
            s.cp(s.region(ph, s.t(ts), full), ph, ts, stage, stage, s.p.ring(ax, d)).start()
    def got(s, ph, ts, k):
        r = s.W.at[ph]
        ref = (lambda: r.at[0, 0, 0:3, 0, 0, 0], lambda: r.at[0, 0, 0:3, :, :, 0], lambda: r.at[0, 0, :, :, :, 0],
               lambda: r.at[0, 0, :, :, :, 0], lambda: r.at[0, 0, :, :, :, 0], lambda: r.at[:, :, :, :, :, 0])[k]()
        wait(ref, s.rsem.at[ph * 3 + ts, k])
    def s3(s, ph, ts, what):
        a = s.order(ph, ts); full = a[:2]; ax = a[2]; tt = s.t(ts)
        R, L = s.p.ring(ax, 1), s.p.ring(ax, 3)
        reg = lambda d: s.region(ph, tt, full, {ax: s.p.coord(ax, d)})
        if what == 'own':
            s.cp(reg(0), ph, ts, 2, 2, R).start()
            s.cp(reg(0), ph, ts, 2, 3, L).start()
        elif what == 'fwdR': s.cp(s.half(reg(-1), full, 0), ph, ts, 2, 4, R).start()
        else: s.cp(s.half(reg(1), full, 1), ph, ts, 2, 4, L).start()
    def sib(s, ph, ts, piece):
        a = s.order(ph, ts); full = a[:2]; ax = a[2]
        d = (0, -1, 1, 2)[piece]
        s.cp(s.region(ph, s.t(ts), full, {ax: s.p.coord(ax, d)}), ph, ts, 3, 5, s.p.dev(c=1 - s.p.c)).start()
    def go(s, ts, f, other=False):
        def h():
            f()
        if ts < 2: h()
        else: pl.when(s.p.c == (1 if other else 0))(h)
    def each(s, f, other=False):
        for ts in range(3): s.go(ts, lambda ts=ts: f(ts), other)
    def phase_a(s, ph):
        s.each(lambda ts: s.direct(0, ph, ts))
    def phase_b(s, ph):
        s.each(lambda ts: (s.got(ph, ts, 0), s.direct(1, ph, ts)))
    def phase_c(s, ph):
        s.each(lambda ts: (s.got(ph, ts, 1), s.s3(ph, ts, 'own'), s.sib(ph, ts, 0)))
    def phase_d(s, ph):
        s.each(lambda ts: (s.got(ph, ts, 2), s.s3(ph, ts, 'fwdR'), s.sib(ph, ts, 1), s.got(ph, ts, 3), s.s3(ph, ts, 'fwdL'), s.sib(ph, ts, 2)))
    def phase_e(s, ph):
        s.each(lambda ts: (s.got(ph, ts, 4), s.sib(ph, ts, 3)))
    def phase_f(s, ph):
        s.each(lambda ts: s.got(ph, ts, 5), other=True)
    def drain(s):
        W = s.W
        for ts, t in ((0, slice(0, 2)), (2, 0)):
            def w(ts=ts, t=t):
                k = 4 if ts == 2 else 0
                wait(W.at[:, 0, 0, 0:3, 0, 0, t], s.ssem.at[k])
                wait(W.at[:, 0, 0, 0:3, :, :, t], s.ssem.at[k + 1])
                wait(W.at[:, :, :, 0:3, :, :, t], s.ssem.at[k + 2])
                wait(W.at[:, :, :, :, :, :, t], s.ssem.at[k + 3])
            if ts == 0: w()
            else: pl.when(s.p.c == 0)(w)
        o = s.s0_src()
        for tc in (0, 1):
            cond = (o <= 4) if tc == 0 else (o >= 4)
            pl.when(cond)(lambda tc=tc: wait(s.pieces.at[:, 0:3], s.s0s.at[tc]))
            pl.when(jnp.logical_and(cond, s.p.c != tc))(lambda: wait(s.pieces.at[:, 0], s.s0s.at[2]))

def barrier(partners):
    b = pltpu.get_barrier_semaphore()
    for d in partners:
        pl.semaphore_signal(b, inc=1, device_id=d, device_id_type=MESH)
    pl.semaphore_wait(b, len(partners))

def fill_pieces(pieces, wqkv, wout, wup, wdown):
    mats = [(wqkv, 0), (wqkv, 1280), (wqkv, 2560), (wout, 0), (wup, 0), (wdown, 0)]
    for ph in range(3):
        for xh in range(2):
            r, off = mats[2 * ph + xh]
            for par in range(2):
                v = r[:, off + par * 640: off + (par + 1) * 640]
                pieces[ph, 2 * xh + par] = jnp.concatenate([v.astype(jnp.float32), jnp.zeros((6, 640), jnp.float32)], axis=0).astype(jnp.bfloat16)


def dot(a, b):
    return jnp.dot(a, b, preferred_element_type=F32)


def dot_nt(a, b):
    return lax.dot_general(a, b, (((1,), (1,)), ((), ())), preferred_element_type=F32)


def dot_tn(a, b):
    return lax.dot_general(a, b, (((0,), (0,)), ((), ())), preferred_element_type=F32)


def at128(v):
    return pl.multiple_of(v, 128)


def window(z, xl):
    return 320 * z - 64 * (z % 2) + 128 * xl


class Spread:
    def __init__(s, p, T, R0, R1, R2, T3, R3, out, ssem, rsem):
        s.p, s.T, s.T3, s.out, s.ssem, s.rsem = p, T, T3, out, ssem, rsem
        s.R = (R0, R1, R2, R3)

    def start(s, k):
        p = s.p
        src = s.T3 if k == 3 else s.T
        if k == 0: devs = [p.dev(c=1 - p.c)]
        else: devs = [p.ring((1, 0, 2)[k - 1], d) for d in (1, 2, 3)]
        for i, dv in enumerate(devs):
            pltpu.make_async_remote_copy(src, s.R[k].at[i], s.ssem.at[k], s.rsem.at[k], device_id=dv, device_id_type=MESH).start()

    def finish(s, k):
        p = s.p
        R = s.R[k]
        wait(R, s.rsem.at[k])
        wait(R, s.ssem.at[k])
        if k < 2:
            acc = s.T[...].astype(F32)
            for i in range(R.shape[0]): acc = acc + R[i].astype(F32)
            s.T[...] = acc.astype(BF)
        elif k == 2:
            s.T3[...] = jnp.zeros((32, 384), BF)
            mine = pl.ds(at128(128 * p.xl), 256)
            other = pl.ds(at128(128 - 128 * p.xl), 256)
            s.T3[:, mine] = (s.T[...].astype(F32) + R[1].astype(F32)).astype(BF)
            s.T3[:, other] = (s.T3[:, other].astype(F32) + R[0].astype(F32) + R[2].astype(F32)).astype(BF)
        else:
            s.out[...] = jnp.zeros((32, D), BF)
            for i in range(4):
                lanes = pl.ds(at128(window((p.z + 4 - i) % 4, 0)), 384)
                v = s.T3[...] if i == 0 else R[i - 1]
                s.out[:, lanes] = (s.out[:, lanes].astype(F32) + v.astype(F32)).astype(BF)


class Gather:
    def __init__(s, p, buf, R0, R1, S1, R2, S2, R3, R4, ssem, rsem):
        s.p, s.buf, s.R0, s.R1, s.S1, s.R2, s.S2, s.R3, s.R4 = p, buf, R0, R1, S1, R2, S2, R3, R4
        s.ssem, s.rsem = ssem, rsem
        s.active = p.z // 2 == p.c

    def send(s, k, src, dst, dv):
        pltpu.make_async_remote_copy(src, dst, s.ssem.at[k], s.rsem.at[k], device_id=dv, device_id_type=MESH).start()

    def start(s, k):
        p = s.p
        if k == 0:
            s.send(0, s.buf.at[1 - p.c], s.R0, p.dev(c=1 - p.c))
        elif k == 1:
            for d in (1, 2, 3):
                z = (p.z + d) % 4
                @pl.when(z // 2 == p.c)
                def _(z=z, d=d):
                    s.send(1, s.buf.at[p.c, :, pl.ds(at128(256 * (z % 2)), 384)], s.R1.at[d - 1], p.dev(z=z))
        else:
            @pl.when(s.active)
            def _():
                if k == 2:
                    s.send(2, s.S1.at[:, pl.ds(at128(128 - 128 * p.xl), 256)], s.R2, p.dev(x=p.xh * 2 + 1 - p.xl))
                elif k == 3:
                    for d in (1, 2, 3): s.send(3, s.S2, s.R3.at[d - 1], p.ring(1, d))
                else:
                    s.send(4, s.S2, s.R4, p.dev(c=1 - p.c))

    def finish(s, k):
        p = s.p
        if k == 0:
            wait(s.R0, s.rsem.at[0])
            wait(s.R0, s.ssem.at[0])
            s.buf[p.c] = s.buf[p.c] + s.R0[...]
            return
        if k == 1:
            pl.when(s.active)(lambda: wait(s.R1.at[0], s.ssem.at[1]))
            pl.when(jnp.logical_not(s.active))(lambda: wait(s.R1.at[0:2], s.ssem.at[1]))
        if k == 4:
            @pl.when(jnp.logical_not(s.active))
            def _():
                wait(s.R4, s.rsem.at[4])
                s.S2[...] = s.R4[...]
            pl.when(s.active)(lambda: wait(s.R4, s.ssem.at[4]))
            return
        @pl.when(s.active)
        def _():
            if k == 1:
                wait(s.R1, s.rsem.at[1])
                mine = pl.ds(at128(256 * (p.z % 2)), 384)
                s.S1[...] = s.buf[p.c, :, mine] + s.R1[0] + s.R1[1] + s.R1[2]
            elif k == 2:
                wait(s.R2, s.rsem.at[2])
                wait(s.R2, s.ssem.at[2])
                s.S2[...] = s.S1[:, pl.ds(at128(128 * p.xl), 256)] + s.R2[...]
            else:
                wait(s.R3, s.rsem.at[3])
                wait(s.R3, s.ssem.at[3])
                s.S2[...] = s.S2[...] + s.R3[0] + s.R3[1] + s.R3[2]


class RS:
    def __init__(s, p, G, GW, RD, bufs, FR, EX, FIN, dss, drs, ss, rs, fs, fr):
        s.p, s.G, s.GW, s.RD, s.bufs, s.FR, s.EX, s.FIN = p, G, GW, RD, bufs, FR, EX, FIN
        s.dss, s.drs, s.ss, s.rs, s.fs, s.fr = dss, drs, ss, rs, fs, fr

    def gref(s, ph):
        return s.G[ph]

    def go(s, ts, f, other=False):
        def h():
            f()
        if ts < 2: h()
        else: pl.when(s.p.c == (1 if other else 0))(h)

    def d2d(s, ph, ts, act, par):
        p = s.p
        g = s.gref(ph)
        t = 3 * (1 - p.c) + ts if act != 'recv' else 3 * p.c + ts
        cp = pltpu.make_async_remote_copy(g.at[par, :, :, :, t], s.RD.at[ph, ts, par], s.dss.at[ts // 2], s.drs.at[ph * 3 + ts, par], device_id=p.dev(c=1 - p.c), device_id_type=MESH)
        if act == 'start': cp.start()
        else: cp.wait_recv()

    def d2d_start(s, ph, par):
        for ts in range(3): s.go(ts, lambda ts=ts: s.d2d(ph, ts, 'start', par), other=True)

    def d2d_add(s, ph, ts, par):
        g = s.gref(ph)
        t = 3 * s.p.c + ts
        s.d2d(ph, ts, 'recv', par)
        def body(z, _):
            g[par, z, :, :, t] = (g[par, z, :, :, t].astype(F32) + s.RD[ph, ts, par, z].astype(F32)).astype(BF)
            return 0
        lax.fori_loop(0, 4, body, 0)

    def order(s, ph, ts):
        return ((1, 0, 2), (2, 0, 1), (0, 1, 2))[ts]

    def fidx(s, ph, ts):
        return (1, 2, 0)[ts]

    def piece(s, ph, ts, st, k):
        p = s.p
        o = s.order(ph, ts)
        ax = o[st]
        done = o[:st]
        par = h = zz = xl = slice(None)
        if 0 in done: xl = p.xl
        if 1 in done: h, par = p.h, p.par
        if 2 in done: zz = p.z
        if ax == 0: xl = k
        if ax == 1: h, par = k // 2, k % 2
        if ax == 2: zz = k
        return s.gref(ph).at[par, zz, xl, h, 3 * p.c + ts]

    def half(s, ph, ts, st, k, hf):
        p = s.p
        o = s.order(ph, ts)
        ax = o[st]
        assert st == 0
        t = 3 * p.c + ts
        if ax == 1: return s.gref(ph).at[k % 2, pl.ds(2 * hf, 2), :, k // 2, t]
        return s.gref(ph).at[hf, k, :, :, t]

    def bhalf(s, ph, ts, hf):
        f = s.fidx(ph, ts)
        b = s.bufs[f][0]
        if f == 1: return b.at[ph, 2, pl.ds(2 * hf, 2)]
        return b.at[ph, 2, hf]

    def cp(s, src, dst, sk, sl, k, dev):
        return pltpu.make_async_remote_copy(src, dst, s.ss.at[sk], s.rs.at[sl, k], device_id=dev, device_id_type=MESH)

    def add(s, dst, srcs):
        lead = dst.shape[:-2]
        if len(lead) >= 1 and lead[0] > 1:
            def body(i, _):
                acc = dst[i].astype(F32)
                for r in srcs: acc = acc + r[i].astype(F32)
                dst[i] = acc.astype(BF)
                return 0
            lax.fori_loop(0, lead[0], body, 0)
        else:
            acc = dst[...].astype(F32)
            for r in srcs: acc = acc + r[...].astype(F32)
            dst[...] = acc.astype(BF)

    def ring_cps(s, ph, ts, st):
        p = s.p
        o = s.order(ph, ts)
        ax = o[st]
        f = s.fidx(ph, ts)
        sl = ph * 3 + ts
        b = s.bufs[f][st]
        sk = st + (3 if ts == 2 else 0)
        if ax == 0:
            k = 1 - p.xl
            src, dv = s.piece(ph, ts, st, k), p.dev(x=p.xh * 2 + k)
            if st == 0: return [s.cp(src.at[par], b.at[ph, 0, par], sk, sl, par, dv) for par in range(2)]
            return [s.cp(src, b.at[ph, 0], sk, sl, 2 + st, dv)]
        res = []
        for i, d in enumerate((1, 3, 2)):
            res.append(s.cp(s.piece(ph, ts, st, p.coord(ax, d)), b.at[ph, i], sk, sl, 2 + st, p.ring(ax, d)))
        return res

    def first_a(s, ph, ts, par):
        ax = s.order(ph, ts)[0]
        if ax == 0:
            s.ring_cps(ph, ts, 0)[par].start()
        elif ax == 2:
            s.sf_half(ph, ts)[1 - par].start()
        else:
            @pl.when(s.p.par == par)
            def _():
                for c in s.sf_half(ph, ts): c.start()

    def sf_half(s, ph, ts):
        p = s.p
        ax = s.order(ph, ts)[0]
        sl = ph * 3 + ts
        k = p.coord(ax, 2)
        return [s.cp(s.half(ph, ts, 0, k, 1), s.bhalf(ph, ts, 1), 0, sl, 0, p.ring(ax, 1)),
                s.cp(s.half(ph, ts, 0, k, 0), s.bhalf(ph, ts, 0), 0, sl, 1, p.ring(ax, 3))]

    def sf_full(s, ph, ts):
        p = s.p
        ax = s.order(ph, ts)[0]
        sl = ph * 3 + ts
        b = s.bufs[s.fidx(ph, ts)][0]
        return [s.cp(s.piece(ph, ts, 0, p.coord(ax, 1)), b.at[ph, 0], 0, sl, 2, p.ring(ax, 1)),
                s.cp(s.piece(ph, ts, 0, p.coord(ax, 3)), b.at[ph, 1], 0, sl, 2, p.ring(ax, 3))]

    def first_b(s, ph, ts):
        p = s.p
        o = s.order(ph, ts)
        ax = o[0]
        if ax == 0: return
        hb = s.sf_half(ph, ts)
        full = s.sf_full(ph, ts)
        hb[0].wait_recv()
        s.add(s.half(ph, ts, 0, p.coord(ax, 1), 1), [s.bhalf(ph, ts, 1)])
        full[0].start()
        hb[1].wait_recv()
        s.add(s.half(ph, ts, 0, p.coord(ax, 3), 0), [s.bhalf(ph, ts, 0)])
        full[1].start()

    def first_c(s, ph, ts):
        p = s.p
        o = s.order(ph, ts)
        ax = o[0]
        me = (p.xl, p.y, p.z)[ax]
        b = s.bufs[s.fidx(ph, ts)][0]
        if ax == 0:
            for par, c in enumerate(s.ring_cps(ph, ts, 0)):
                c.wait_recv()
                s.add(s.piece(ph, ts, 0, me).at[par], [b.at[ph, 0, par]])
            return
        wait(b.at[ph, 0:2], s.rs.at[ph * 3 + ts, 2])
        s.add(s.piece(ph, ts, 0, me), [b.at[ph, i] for i in range(2)])

    def next_start(s, ph, ts, st):
        for c in s.ring_cps(ph, ts, st): c.start()

    def next_finish(s, ph, ts, st):
        p = s.p
        ax = s.order(ph, ts)[st]
        me = (p.xl, p.y, p.z)[ax]
        b = s.bufs[s.fidx(ph, ts)][st]
        wait(b.at[ph], s.rs.at[ph * 3 + ts, 2 + st])
        s.add(s.piece(ph, ts, st, me), [b.at[ph, i] for i in range(1 if ax == 0 else 3)])

    def each(s, f):
        for ts in range(3): s.go(ts, lambda ts=ts: f(ts))

    def first(s, ph, par):
        s.each(lambda ts: (s.d2d_add(ph, ts, par), s.first_a(ph, ts, par)))

    def step(s, ph, k):
        if k == 2: s.each(lambda ts: s.first_b(ph, ts))
        elif k == 3: s.each(lambda ts: (s.first_c(ph, ts), s.next_start(ph, ts, 1)))
        elif k == 4: s.each(lambda ts: (s.next_finish(ph, ts, 1), s.next_start(ph, ts, 2)))
        elif k == 5:
            s.each(lambda ts: s.next_finish(ph, ts, 2))
            s.final_start(ph)

    def fin_cps(s, ph, k):
        p = s.p
        o = 4 * p.c + k
        chunk = 2 * p.xh + p.par
        dev = p.dev(x=(o % 2) * 2 + p.xl, y=2 * p.h + o // 4, c=(o // 2) % 2)
        return pltpu.make_async_remote_copy(s.EX.at[ph, k], s.FIN.at[ph, chunk, p.c], s.fs.at[0], s.fr.at[ph, p.c], device_id=dev, device_id_type=MESH)

    def myo(s):
        p = s.p
        return (p.par * 2 + p.c) * 2 + p.xh

    def final_start(s, ph):
        p = s.p
        g = s.gref(ph)
        def put(ts):
            s.FR[ts] = g[p.par, p.z, p.xl, p.h, 3 * p.c + ts]
        put(0); put(1)
        pl.when(p.c == 0)(lambda: put(2))
        i = lax.broadcasted_iota(jnp.int32, (80, 48), 1)
        k = lax.broadcasted_iota(jnp.int32, (80, 48), 0)
        r = 48 * p.c + i
        q = (r * 205) >> 11
        col = (q - 4 * p.c) * 16 + (r - q * 10)
        pt = jnp.where(k == col, 1.0, 0.0).astype(BF)
        s.EX[ph] = dot(pt, s.FR[...].reshape(48, CW)).astype(BF).reshape(5, 16, CW)
        for k in range(5):
            def send(k=k):
                me = 4 * p.c + k == s.myo()
                @pl.when(me)
                def _():
                    s.FIN[ph, 2 * p.xh + p.par, p.c] = s.EX[ph, k]
                @pl.when(jnp.logical_not(me))
                def _():
                    s.fin_cps(ph, k).start()
            if k < 4: send()
            else: pl.when(p.c == 0)(send)

    def final_wait(s, ph):
        p = s.p
        o = s.myo()
        for sc in range(2):
            used = (o <= 4) if sc == 0 else (o >= 4)
            pl.when(jnp.logical_and(used, p.c == sc))(lambda: wait(s.FIN.at[ph, 0:3, 0], s.fr.at[ph, sc]))
            pl.when(jnp.logical_and(used, p.c != sc))(lambda: wait(s.FIN.at[ph, :, 0], s.fr.at[ph, sc]))

    def drain(s):
        p = s.p
        G = s.GW
        wait(G.at[:, :, :, :, :, 0:2], s.dss.at[0])
        pl.when(p.c == 1)(lambda: wait(G.at[:, :, :, :, :, 0], s.dss.at[1]))
        wait(G.at[:, :, 0:3, :, :, 0:2], s.ss.at[0])
        wait(G.at[:, 0, :, 0, 0, 0:2], s.ss.at[1])
        wait(G.at[:, 0, 0:3, 0, 0, 0:2], s.ss.at[2])
        @pl.when(p.c == 0)
        def _():
            wait(G.at[:, :, :, :, 0, 0], s.ss.at[3])
            wait(G.at[:, 0, 0:3, :, :, 0], s.ss.at[4])
            wait(G.at[:, 0, 0:3, 0, 0, 0], s.ss.at[5])
        o = s.myo()
        n = jnp.where(p.c == 0, jnp.where(o <= 4, 4, 5), jnp.where(o >= 4, 3, 4))
        for k in (3, 4, 5):
            pl.when(n == k)(lambda k=k: wait(s.EX.at[:, 0:k], s.fs.at[0]))


def clear_last(stg, FR):
    stg[:, 4] = jnp.zeros((3, 16, CW), BF)
    FR[2] = jnp.zeros((16, CW), BF)


FIRST, Q, K, V, MIXED, SECOND, ACTIVE, GU, GAO, GMX, GQ, GK, GV = range(13)
RB = 32
UNROLL = 4


def block_kernel(lat_in, cot_in, sid, *refs):
    small_in, (o_lat, o_in), small_out = refs[0:8], refs[8:10], refs[10:16]
    block_body(lat_in, cot_in, sid, small_in, o_lat, o_in, small_out, *refs[16:])


def block_body(lat_in, cot_in, sid_in, small_in, o_lat, o_in, small_out,
                 W, stg, pieces, A, N1, N2, MID, DG, PR, I1, I2, VEC, CS, GW, RD, b00, b01, b02, b10, b11, b12, b20, b21, b22,
                 FR, EX, FIN, SB, SBT, SB0, SB1, SB2, SBT3, SB3, SG, SG0, SG1, SGS1, SG2, SGS2, SG3, SG4,
                 lat, cot, sid, gt, b1, g2, b2, wq, wo, wu, wd, o_tab, o_vec, o_qkv, o_out, o_up, o_down, ssem, rsem, s0s, s0r, dss, drs, gss, grs, fs, fr, sbs, sbr, sgs, sgr, io):
    p = Pos()
    ag = AG(p, W, stg, pieces, ssem, rsem, None, s0s, s0r)
    G = [GW.at[0], GW.at[1], GW.at[2]]
    rs = RS(p, G, GW, RD, [[b00, b01, b02], [b10, b11, b12], [b20, b21, b22]], FR, EX, FIN, dss, drs, gss, grs, fs, fr)
    sb = Spread(p, SBT, SB0, SB1, SB2, SBT3, SB3, SB, sbs, sbr)
    sg = Gather(p, SG, SG0, SG1, SGS1, SG2, SGS2, SG3, SG4, sgs, sgr)
    idx = lax.axis_index("dp") * 2 + p.xh

    parts = ag.partners()
    bar = pltpu.get_barrier_semaphore()
    for d in parts:
        pl.semaphore_signal(bar, inc=1, device_id=d, device_id_type=MESH)
    in_lat = pltpu.make_async_copy(lat_in, lat, io.at[0])
    in_cot = pltpu.make_async_copy(cot_in, cot, io.at[1])
    in_sid = pltpu.make_async_copy(sid_in, sid, io.at[12])
    in_sid.start()
    ins = [pltpu.make_async_copy(a, v, io.at[4 + i]) for i, (a, v) in enumerate(zip(small_in, (gt, b1, g2, b2, wq, wo, wu, wd)))]
    for c in ins: c.start()
    in_lat.start(); in_cot.start()
    for c in ins: c.wait()
    fill_pieces(pieces, wq, wo, wu, wd)
    pl.when(p.c == 1)(lambda: clear_last(stg, FR))
    j = lax.broadcasted_iota(jnp.int32, (16, 256), 0)
    lane = lax.broadcasted_iota(jnp.int32, (16, 256), 1) + window(p.z, p.xl)
    own = jnp.where(jnp.logical_and(lane == idx * 10 + j, j < 10), 1.0, 0.0)
    own16 = own[0:10].astype(BF)
    spread = [dot_tn(gt[...], own16)] + [dot(jnp.broadcast_to(b[...].reshape(1, 10), (8, 10)), own16)[0:1] for b in (b1, g2, b2)] + [jnp.zeros((13, 256), F32)]
    SBT[...] = jnp.concatenate(spread, axis=0).astype(BF)
    pl.semaphore_wait(bar, len(parts))

    sb.start(0)
    for ph in range(3): ag.s0(ph)

    def ln1(r, _):
        rows = pl.ds(pl.multiple_of(r * RB, RB), RB)
        x = lat[rows, :].astype(F32)
        mu = jnp.mean(x, axis=-1, keepdims=True)
        xc = x - mu
        inv = lax.rsqrt(jnp.mean(xc * xc, axis=-1, keepdims=True) + EPS)
        N1[rows, :] = xc * inv
        I1[rows, :] = jnp.broadcast_to(inv, (RB, 128))
        return 0
    in_lat.wait(); in_cot.wait(); in_sid.wait()
    lax.fori_loop(0, L // RB, ln1, 0, unroll=UNROLL)
    ag.s0_recv(0); ag.compact(0); ag.phase_a(0)
    sb.finish(0); sb.start(1)
    ag.s0_recv(1); ag.compact(1); ag.phase_a(1)
    ag.phase_b(0)
    sb.finish(1); sb.start(2)
    ag.s0_recv(2); ag.compact(2); ag.phase_a(2)
    ag.phase_b(1)
    ag.phase_c(0)
    sb.finish(2); sb.start(3)
    ag.phase_b(2)
    ag.phase_c(1)
    A[MIXED] = jnp.zeros((L, D), BF)
    for k in (GQ, GK, GV): A[k] = jnp.zeros((L, D), BF)
    CS[...] = jnp.zeros_like(CS)
    ag.phase_d(0)
    ag.phase_c(2)
    sb.finish(3)
    lane32 = lax.broadcasted_iota(jnp.int32, (8, 32), 1)
    sub8 = lax.broadcasted_iota(jnp.int32, (8, 32), 0)
    tgt = jnp.where(sub8 == 0, sid[0], jnp.where(sub8 < 4, 15 + sub8, -1))
    pick = jnp.where(lane32 == tgt, 1.0, 0.0).astype(BF)
    VEC[...] = dot(pick, SB[...])

    def mk_first(r, _):
        rows = pl.ds(pl.multiple_of(r * RB, RB), RB)
        A[FIRST, rows, :] = (N1[rows, :] * VEC[0:1, :] + VEC[1:2, :]).astype(BF)
        return 0
    lax.fori_loop(0, L // RB, mk_first, 0, unroll=UNROLL)
    ag.phase_d(1)
    ag.phase_e(0)
    ag.phase_f(0)

    def wpan(ph, xh, par): return W[ph, xh, par].reshape(D, CW)
    def cols(par): return pl.ds(par * CW, CW)

    for par in range(2):
        A[Q, :, cols(par)] = dot(A[FIRST], wpan(0, 0, par)).astype(BF)
    ag.phase_d(2)
    for par in range(2):
        A[K, :, cols(par)] = dot(A[FIRST], wpan(0, 1, par)).astype(BF)
    ag.phase_e(1)
    ag.phase_f(1)
    for par in range(2):
        A[V, :, cols(par)] = dot(A[FIRST], wpan(1, 0, par)).astype(BF)

    lane256 = lax.broadcasted_iota(jnp.int32, (1, 256), 1)
    def masks(w):
        m = jnp.where(jnp.logical_and(lane256 >= 32 * w, lane256 < 32 * w + HD), 1.0, 0.0)
        return m, m.astype(BF)
    def win(pn, w):
        return pl.ds(pl.multiple_of(pn * CW + w * 128, 128), 256)

    for pn in range(2):
        def att(w, _, pn=pn):
            cw = win(pn, w)
            m32, m16 = masks(w)
            sc = dot_nt(A[Q, :, cw] * m16, A[K, :, cw]) * SCALE
            e = jnp.exp(sc - jnp.max(sc, axis=-1, keepdims=True))
            pr = e * (1.0 / jnp.sum(e, axis=-1, keepdims=True))
            PR[pn * 4 + w] = pr
            mx = dot(pr.astype(BF), A[V, :, cw]) * m32
            A[MIXED, :, cw] = A[MIXED, :, cw] + mx.astype(BF)
            return 0
        lax.fori_loop(0, 4, att, 0, unroll=True)
    ag.phase_e(2)
    for par in range(2):
        MID[:, cols(par)] = lat[:, cols(par)].astype(F32) + dot(A[MIXED], wpan(1, 1, par))

    def ln2(r, _):
        rows = pl.ds(pl.multiple_of(r * RB, RB), RB)
        x = MID[rows, :]
        mu = jnp.mean(x, axis=-1, keepdims=True)
        xc = x - mu
        inv = lax.rsqrt(jnp.mean(xc * xc, axis=-1, keepdims=True) + EPS)
        n = xc * inv
        N2[rows, :] = n
        I2[rows, :] = jnp.broadcast_to(inv, (RB, 128))
        A[SECOND, rows, :] = (n * VEC[2:3, :] + VEC[3:4, :]).astype(BF)
        return 0
    lax.fori_loop(0, L // RB, ln2, 0, unroll=UNROLL)
    ag.phase_f(2)
    for par in range(2):
        DG[:, cols(par)] = dot(A[SECOND], wpan(2, 0, par))

    def gelu(r, _):
        rows = pl.ds(pl.multiple_of(r * RB, RB), RB)
        u = DG[rows, :]
        c0 = math.sqrt(2.0 / math.pi)
        u2 = u * u
        th = jnp.tanh(c0 * (u + 0.044715 * u2 * u))
        hp = 0.5 * (1.0 + th)
        A[ACTIVE, rows, :] = (u * hp).astype(BF)
        DG[rows, :] = hp + 0.5 * u * (1.0 - th * th) * (c0 * (1.0 + 3 * 0.044715 * u2))
        return 0
    lax.fori_loop(0, L // RB, gelu, 0, unroll=UNROLL)

    def back(src, ph, xh, n):
        acc = None
        for par in range(2):
            t = dot_nt(src(par), W[ph, xh, par, 2 * n:2 * n + 2].reshape(CW, CW))
            acc = t if acc is None else acc + t
        return acc

    half = pl.ds(pl.multiple_of(p.xh * CW, 128), CW)

    def wgrad(ph, par, left, right):
        for n in range(2):
            v = dot_tn(A[left, :, cols(n)], right[:, half])
            G[ph][par, 2 * n:2 * n + 2] = v.astype(BF).reshape(2, 2, 2, 5, 16, CW)
        rs.d2d_start(ph, par)

    wgrad(2, 1, ACTIVE, cot)
    for n in range(2):
        A[GU, :, cols(n)] = (back(lambda par: cot[:, cols(par)], 2, 1, n) * DG[:, cols(n)]).astype(BF)
    wgrad(2, 0, SECOND, A.at[GU])
    for n in range(2):
        DG[:, cols(n)] = back(lambda par: A[GU, :, cols(par)], 2, 0, n)

    rs.first(2, 1)

    def ln2b(r, _):
        rows = pl.ds(pl.multiple_of(r * RB, RB), RB)
        gs = DG[rows, :]
        n = N2[rows, :]
        CS[1] += jnp.sum((gs * n).reshape(RB // 8, 8, D), axis=0)
        CS[2] += jnp.sum(gs.reshape(RB // 8, 8, D), axis=0)
        dn = gs * VEC[2:3, :]
        m1 = jnp.mean(dn, axis=-1, keepdims=True)
        m2 = jnp.mean(dn * n, axis=-1, keepdims=True)
        gm = cot[rows, :].astype(F32) + I2[rows, 0:1] * (dn - m1 - n * m2)
        N2[rows, :] = gm
        A[GAO, rows, :] = gm.astype(BF)
        return 0
    lax.fori_loop(0, L // RB, ln2b, 0, unroll=UNROLL)
    wgrad(1, 1, MIXED, A.at[GAO])
    for n in range(2):
        A[GMX, :, cols(n)] = back(lambda par: A[GAO, :, cols(par)], 1, 1, n).astype(BF)
        if n == 0: rs.first(2, 0)

    for i in range(2):
        pn = p.xh if i == 0 else 1 - p.xh
        def attb(w, _, pn=pn):
            cw = win(pn, w)
            m32, m16 = masks(w)
            gm = A[GMX, :, cw] * m16
            qm = A[Q, :, cw] * m16
            pr = PR[pn * 4 + w]
            gp = dot_nt(gm, A[V, :, cw])
            rt = jnp.sum(gp * pr, axis=-1, keepdims=True)
            gsc = (pr * (gp - rt)).astype(BF)
            A[GV, :, cw] = A[GV, :, cw] + dot_tn(pr.astype(BF), gm).astype(BF)
            A[GQ, :, cw] = A[GQ, :, cw] + (dot(gsc, A[K, :, cw]) * SCALE * m32).astype(BF)
            A[GK, :, cw] = A[GK, :, cw] + (dot_tn(gsc, qm) * SCALE).astype(BF)
            return 0
        lax.fori_loop(0, 2, attb, 0, unroll=True)
        if i == 0:
            rs.first(1, 1)
            rs.step(2, 2)
        else:
            rs.first(1, 0)
            rs.first(0, 0)
            rs.first(0, 1)
            rs.step(2, 3)
        lax.fori_loop(2, 4, attb, 0, unroll=True)
        if i == 0:
            wgrad(1, 0, FIRST, A.at[GV])
            wgrad(0, 0, FIRST, A.at[GQ])
            wgrad(0, 1, FIRST, A.at[GK])
    rs.step(1, 2)
    rs.step(0, 2)
    for n in range(2):
        acc = None
        for g, (ph, xh) in ((GQ, (0, 0)), (GK, (0, 1)), (GV, (1, 0))):
            t = back(lambda par: A[g, :, cols(par)], ph, xh, n)
            acc = t if acc is None else acc + t
        DG[:, cols(n)] = acc
    rs.step(2, 4)

    def ln1b(r, _):
        rows = pl.ds(pl.multiple_of(r * RB, RB), RB)
        gf = DG[rows, :]
        n = N1[rows, :]
        CS[3] += jnp.sum((gf * n).reshape(RB // 8, 8, D), axis=0)
        CS[0] += jnp.sum(gf.reshape(RB // 8, 8, D), axis=0)
        dn = gf * VEC[0:1, :]
        m1 = jnp.mean(dn, axis=-1, keepdims=True)
        m2 = jnp.mean(dn * n, axis=-1, keepdims=True)
        DG[rows, :] = N2[rows, :] + I1[rows, 0:1] * (dn - m1 - n * m2)
        return 0
    lax.fori_loop(0, L // RB, ln1b, 0, unroll=UNROLL)
    out_in = pltpu.make_async_copy(DG, o_in, io.at[3])
    out_in.start()
    sub24 = lax.broadcasted_iota(jnp.int32, (24, 640), 0)
    for k in range(2):
        v = [jnp.sum(CS[i, :, k * 640:(k + 1) * 640], axis=0, keepdims=True) for i in range(4)]
        SG[k] = (jnp.where(sub24 == sid[0], v[3], 0.0) + jnp.where(sub24 == 16, v[0], 0.0)
                 + jnp.where(sub24 == 17, v[1], 0.0) + jnp.where(sub24 == 18, v[2], 0.0))
    sg.start(0)
    rs.step(1, 3)
    rs.step(0, 3)
    for par in range(2):
        A[SECOND, :, cols(par)] = (MID[:, cols(par)] + dot(A[ACTIVE], wpan(2, 1, par))).astype(BF)
    out_lat = pltpu.make_async_copy(A.at[SECOND], o_lat, io.at[2])
    out_lat.start()
    sg.finish(0); sg.start(1)
    rs.step(2, 5)
    rs.step(1, 4)
    rs.step(0, 4)
    sg.finish(1); sg.start(2)
    ag.drain()
    rs.step(1, 5)
    rs.step(0, 5)
    sg.finish(2); sg.start(3)

    outs = [(o_qkv, 0), (o_qkv, 1280), (o_qkv, 2560), (o_out, 0), (o_up, 0), (o_down, 0)]
    def emit(ph):
        rs.final_wait(ph)
        o_id = rs.myo()
        sel = jnp.where(o_id > 4, 1, 0)
        @pl.when(o_id == 4)
        def _():
            FIN[ph, :, 0] = FIN[ph, :, 0] + FIN[ph, :, 1]
        for xh in range(2):
            for par in range(2):
                o, off = outs[2 * ph + par]
                v = FIN[ph, 2 * xh + par, sel].astype(F32)
                o[:, off + xh * 640: off + (xh + 1) * 640] = v[0:10]
    emit(2)
    sg.finish(3); sg.start(4)
    emit(1)
    sg.finish(4)
    hi = lax.Precision.HIGHEST
    tab = lax.dot_general(own, SGS2[...], (((1,), (1,)), ((), ())), precision=hi, preferred_element_type=F32)
    vec = lax.dot_general(SGS2[16:24], own, (((1,), (1,)), ((), ())), precision=hi, preferred_element_type=F32)
    o_tab[...] = tab[0:10, 0:16]
    o_vec[...] = vec[:, 0:10]
    emit(0)
    outs = [pltpu.make_async_copy(v, o, io.at[4 + i]) for i, (v, o) in enumerate(zip((o_tab, o_vec, o_qkv, o_out, o_up, o_down), small_out))]
    for c in outs: c.start()
    rs.drain()
    out_lat.wait(); out_in.wait()
    for c in outs: c.wait()


def results_kernel(lat, inp, tab, vec, qkv, out, up, down, o_lat, o_in, o_tab, o_b1, o_g2, o_b2, o_qkv, o_out, o_up, o_down,
                   v_lat, v_in, v_tab, v_vec, v_qkv, v_out, v_up, v_down, v_b1, v_g2, v_b2, sem):
    first = pltpu.make_async_copy(vec, v_vec, sem.at[0])
    first.start()
    moves = []
    for a, v, o, n in ((inp, v_in, o_in, 4), (lat, v_lat, o_lat, 2), (qkv, v_qkv, o_qkv, 1), (out, v_out, o_out, 1), (up, v_up, o_up, 1), (down, v_down, o_down, 1), (tab, v_tab, o_tab, 1)):
        for k in range(n):
            c = a.shape[0] // n
            cut = (lambda r: r.at[pl.ds(k * c, c)]) if n > 1 else (lambda r: r)
            i = 2 + 2 * len(moves)
            moves.append((pltpu.make_async_copy(cut(a), cut(v), sem.at[i]), pltpu.make_async_copy(cut(v), cut(o), sem.at[i + 1])))
    for a, _ in moves: a.start()
    first.wait()
    small = []
    for i, (v, o) in enumerate(((v_b1, o_b1), (v_g2, o_g2), (v_b2, o_b2))):
        v[...] = v_vec[i]
        small.append(pltpu.make_async_copy(v, o, sem.at[24 + i]))
        small[-1].start()
    for a, b in moves:
        a.wait()
        b.start()
    for _, b in moves: b.wait()
    for c in small: c.wait()


def per_device(latents, script_ids, gain_table, bias_one, w_qkv, w_out, gain_two, bias_two, w_up, w_down, cotangent):
    V_ = pltpu.VMEM
    dma = pltpu.SemaphoreType.DMA
    blk = (16, CW)
    scratch = [
        V_((3, 2, 2, 4, 2, 2, 5, 16, CW), BF), V_((3, 5) + blk, BF), V_((3, 4) + blk, BF),
        V_((13, L, D), BF), V_((L, D), F32), V_((L, D), F32), V_((L, D), F32), V_((L, D), F32),
        V_((8, 256, 256), F32), V_((L, 128), F32), V_((L, 128), F32), V_((8, D), F32), V_((4, 8, D), F32),
        V_((3, 2, 4, 2, 2, 5) + blk, BF), V_((3, 3, 2, 4, 2, 2) + blk, BF),
        V_((3, 1, 2, 4, 2) + blk, BF), V_((3, 3, 4) + blk, BF), V_((3, 3) + blk, BF),
        V_((3, 3, 4, 2) + blk, BF), V_((3, 1, 4) + blk, BF), V_((3, 3) + blk, BF),
        V_((3, 3, 2, 2, 2) + blk, BF), V_((3, 1, 2, 2) + blk, BF), V_((3, 3) + blk, BF),
        V_((3,) + blk, BF), V_((3, 5) + blk, BF), V_((3, 4, 2) + blk, BF),
        V_((32, D), BF), V_((32, 256), BF), V_((1, 32, 256), BF), V_((3, 32, 256), BF), V_((3, 32, 256), BF), V_((32, 384), BF), V_((3, 32, 384), BF),
        V_((2, 24, 640), F32), V_((24, 640), F32), V_((3, 24, 384), F32), V_((24, 384), F32), V_((24, 256), F32), V_((24, 256), F32), V_((3, 24, 256), F32), V_((24, 256), F32), V_((L, D), BF), V_((L, D), BF), pltpu.SMEM((1,), jnp.int32),
        V_((10, 16), BF), V_((10,), BF), V_((10,), BF), V_((10,), BF), V_((10, 3 * D), BF), V_((10, D), BF), V_((10, D), BF), V_((10, D), BF),
        V_((10, 16), F32), V_((8, 10), F32), V_((10, 3 * D), F32), V_((10, D), F32), V_((10, D), F32), V_((10, D), F32),
        dma((8,)), dma((9, 6)), dma((3,)), dma((3,)),
        dma((2,)), dma((9, 2)), dma((6,)), dma((9, 5)), dma((1,)), dma((3, 2)),
        dma((4,)), dma((4,)), dma((5,)), dma((5,)), dma((13,)),
    ]
    hbm = pl.BlockSpec(memory_space=pl.ANY)
    f32 = lambda *d: jax.ShapeDtypeStruct(d, F32)
    res = pl.pallas_call(
        block_kernel,
        out_shape=[jax.ShapeDtypeStruct((L, D), BF), f32(L, D), f32(10, 16), f32(8, 10), f32(10, 3 * D), f32(10, D), f32(10, D), f32(10, D)],
        in_specs=[hbm, hbm, pl.BlockSpec(memory_space=pltpu.HBM)] + [hbm] * 8,
        out_specs=[hbm] * 8,
        scratch_shapes=scratch,
        compiler_params=pltpu.CompilerParams(collective_id=0, has_side_effects=True, vmem_limit_bytes=62 * 2**20),
        name="block",
    )(latents.reshape(L, D), cotangent.reshape(L, D), script_ids, gain_table, bias_one, gain_two, bias_two, w_qkv, w_out, w_up, w_down)
    o_lat, o_in, o_tab, o_b1, o_g2, o_b2, o_qkv, o_out, o_up, o_down = pl.pallas_call(
        results_kernel,
        out_shape=[jax.ShapeDtypeStruct((L, D), BF), f32(L, D), f32(10, 16), f32(10), f32(10), f32(10), f32(10, 3 * D), f32(10, D), f32(10, D), f32(10, D)],
        in_specs=[hbm] * 8,
        out_specs=[hbm] * 10,
        scratch_shapes=[V_((L, D), BF), V_((L, D), F32), V_((10, 16), F32), V_((8, 10), F32), V_((10, 3 * D), F32), V_((10, D), F32), V_((10, D), F32), V_((10, D), F32),
                        V_((10,), F32), V_((10,), F32), V_((10,), F32), dma((27,))],
        compiler_params=pltpu.CompilerParams(vmem_limit_bytes=62 * 2**20),
        name="results",
    )(*res)
    return (o_lat.reshape(1, L, D), o_in.reshape(1, L, D), o_tab, o_b1, o_qkv, o_out, o_g2, o_b2, o_up, o_down)


def solution(mesh):
    row = P(("dp", "fsdp"), None)
    vec = P(("dp", "fsdp"))
    item = P("dp", None, None)
    return jax.shard_map(
        per_device,
        mesh=mesh,
        in_specs=(item, P("dp"), row, vec, row, row, vec, vec, row, row, item),
        out_specs=(item, item, row, vec, row, row, vec, vec, row, row),
        check_vma=False,
    )
```

```python
import math

import jax
import jax.numpy as jnp
from jax import lax
from jax.experimental import pallas as pl
from jax.experimental.pallas import tpu as pltpu
from jax.sharding import PartitionSpec as P

HEADS = 8
HD = 160
D = 1280
L = 256
EPS = 1e-5
SCALE = 1.0 / math.sqrt(HD)
BF = jnp.bfloat16
F32 = jnp.float32

MESH = pl.DeviceIdType.MESH
CW = 640

class Pos:
    def __init__(s):
        dp = lax.axis_index("dp"); s.xh = lax.axis_index("fsdp")
        s.c = (dp & 1); s.y = (((dp >> 1)) & 3); s.xl = ((dp >> 3) & 1); s.z = dp >> 4
        s.x = s.xh * 2 + s.xl; s.h = (s.y >> 1); s.par = (s.y & 1)
        s.coords = [[(v + d) & 3 if d else v for d in range(4)] for v in (s.x, s.y, s.z)]
        s.rings = [[s.dev(**{n: s.coords[ax][d]}) for d in range(4)] for ax, n in enumerate('xyz')]
        s.sibling = s.dev(c=1 - s.c)
        s.pair = s.dev(x=s.xh * 2 + 1 - s.xl)
    def dev(s, x=None, y=None, z=None, c=None):
        x = s.x if x is None else x; y = s.y if y is None else y
        z = s.z if z is None else z; c = s.c if c is None else c
        return (((z * 2 + (x & 1)) * 4 + y) * 2 + c, (x >> 1))
    def ring(s, ax, d):
        return s.rings[ax][d & 3]
    def coord(s, ax, d):
        return s.coords[ax][d & 3]

def wait(ref, sem):
    pltpu.make_async_copy(ref, ref, sem).wait()

class AG:
    def __init__(s, p, W, stg, pieces, ssem, rsem, sib_r, s0s, s0r):
        s.p, s.W, s.stg, s.pieces = p, W, stg, pieces
        s.ssem, s.rsem, s.s0s, s.s0r = ssem, rsem, s0s, s0r
    def partners(s):
        p = s.p
        out = []
        for ax in range(3):
            for d in (1, 2, 3): out.append(p.ring(ax, d))
        for dy in (0, 1):
            for dx in (0, 1):
                for dc in (0, 1):
                    if (dy, dx, dc) == (0, 0, 0): continue
                    if (dy, dx, dc) == (0, 1, 0): continue
                    y = p.y ^ dy if dy else p.y
                    x = ((p.x + 2 * dx) & 3)
                    out.append(p.dev(x=x, y=y, c=((p.c + dc) & 1)))
        return out
    def s0_targets(s):
        p = s.p
        res = []
        for dy in (0, 1):
            for dx in (0, 1):
                y = p.y ^ dy if dy else p.y
                x = ((p.x + 2 * dx) & 3)
                res.append((dy, dx, y, x))
        return res
    def s0_src(s):
        p = s.p
        return (p.par * 2 + p.c) * 2 + p.xh
    def s0(s, ph):
        p = s.p; o = s.s0_src()
        for tc in (0, 1):
            cond = (o <= 4) if tc == 0 else (o >= 4)
            @pl.when(cond)
            def _(tc=tc):
                for dy, dx, y, x in s.s0_targets():
                    src = s.pieces.at[ph, ((x >> 1)) * 2 + (y & 1)]
                    dst = s.stg.at[ph, o - 4 * tc]
                    def send(sem):
                        pltpu.make_async_remote_copy(src, dst, s.s0s.at[sem], s.s0r.at[ph], device_id=p.dev(y=y, x=x, c=tc), device_id_type=MESH).start()
                    if dy == 0 and dx == 0:
                        @pl.when(p.c == tc)
                        def _():
                            pltpu.make_async_copy(src, dst, s.s0r.at[ph]).start()
                        @pl.when(p.c != tc)
                        def _():
                            send(2)
                    else:
                        send(tc)
    def s0_recv(s, ph):
        pl.when(s.p.c == 0)(lambda: wait(s.stg.at[ph], s.s0r.at[ph]))
        pl.when(s.p.c == 1)(lambda: wait(s.stg.at[ph, 0:4], s.s0r.at[ph]))
    def compact(s, ph):
        p = s.p
        i = lax.broadcasted_iota(jnp.int32, (48, 80), 0)
        k = lax.broadcasted_iota(jnp.int32, (48, 80), 1)
        r = 48 * p.c + i
        q = (r * 205) >> 11
        col = (q - 4 * p.c) * 16 + (r - q * 10)
        P = jnp.where(k == col, 1.0, 0.0).astype(jnp.bfloat16)
        res = jnp.dot(P, s.stg[ph].reshape(80, CW), preferred_element_type=jnp.float32).astype(jnp.bfloat16)
        def put(ts):
            s.W[ph, p.xh, p.par, p.z, p.xl, p.h, 3 * p.c + ts] = res[ts * 16:(ts + 1) * 16]
        put(0); put(1)
        pl.when(p.c == 0)(lambda: put(2))
    def order(s, ph, ts):
        a = (ph + ts) % 3
        return ((a + 1) % 3, (a + 2) % 3, a)
    def region(s, ph, t, full, over=None):
        p = s.p; o = over or {}
        x = o.get(0); y = o.get(1); z = o.get(2)
        xh, xl = (p.xh, p.xl) if x is None else ((x >> 1), (x & 1))
        h, par = (p.h, p.par) if y is None else ((y >> 1), (y & 1))
        zz = p.z if z is None else z
        if 0 in full: xh = xl = slice(None)
        if 1 in full: h = par = slice(None)
        if 2 in full: zz = slice(None)
        return [ph, xh, par, zz, xl, h, t]
    def ref(s, reg): return s.W.at[tuple(reg)]
    def cp(s, reg, ph, ts, kind, k, dev):
        r = s.ref(reg)
        return pltpu.make_async_remote_copy(r, r, s.ssem.at[kind + (4 if ts == 2 else 0)], s.rsem.at[ph * 3 + ts, k], device_id=dev, device_id_type=MESH)
    def half(s, reg, full, hf):
        reg = list(reg)
        i = 3 if 2 in full else (1 if 0 in full else 2)
        reg[i] = pl.ds(hf * 2, 2) if i == 3 else pl.ds(hf, 1)
        return reg
    def t(s, ts): return 3 * s.p.c + ts
    def direct(s, stage, ph, ts):
        a = s.order(ph, ts); full = a[:stage]; ax = a[stage]
        for d in (1, 3, 2):
            s.cp(s.region(ph, s.t(ts), full), ph, ts, stage, stage, s.p.ring(ax, d)).start()
    def got(s, ph, ts, k):
        r = s.W.at[ph]
        ref = (lambda: r.at[0, 0, 0:3, 0, 0, 0], lambda: r.at[0, 0, 0:3, :, :, 0], lambda: r.at[0, 0, :, :, :, 0],
               lambda: r.at[0, 0, :, :, :, 0], lambda: r.at[0, 0, :, :, :, 0], lambda: r.at[:, :, :, :, :, 0])[k]()
        wait(ref, s.rsem.at[ph * 3 + ts, k])
    def s3(s, ph, ts, what):
        a = s.order(ph, ts); full = a[:2]; ax = a[2]; tt = s.t(ts)
        R, L = s.p.ring(ax, 1), s.p.ring(ax, 3)
        reg = lambda d: s.region(ph, tt, full, {ax: s.p.coord(ax, d)})
        if what == 'own':
            s.cp(reg(0), ph, ts, 2, 2, R).start()
            s.cp(reg(0), ph, ts, 2, 3, L).start()
        elif what == 'fwdR': s.cp(s.half(reg(-1), full, 0), ph, ts, 2, 4, R).start()
        else: s.cp(s.half(reg(1), full, 1), ph, ts, 2, 4, L).start()
    def sib(s, ph, ts, piece):
        a = s.order(ph, ts); full = a[:2]; ax = a[2]
        d = (0, -1, 1, 2)[piece]
        s.cp(s.region(ph, s.t(ts), full, {ax: s.p.coord(ax, d)}), ph, ts, 3, 5, s.p.sibling).start()
    def go(s, ts, f, other=False):
        def h():
            f()
        if ts < 2: h()
        else: pl.when(s.p.c == (1 if other else 0))(h)
    def each(s, f, other=False):
        for ts in range(3): s.go(ts, lambda ts=ts: f(ts), other)
    def phase_a(s, ph):
        s.each(lambda ts: s.direct(0, ph, ts))
    def phase_b(s, ph):
        s.each(lambda ts: (s.got(ph, ts, 0), s.direct(1, ph, ts)))
    def phase_c(s, ph):
        s.each(lambda ts: (s.got(ph, ts, 1), s.s3(ph, ts, 'own'), s.sib(ph, ts, 0)))
    def phase_d(s, ph):
        s.each(lambda ts: (s.got(ph, ts, 2), s.s3(ph, ts, 'fwdR'), s.sib(ph, ts, 1), s.got(ph, ts, 3), s.s3(ph, ts, 'fwdL'), s.sib(ph, ts, 2)))
    def phase_e(s, ph):
        s.each(lambda ts: (s.got(ph, ts, 4), s.sib(ph, ts, 3)))
    def phase_f(s, ph):
        s.each(lambda ts: s.got(ph, ts, 5), other=True)
    def drain(s):
        W = s.W
        for ts, t in ((0, slice(0, 2)), (2, 0)):
            def w(ts=ts, t=t):
                k = 4 if ts == 2 else 0
                wait(W.at[:, 0, 0, 0:3, 0, 0, t], s.ssem.at[k])
                wait(W.at[:, 0, 0, 0:3, :, :, t], s.ssem.at[k + 1])
                wait(W.at[:, :, :, 0:3, :, :, t], s.ssem.at[k + 2])
                wait(W.at[:, :, :, :, :, :, t], s.ssem.at[k + 3])
            if ts == 0: w()
            else: pl.when(s.p.c == 0)(w)
        o = s.s0_src()
        for tc in (0, 1):
            cond = (o <= 4) if tc == 0 else (o >= 4)
            pl.when(cond)(lambda tc=tc: wait(s.pieces.at[:, 0:3], s.s0s.at[tc]))
            pl.when(jnp.logical_and(cond, s.p.c != tc))(lambda: wait(s.pieces.at[:, 0], s.s0s.at[2]))

def barrier(partners):
    b = pltpu.get_barrier_semaphore()
    for d in partners:
        pl.semaphore_signal(b, inc=1, device_id=d, device_id_type=MESH)
    pl.semaphore_wait(b, len(partners))

def fill_pieces(pieces, wqkv, wout, wup, wdown):
    mats = [(wqkv, 0), (wqkv, 1280), (wqkv, 2560), (wout, 0), (wup, 0), (wdown, 0)]
    for ph in range(3):
        for xh in range(2):
            r, off = mats[2 * ph + xh]
            for par in range(2):
                v = r[:, off + par * 640: off + (par + 1) * 640]
                pieces[ph, 2 * xh + par] = jnp.concatenate([v.astype(jnp.float32), jnp.zeros((6, 640), jnp.float32)], axis=0).astype(jnp.bfloat16)


def dot(a, b):
    return jnp.dot(a, b, preferred_element_type=F32)


def dot_nt(a, b):
    return lax.dot_general(a, b, (((1,), (1,)), ((), ())), preferred_element_type=F32)


def dot_tn(a, b):
    return lax.dot_general(a, b, (((0,), (0,)), ((), ())), preferred_element_type=F32)


def at128(v):
    return pl.multiple_of(v, 128)


def window(z, xl):
    return 320 * z - 64 * ((z & 1)) + 128 * xl


class Spread:
    def __init__(s, p, T, R0, R1, R2, T3, R3, out, ssem, rsem):
        s.p, s.T, s.T3, s.out, s.ssem, s.rsem = p, T, T3, out, ssem, rsem
        s.R = (R0, R1, R2, R3)

    def start(s, k):
        p = s.p
        src = s.T3 if k == 3 else s.T
        if k == 0: devs = [p.sibling]
        else: devs = [p.ring((1, 0, 2)[k - 1], d) for d in (1, 2, 3)]
        for i, dv in enumerate(devs):
            pltpu.make_async_remote_copy(src, s.R[k].at[i], s.ssem.at[k], s.rsem.at[k], device_id=dv, device_id_type=MESH).start()

    def finish(s, k):
        p = s.p
        R = s.R[k]
        wait(R, s.rsem.at[k])
        wait(R, s.ssem.at[k])
        if k < 2:
            acc = s.T[...].astype(F32)
            for i in range(R.shape[0]): acc = acc + R[i].astype(F32)
            s.T[...] = acc.astype(BF)
        elif k == 2:
            s.T3[...] = jnp.zeros((32, 384), BF)
            mine = pl.ds(at128(128 * p.xl), 256)
            other = pl.ds(at128(128 - 128 * p.xl), 256)
            s.T3[:, mine] = (s.T[...].astype(F32) + R[1].astype(F32)).astype(BF)
            s.T3[:, other] = (s.T3[:, other].astype(F32) + R[0].astype(F32) + R[2].astype(F32)).astype(BF)
        else:
            s.out[...] = jnp.zeros((32, D), BF)
            for i in range(4):
                lanes = pl.ds(at128(window(((p.z + 4 - i) & 3), 0)), 384)
                v = s.T3[...] if i == 0 else R[i - 1]
                s.out[:, lanes] = (s.out[:, lanes].astype(F32) + v.astype(F32)).astype(BF)


class Gather:
    def __init__(s, p, buf, R0, R1, S1, R2, S2, R3, R4, ssem, rsem):
        s.p, s.buf, s.R0, s.R1, s.S1, s.R2, s.S2, s.R3, s.R4 = p, buf, R0, R1, S1, R2, S2, R3, R4
        s.ssem, s.rsem = ssem, rsem
        s.active = (p.z >> 1) == p.c

    def send(s, k, src, dst, dv):
        pltpu.make_async_remote_copy(src, dst, s.ssem.at[k], s.rsem.at[k], device_id=dv, device_id_type=MESH).start()

    def start(s, k):
        p = s.p
        if k == 0:
            s.send(0, s.buf.at[1 - p.c], s.R0, p.sibling)
        elif k == 1:
            for d in (1, 2, 3):
                z = ((p.z + d) & 3)
                @pl.when((z >> 1) == p.c)
                def _(z=z, d=d):
                    s.send(1, s.buf.at[p.c, :, pl.ds(at128(256 * ((z & 1))), 384)], s.R1.at[d - 1], p.dev(z=z))
        else:
            @pl.when(s.active)
            def _():
                if k == 2:
                    s.send(2, s.S1.at[:, pl.ds(at128(128 - 128 * p.xl), 256)], s.R2, p.pair)
                elif k == 3:
                    for d in (1, 2, 3): s.send(3, s.S2, s.R3.at[d - 1], p.ring(1, d))
                else:
                    s.send(4, s.S2, s.R4, p.sibling)

    def finish(s, k):
        p = s.p
        if k == 0:
            wait(s.R0, s.rsem.at[0])
            wait(s.R0, s.ssem.at[0])
            s.buf[p.c] = s.buf[p.c] + s.R0[...]
            return
        if k == 1:
            pl.when(s.active)(lambda: wait(s.R1.at[0], s.ssem.at[1]))
            pl.when(jnp.logical_not(s.active))(lambda: wait(s.R1.at[0:2], s.ssem.at[1]))
        if k == 4:
            @pl.when(jnp.logical_not(s.active))
            def _():
                wait(s.R4, s.rsem.at[4])
                s.S2[...] = s.R4[...]
            pl.when(s.active)(lambda: wait(s.R4, s.ssem.at[4]))
            return
        @pl.when(s.active)
        def _():
            if k == 1:
                wait(s.R1, s.rsem.at[1])
                mine = pl.ds(at128(256 * ((p.z & 1))), 384)
                s.S1[...] = s.buf[p.c, :, mine] + s.R1[0] + s.R1[1] + s.R1[2]
            elif k == 2:
                wait(s.R2, s.rsem.at[2])
                wait(s.R2, s.ssem.at[2])
                s.S2[...] = s.S1[:, pl.ds(at128(128 * p.xl), 256)] + s.R2[...]
            else:
                wait(s.R3, s.rsem.at[3])
                wait(s.R3, s.ssem.at[3])
                s.S2[...] = s.S2[...] + s.R3[0] + s.R3[1] + s.R3[2]


class RS:
    def __init__(s, p, G, GW, RD, bufs, FR, EX, FIN, dss, drs, ss, rs, fs, fr):
        s.p, s.G, s.GW, s.RD, s.bufs, s.FR, s.EX, s.FIN = p, G, GW, RD, bufs, FR, EX, FIN
        s.dss, s.drs, s.ss, s.rs, s.fs, s.fr = dss, drs, ss, rs, fs, fr

    def gref(s, ph):
        return s.G[ph]

    def go(s, ts, f, other=False):
        def h():
            f()
        if ts < 2: h()
        else: pl.when(s.p.c == (1 if other else 0))(h)

    def d2d(s, ph, ts, act, par):
        p = s.p
        g = s.gref(ph)
        t = 3 * (1 - p.c) + ts if act != 'recv' else 3 * p.c + ts
        cp = pltpu.make_async_remote_copy(g.at[par, :, :, :, t], s.RD.at[ph, ts, par], s.dss.at[(ts >> 1)], s.drs.at[ph * 3 + ts, par], device_id=p.sibling, device_id_type=MESH)
        if act == 'start': cp.start()
        else: cp.wait_recv()

    def d2d_start(s, ph, par):
        for ts in range(3): s.go(ts, lambda ts=ts: s.d2d(ph, ts, 'start', par), other=True)

    def d2d_add(s, ph, ts, par):
        g = s.gref(ph)
        t = 3 * s.p.c + ts
        s.d2d(ph, ts, 'recv', par)
        def body(z, _):
            g[par, z, :, :, t] = (g[par, z, :, :, t].astype(F32) + s.RD[ph, ts, par, z].astype(F32)).astype(BF)
            return 0
        lax.fori_loop(0, 4, body, 0)

    def order(s, ph, ts):
        return ((1, 0, 2), (2, 0, 1), (0, 2, 1))[ts]

    def fidx(s, ph, ts):
        return (1, 2, 0)[ts]

    def piece(s, ph, ts, st, k):
        p = s.p
        o = s.order(ph, ts)
        ax = o[st]
        done = o[:st]
        par = h = zz = xl = slice(None)
        if 0 in done: xl = p.xl
        if 1 in done: h, par = p.h, p.par
        if 2 in done: zz = p.z
        if ax == 0: xl = k
        if ax == 1: h, par = (k >> 1), (k & 1)
        if ax == 2: zz = k
        return s.gref(ph).at[par, zz, xl, h, 3 * p.c + ts]

    def half(s, ph, ts, st, k, hf):
        p = s.p
        o = s.order(ph, ts)
        ax = o[st]
        assert st == 0
        t = 3 * p.c + ts
        if ax == 1: return s.gref(ph).at[(k & 1), pl.ds(2 * hf, 2), :, (k >> 1), t]
        return s.gref(ph).at[hf, k, :, :, t]

    def bhalf(s, ph, ts, hf):
        f = s.fidx(ph, ts)
        b = s.bufs[f][0]
        if f == 1: return b.at[ph, 2, pl.ds(2 * hf, 2)]
        return b.at[ph, 2, hf]

    def cp(s, src, dst, sk, sl, k, dev):
        return pltpu.make_async_remote_copy(src, dst, s.ss.at[sk], s.rs.at[sl, k], device_id=dev, device_id_type=MESH)

    def add(s, dst, srcs):
        lead = dst.shape[:-2]
        if len(lead) >= 1 and lead[0] > 1:
            def body(i, _):
                acc = dst[i].astype(F32)
                for r in srcs: acc = acc + r[i].astype(F32)
                dst[i] = acc.astype(BF)
                return 0
            lax.fori_loop(0, lead[0], body, 0)
        else:
            acc = dst[...].astype(F32)
            for r in srcs: acc = acc + r[...].astype(F32)
            dst[...] = acc.astype(BF)

    def ring_cps(s, ph, ts, st):
        p = s.p
        o = s.order(ph, ts)
        ax = o[st]
        f = s.fidx(ph, ts)
        sl = ph * 3 + ts
        b = s.bufs[f][st]
        sk = st + (3 if ts == 2 else 0)
        if ax == 0:
            k = 1 - p.xl
            src, dv = s.piece(ph, ts, st, k), p.pair
            if st == 0: return [s.cp(src.at[par], b.at[ph, 0, par], sk, sl, par, dv) for par in range(2)]
            return [s.cp(src, b.at[ph, 0], sk, sl, 2 + st, dv)]
        res = []
        for i, d in enumerate((1, 3, 2)):
            res.append(s.cp(s.piece(ph, ts, st, p.coord(ax, d)), b.at[ph, i], sk, sl, 2 + st, p.ring(ax, d)))
        return res

    def first_a(s, ph, ts, par):
        ax = s.order(ph, ts)[0]
        if ax == 0:
            s.ring_cps(ph, ts, 0)[par].start()
        elif ax == 2:
            s.sf_half(ph, ts)[1 - par].start()
        else:
            @pl.when(s.p.par == par)
            def _():
                for c in s.sf_half(ph, ts): c.start()

    def sf_half(s, ph, ts):
        p = s.p
        ax = s.order(ph, ts)[0]
        sl = ph * 3 + ts
        k = p.coord(ax, 2)
        return [s.cp(s.half(ph, ts, 0, k, 1), s.bhalf(ph, ts, 1), 0, sl, 0, p.ring(ax, 1)),
                s.cp(s.half(ph, ts, 0, k, 0), s.bhalf(ph, ts, 0), 0, sl, 1, p.ring(ax, 3))]

    def sf_full(s, ph, ts):
        p = s.p
        ax = s.order(ph, ts)[0]
        sl = ph * 3 + ts
        b = s.bufs[s.fidx(ph, ts)][0]
        return [s.cp(s.piece(ph, ts, 0, p.coord(ax, 1)), b.at[ph, 0], 0, sl, 2, p.ring(ax, 1)),
                s.cp(s.piece(ph, ts, 0, p.coord(ax, 3)), b.at[ph, 1], 0, sl, 2, p.ring(ax, 3))]

    def first_b(s, ph, ts):
        p = s.p
        o = s.order(ph, ts)
        ax = o[0]
        if ax == 0: return
        hb = s.sf_half(ph, ts)
        full = s.sf_full(ph, ts)
        hb[0].wait_recv()
        s.add(s.half(ph, ts, 0, p.coord(ax, 1), 1), [s.bhalf(ph, ts, 1)])
        full[0].start()
        hb[1].wait_recv()
        s.add(s.half(ph, ts, 0, p.coord(ax, 3), 0), [s.bhalf(ph, ts, 0)])
        full[1].start()

    def first_c(s, ph, ts):
        p = s.p
        o = s.order(ph, ts)
        ax = o[0]
        me = (p.xl, p.y, p.z)[ax]
        b = s.bufs[s.fidx(ph, ts)][0]
        if ax == 0:
            for par, c in enumerate(s.ring_cps(ph, ts, 0)):
                c.wait_recv()
                s.add(s.piece(ph, ts, 0, me).at[par], [b.at[ph, 0, par]])
            return
        wait(b.at[ph, 0:2], s.rs.at[ph * 3 + ts, 2])
        s.add(s.piece(ph, ts, 0, me), [b.at[ph, i] for i in range(2)])

    def next_start(s, ph, ts, st):
        for c in s.ring_cps(ph, ts, st): c.start()

    def next_finish(s, ph, ts, st):
        p = s.p
        ax = s.order(ph, ts)[st]
        me = (p.xl, p.y, p.z)[ax]
        b = s.bufs[s.fidx(ph, ts)][st]
        wait(b.at[ph], s.rs.at[ph * 3 + ts, 2 + st])
        s.add(s.piece(ph, ts, st, me), [b.at[ph, i] for i in range(1 if ax == 0 else 3)])

    def each(s, f):
        for ts in range(3): s.go(ts, lambda ts=ts: f(ts))

    def first(s, ph, par):
        s.each(lambda ts: (s.d2d_add(ph, ts, par), s.first_a(ph, ts, par)))

    def step(s, ph, k):
        if k == 2: s.each(lambda ts: s.first_b(ph, ts))
        elif k == 3: s.each(lambda ts: (s.first_c(ph, ts), s.next_start(ph, ts, 1)))
        elif k == 4: s.each(lambda ts: (s.next_finish(ph, ts, 1), s.next_start(ph, ts, 2)))
        elif k == 5:
            s.each(lambda ts: s.next_finish(ph, ts, 2))
            s.final_start(ph)

    def fin_cps(s, ph, k):
        p = s.p
        o = 4 * p.c + k
        chunk = 2 * p.xh + p.par
        dev = p.dev(x=((o & 1)) * 2 + p.xl, y=2 * p.h + (o >> 2), c=(((o >> 1)) & 1))
        return pltpu.make_async_remote_copy(s.EX.at[ph, k], s.FIN.at[ph, chunk, p.c], s.fs.at[0], s.fr.at[ph, p.c], device_id=dev, device_id_type=MESH)

    def myo(s):
        p = s.p
        return (p.par * 2 + p.c) * 2 + p.xh

    def final_start(s, ph):
        p = s.p
        g = s.gref(ph)
        def put(ts):
            s.FR[ts] = g[p.par, p.z, p.xl, p.h, 3 * p.c + ts]
        put(0); put(1)
        pl.when(p.c == 0)(lambda: put(2))
        i = lax.broadcasted_iota(jnp.int32, (80, 48), 1)
        k = lax.broadcasted_iota(jnp.int32, (80, 48), 0)
        r = 48 * p.c + i
        q = (r * 205) >> 11
        col = (q - 4 * p.c) * 16 + (r - q * 10)
        pt = jnp.where(k == col, 1.0, 0.0).astype(BF)
        s.EX[ph] = dot(pt, s.FR[...].reshape(48, CW)).astype(BF).reshape(5, 16, CW)
        for k in range(5):
            def send(k=k):
                me = 4 * p.c + k == s.myo()
                @pl.when(me)
                def _():
                    s.FIN[ph, 2 * p.xh + p.par, p.c] = s.EX[ph, k]
                @pl.when(jnp.logical_not(me))
                def _():
                    s.fin_cps(ph, k).start()
            if k < 4: send()
            else: pl.when(p.c == 0)(send)

    def final_wait(s, ph):
        p = s.p
        o = s.myo()
        for sc in range(2):
            used = (o <= 4) if sc == 0 else (o >= 4)
            pl.when(jnp.logical_and(used, p.c == sc))(lambda: wait(s.FIN.at[ph, 0:3, 0], s.fr.at[ph, sc]))
            pl.when(jnp.logical_and(used, p.c != sc))(lambda: wait(s.FIN.at[ph, :, 0], s.fr.at[ph, sc]))

    def drain(s):
        p = s.p
        G = s.GW
        wait(G.at[:, :, :, :, :, 0:2], s.dss.at[0])
        pl.when(p.c == 1)(lambda: wait(G.at[:, :, :, :, :, 0], s.dss.at[1]))
        wait(G.at[:, :, 0:3, :, :, 0:2], s.ss.at[0])
        wait(G.at[:, 0, :, 0, 0, 0:2], s.ss.at[1])
        wait(G.at[:, 0, 0:3, 0, 0, 0:2], s.ss.at[2])
        @pl.when(p.c == 0)
        def _():
            wait(G.at[:, :, :, :, 0, 0], s.ss.at[3])
            wait(G.at[:, 0, 0:3, :, :, 0], s.ss.at[4])
            wait(G.at[:, 0, 0:3, 0, 0, 0], s.ss.at[5])
        o = s.myo()
        n = jnp.where(p.c == 0, jnp.where(o <= 4, 4, 5), jnp.where(o >= 4, 3, 4))
        for k in (3, 4, 5):
            pl.when(n == k)(lambda k=k: wait(s.EX.at[:, 0:k], s.fs.at[0]))


def clear_last(stg, FR):
    stg[:, 4] = jnp.zeros((3, 16, CW), BF)
    FR[2] = jnp.zeros((16, CW), BF)


FIRST, Q, K, V, MIXED, SECOND, ACTIVE, GU, GAO, GMX, GQ, GK, GV = range(13)
RB = 32
UNROLL = 4


def block_kernel(lat_in, cot_in, sid, *refs):
    small_in, (o_lat, o_in), small_out = refs[0:8], refs[8:10], refs[10:16]
    block_body(lat_in, cot_in, sid, small_in, o_lat, o_in, small_out, *refs[16:])


def block_body(lat_in, cot_in, sid, small_in, o_lat, o_in, small_out,
                 W, stg, pieces, A, N1, N2, MID, DG, PR, I1, I2, VEC, CS, GW, RD, b00, b01, b02, b10, b11, b12, b20, b21, b22,
                 FR, EX, FIN, SB, SBT, SB0, SB1, SB2, SBT3, SB3, SG, SG0, SG1, SGS1, SG2, SGS2, SG3, SG4,
                 lat, cot, gt, b1, g2, b2, wq, wo, wu, wd, o_tab, o_vec, o_qkv, o_out, o_up, o_down, ssem, rsem, s0s, s0r, dss, drs, gss, grs, fs, fr, sbs, sbr, sgs, sgr, io):
    p = Pos()
    ag = AG(p, W, stg, pieces, ssem, rsem, None, s0s, s0r)
    G = [GW.at[0], GW.at[1], GW.at[2]]
    rs = RS(p, G, GW, RD, [[b00, b01, b02], [b10, b11, b12], [b20, b21, b22]], FR, EX, FIN, dss, drs, gss, grs, fs, fr)
    sb = Spread(p, SBT, SB0, SB1, SB2, SBT3, SB3, SB, sbs, sbr)
    sg = Gather(p, SG, SG0, SG1, SGS1, SG2, SGS2, SG3, SG4, sgs, sgr)
    idx = lax.axis_index("dp") * 2 + p.xh

    parts = ag.partners()
    bar = pltpu.get_barrier_semaphore()
    for d in parts:
        pl.semaphore_signal(bar, inc=1, device_id=d, device_id_type=MESH)
    in_lat = pltpu.make_async_copy(lat_in, lat, io.at[0])
    in_cot = pltpu.make_async_copy(cot_in, cot, io.at[1])
    ins = [pltpu.make_async_copy(a, v, io.at[4 + i]) for i, (a, v) in enumerate(zip(small_in, (gt, b1, g2, b2, wq, wo, wu, wd)))]
    for c in ins: c.start()
    in_lat.start(); in_cot.start()
    for c in ins: c.wait()
    fill_pieces(pieces, wq, wo, wu, wd)
    pl.when(p.c == 1)(lambda: clear_last(stg, FR))
    j = lax.broadcasted_iota(jnp.int32, (16, 256), 0)
    lane = lax.broadcasted_iota(jnp.int32, (16, 256), 1) + window(p.z, p.xl)
    own = jnp.where(jnp.logical_and(lane == idx * 10 + j, j < 10), 1.0, 0.0)
    own16 = own[0:10].astype(BF)
    spread = [dot_tn(gt[...], own16)] + [dot(jnp.broadcast_to(b[...].reshape(1, 10), (8, 10)), own16)[0:1] for b in (b1, g2, b2)] + [jnp.zeros((13, 256), F32)]
    SBT[...] = jnp.concatenate(spread, axis=0).astype(BF)
    pl.semaphore_wait(bar, len(parts))

    sb.start(0)
    for ph in range(3): ag.s0(ph)

    def ln1(r, _):
        rows = pl.ds(pl.multiple_of(r * RB, RB), RB)
        x = lat[rows, :].astype(F32)
        mu = jnp.mean(x, axis=-1, keepdims=True)
        xc = x - mu
        inv = lax.rsqrt(jnp.mean(xc * xc, axis=-1, keepdims=True) + EPS)
        N1[rows, :] = xc * inv
        I1[rows, :] = jnp.broadcast_to(inv, (RB, 128))
        return 0
    in_lat.wait(); in_cot.wait()
    lax.fori_loop(0, L // RB, ln1, 0, unroll=UNROLL)
    ag.s0_recv(0); ag.compact(0); ag.phase_a(0)
    sb.finish(0); sb.start(1)
    ag.s0_recv(1); ag.compact(1); ag.phase_a(1)
    ag.phase_b(0)
    sb.finish(1); sb.start(2)
    ag.s0_recv(2); ag.compact(2); ag.phase_a(2)
    ag.phase_b(1)
    ag.phase_c(0)
    sb.finish(2); sb.start(3)
    ag.phase_b(2)
    ag.phase_c(1)
    A[MIXED] = jnp.zeros((L, D), BF)
    for k in (GQ, GK, GV): A[k] = jnp.zeros((L, D), BF)
    CS[...] = jnp.zeros_like(CS)
    ag.phase_d(0)
    ag.phase_c(2)
    sb.finish(3)
    lane32 = lax.broadcasted_iota(jnp.int32, (8, 32), 1)
    sub8 = lax.broadcasted_iota(jnp.int32, (8, 32), 0)
    script = jnp.broadcast_to(sid[...].reshape(1, 1), (1, 640))
    tgt = jnp.where(sub8 == 0, script[:, 0:32], jnp.where(sub8 < 4, 15 + sub8, -1))
    pick = jnp.where(lane32 == tgt, 1.0, 0.0).astype(BF)
    VEC[...] = dot(pick, SB[...])

    def mk_first(r, _):
        rows = pl.ds(pl.multiple_of(r * RB, RB), RB)
        A[FIRST, rows, :] = (N1[rows, :] * VEC[0:1, :] + VEC[1:2, :]).astype(BF)
        return 0
    lax.fori_loop(0, L // RB, mk_first, 0, unroll=UNROLL)
    ag.phase_d(1)
    ag.phase_e(0)
    ag.phase_f(0)

    def wpan(ph, xh, par): return W[ph, xh, par].reshape(D, CW)
    def cols(par): return pl.ds(par * CW, CW)

    for par in range(2):
        A[Q, :, cols(par)] = dot(A[FIRST], wpan(0, 0, par)).astype(BF)
    ag.phase_d(2)
    for par in range(2):
        A[K, :, cols(par)] = dot(A[FIRST], wpan(0, 1, par)).astype(BF)
    ag.phase_e(1)
    ag.phase_f(1)
    for par in range(2):
        A[V, :, cols(par)] = dot(A[FIRST], wpan(1, 0, par)).astype(BF)

    lane256 = lax.broadcasted_iota(jnp.int32, (1, 256), 1)
    def masks(w):
        m = jnp.where(jnp.logical_and(lane256 >= 32 * w, lane256 < 32 * w + HD), 1.0, 0.0)
        return m, m.astype(BF)
    def win(pn, w):
        return pl.ds(pl.multiple_of(pn * CW + w * 128, 128), 256)

    for pn in range(2):
        def att(w, _, pn=pn):
            cw = win(pn, w)
            m32, m16 = masks(w)
            sc = dot_nt(A[Q, :, cw] * m16, A[K, :, cw]) * SCALE
            e = jnp.exp(sc - jnp.max(sc, axis=-1, keepdims=True))
            pr = e * (1.0 / jnp.sum(e, axis=-1, keepdims=True))
            PR[pn * 4 + w] = pr
            mx = dot(pr.astype(BF), A[V, :, cw]) * m32
            A[MIXED, :, cw] = A[MIXED, :, cw] + mx.astype(BF)
            return 0
        lax.fori_loop(0, 4, att, 0, unroll=True)
    ag.phase_e(2)
    for par in range(2):
        MID[:, cols(par)] = lat[:, cols(par)].astype(F32) + dot(A[MIXED], wpan(1, 1, par))

    def ln2(r, _):
        rows = pl.ds(pl.multiple_of(r * RB, RB), RB)
        x = MID[rows, :]
        mu = jnp.mean(x, axis=-1, keepdims=True)
        xc = x - mu
        inv = lax.rsqrt(jnp.mean(xc * xc, axis=-1, keepdims=True) + EPS)
        n = xc * inv
        N2[rows, :] = n
        I2[rows, :] = jnp.broadcast_to(inv, (RB, 128))
        A[SECOND, rows, :] = (n * VEC[2:3, :] + VEC[3:4, :]).astype(BF)
        return 0
    lax.fori_loop(0, L // RB, ln2, 0, unroll=UNROLL)
    ag.phase_f(2)
    for par in range(2):
        DG[:, cols(par)] = dot(A[SECOND], wpan(2, 0, par))

    def gelu(r, _):
        rows = pl.ds(pl.multiple_of(r * RB, RB), RB)
        u = DG[rows, :]
        c0 = math.sqrt(2.0 / math.pi)
        u2 = u * u
        th = jnp.tanh(c0 * (u + 0.044715 * u2 * u))
        hp = 0.5 * (1.0 + th)
        A[ACTIVE, rows, :] = (u * hp).astype(BF)
        DG[rows, :] = hp + 0.5 * u * (1.0 - th * th) * (c0 * (1.0 + 3 * 0.044715 * u2))
        return 0
    lax.fori_loop(0, L // RB, gelu, 0, unroll=UNROLL)

    def back(src, ph, xh, n):
        acc = None
        for par in range(2):
            t = dot_nt(src(par), W[ph, xh, par, 2 * n:2 * n + 2].reshape(CW, CW))
            acc = t if acc is None else acc + t
        return acc

    half = pl.ds(pl.multiple_of(p.xh * CW, 128), CW)

    def wgrad(ph, par, left, right):
        for n in range(2):
            v = dot_tn(A[left, :, cols(n)], right[:, half])
            G[ph][par, 2 * n:2 * n + 2] = v.astype(BF).reshape(2, 2, 2, 5, 16, CW)
        rs.d2d_start(ph, par)

    wgrad(2, 1, ACTIVE, cot)
    for n in range(2):
        A[GU, :, cols(n)] = (back(lambda par: cot[:, cols(par)], 2, 1, n) * DG[:, cols(n)]).astype(BF)
    wgrad(2, 0, SECOND, A.at[GU])
    for n in range(2):
        DG[:, cols(n)] = back(lambda par: A[GU, :, cols(par)], 2, 0, n)

    rs.first(2, 1)

    def ln2b(r, _):
        rows = pl.ds(pl.multiple_of(r * RB, RB), RB)
        gs = DG[rows, :]
        n = N2[rows, :]
        CS[1] += jnp.sum((gs * n).reshape(RB // 8, 8, D), axis=0)
        CS[2] += jnp.sum(gs.reshape(RB // 8, 8, D), axis=0)
        dn = gs * VEC[2:3, :]
        m1 = jnp.mean(dn, axis=-1, keepdims=True)
        m2 = jnp.mean(dn * n, axis=-1, keepdims=True)
        gm = cot[rows, :].astype(F32) + I2[rows, 0:1] * (dn - m1 - n * m2)
        N2[rows, :] = gm
        A[GAO, rows, :] = gm.astype(BF)
        return 0
    lax.fori_loop(0, L // RB, ln2b, 0, unroll=UNROLL)
    wgrad(1, 1, MIXED, A.at[GAO])
    for n in range(2):
        A[GMX, :, cols(n)] = back(lambda par: A[GAO, :, cols(par)], 1, 1, n).astype(BF)
        if n == 0: rs.first(2, 0)

    for i in range(2):
        pn = p.xh if i == 0 else 1 - p.xh
        def attb(w, _, pn=pn):
            cw = win(pn, w)
            m32, m16 = masks(w)
            gm = A[GMX, :, cw] * m16
            qm = A[Q, :, cw] * m16
            pr = PR[pn * 4 + w]
            gp = dot_nt(gm, A[V, :, cw])
            rt = jnp.sum(gp * pr, axis=-1, keepdims=True)
            gsc = (pr * (gp - rt)).astype(BF)
            A[GV, :, cw] = A[GV, :, cw] + dot_tn(pr.astype(BF), gm).astype(BF)
            A[GQ, :, cw] = A[GQ, :, cw] + (dot(gsc, A[K, :, cw]) * SCALE * m32).astype(BF)
            A[GK, :, cw] = A[GK, :, cw] + (dot_tn(gsc, qm) * SCALE).astype(BF)
            return 0
        lax.fori_loop(0, 2, attb, 0, unroll=True)
        if i == 0:
            rs.first(1, 1)
            rs.step(2, 2)
        else:
            rs.first(1, 0)
            rs.first(0, 0)
            rs.first(0, 1)
            rs.step(2, 3)
        lax.fori_loop(2, 4, attb, 0, unroll=True)
        if i == 0:
            wgrad(1, 0, FIRST, A.at[GV])
            wgrad(0, 0, FIRST, A.at[GQ])
            wgrad(0, 1, FIRST, A.at[GK])
    rs.step(1, 2)
    rs.step(0, 2)
    for n in range(2):
        acc = None
        for g, (ph, xh) in ((GQ, (0, 0)), (GK, (0, 1)), (GV, (1, 0))):
            t = back(lambda par: A[g, :, cols(par)], ph, xh, n)
            acc = t if acc is None else acc + t
        DG[:, cols(n)] = acc
    rs.step(2, 4)

    def ln1b(r, _):
        rows = pl.ds(pl.multiple_of(r * RB, RB), RB)
        gf = DG[rows, :]
        n = N1[rows, :]
        CS[3] += jnp.sum((gf * n).reshape(RB // 8, 8, D), axis=0)
        CS[0] += jnp.sum(gf.reshape(RB // 8, 8, D), axis=0)
        dn = gf * VEC[0:1, :]
        m1 = jnp.mean(dn, axis=-1, keepdims=True)
        m2 = jnp.mean(dn * n, axis=-1, keepdims=True)
        DG[rows, :] = N2[rows, :] + I1[rows, 0:1] * (dn - m1 - n * m2)
        return 0
    lax.fori_loop(0, L // RB, ln1b, 0, unroll=UNROLL)
    out_in = pltpu.make_async_copy(DG, o_in, io.at[3])
    out_in.start()
    sub24 = lax.broadcasted_iota(jnp.int32, (24, 640), 0)
    for k in range(2):
        v = [jnp.sum(CS[i, :, k * 640:(k + 1) * 640], axis=0, keepdims=True) for i in range(4)]
        SG[k] = (jnp.where(sub24 == script, v[3], 0.0) + jnp.where(sub24 == 16, v[0], 0.0)
                 + jnp.where(sub24 == 17, v[1], 0.0) + jnp.where(sub24 == 18, v[2], 0.0))
    sg.start(0)
    rs.step(1, 3)
    rs.step(0, 3)
    for par in range(2):
        A[SECOND, :, cols(par)] = (MID[:, cols(par)] + dot(A[ACTIVE], wpan(2, 1, par))).astype(BF)
    out_lat = pltpu.make_async_copy(A.at[SECOND], o_lat, io.at[2])
    out_lat.start()
    sg.finish(0); sg.start(1)
    rs.step(2, 5)
    rs.step(1, 4)
    rs.step(0, 4)
    sg.finish(1); sg.start(2)
    ag.drain()
    rs.step(1, 5)
    rs.step(0, 5)
    sg.finish(2); sg.start(3)

    outs = [(o_qkv, 0), (o_qkv, 1280), (o_qkv, 2560), (o_out, 0), (o_up, 0), (o_down, 0)]
    def emit(ph):
        rs.final_wait(ph)
        o_id = rs.myo()
        sel = jnp.where(o_id > 4, 1, 0)
        @pl.when(o_id == 4)
        def _():
            FIN[ph, :, 0] = FIN[ph, :, 0] + FIN[ph, :, 1]
        for xh in range(2):
            for par in range(2):
                o, off = outs[2 * ph + par]
                v = FIN[ph, 2 * xh + par, sel].astype(F32)
                o[:, off + xh * 640: off + (xh + 1) * 640] = v[0:10]
    emit(2)
    sg.finish(3); sg.start(4)
    emit(1)
    sg.finish(4)
    hi = lax.Precision.HIGHEST
    tab = lax.dot_general(own, SGS2[...], (((1,), (1,)), ((), ())), precision=hi, preferred_element_type=F32)
    vec = lax.dot_general(SGS2[16:24], own, (((1,), (1,)), ((), ())), precision=hi, preferred_element_type=F32)
    o_tab[...] = tab[0:10, 0:16]
    o_vec[...] = vec[:, 0:10]
    emit(0)
    outs = [pltpu.make_async_copy(v, o, io.at[4 + i]) for i, (v, o) in enumerate(zip((o_tab, o_vec, o_qkv, o_out, o_up, o_down), small_out))]
    for c in outs: c.start()
    rs.drain()
    out_lat.wait(); out_in.wait()
    for c in outs: c.wait()


def results_kernel(lat, inp, tab, vec, qkv, out, up, down, o_lat, o_in, o_tab, o_b1, o_g2, o_b2, o_qkv, o_out, o_up, o_down,
                   v_lat, v_in, v_tab, v_vec, v_qkv, v_out, v_up, v_down, v_b1, v_g2, v_b2, sem):
    first = pltpu.make_async_copy(vec, v_vec, sem.at[0])
    first.start()
    moves = []
    for a, v, o, n in ((inp, v_in, o_in, 4), (lat, v_lat, o_lat, 2), (qkv, v_qkv, o_qkv, 1), (out, v_out, o_out, 1), (up, v_up, o_up, 1), (down, v_down, o_down, 1), (tab, v_tab, o_tab, 1)):
        for k in range(n):
            c = a.shape[0] // n
            cut = (lambda r: r.at[pl.ds(k * c, c)]) if n > 1 else (lambda r: r)
            i = 2 + 2 * len(moves)
            moves.append((pltpu.make_async_copy(cut(a), cut(v), sem.at[i]), pltpu.make_async_copy(cut(v), cut(o), sem.at[i + 1])))
    for a, _ in moves: a.start()
    first.wait()
    small = []
    for i, (v, o) in enumerate(((v_b1, o_b1), (v_g2, o_g2), (v_b2, o_b2))):
        v[...] = v_vec[i]
        small.append(pltpu.make_async_copy(v, o, sem.at[24 + i]))
        small[-1].start()
    for a, b in moves:
        a.wait()
        b.start()
    for _, b in moves: b.wait()
    for c in small: c.wait()


def per_device(latents, script_ids, gain_table, bias_one, w_qkv, w_out, gain_two, bias_two, w_up, w_down, cotangent):
    V_ = pltpu.VMEM
    dma = pltpu.SemaphoreType.DMA
    blk = (16, CW)
    scratch = [
        V_((3, 2, 2, 4, 2, 2, 5, 16, CW), BF), V_((3, 5) + blk, BF), V_((3, 4) + blk, BF),
        V_((13, L, D), BF), V_((L, D), F32), V_((L, D), F32), V_((L, D), F32), V_((L, D), F32),
        V_((8, 256, 256), F32), V_((L, 128), F32), V_((L, 128), F32), V_((8, D), F32), V_((4, 8, D), F32),
        V_((3, 2, 4, 2, 2, 5) + blk, BF), V_((3, 3, 2, 4, 2, 2) + blk, BF),
        V_((3, 1, 2, 4, 2) + blk, BF), V_((3, 3, 2, 2) + blk, BF), V_((3, 3) + blk, BF),
        V_((3, 3, 4, 2) + blk, BF), V_((3, 1, 4) + blk, BF), V_((3, 3) + blk, BF),
        V_((3, 3, 2, 2, 2) + blk, BF), V_((3, 1, 2, 2) + blk, BF), V_((3, 3) + blk, BF),
        V_((3,) + blk, BF), V_((3, 5) + blk, BF), V_((3, 4, 2) + blk, BF),
        V_((32, D), BF), V_((32, 256), BF), V_((1, 32, 256), BF), V_((3, 32, 256), BF), V_((3, 32, 256), BF), V_((32, 384), BF), V_((3, 32, 384), BF),
        V_((2, 24, 640), F32), V_((24, 640), F32), V_((3, 24, 384), F32), V_((24, 384), F32), V_((24, 256), F32), V_((24, 256), F32), V_((3, 24, 256), F32), V_((24, 256), F32), V_((L, D), BF), V_((L, D), BF),
        V_((10, 16), BF), V_((10,), BF), V_((10,), BF), V_((10,), BF), V_((10, 3 * D), BF), V_((10, D), BF), V_((10, D), BF), V_((10, D), BF),
        V_((10, 16), F32), V_((8, 10), F32), V_((10, 3 * D), F32), V_((10, D), F32), V_((10, D), F32), V_((10, D), F32),
        dma((8,)), dma((9, 6)), dma((3,)), dma((3,)),
        dma((2,)), dma((9, 2)), dma((6,)), dma((9, 5)), dma((1,)), dma((3, 2)),
        dma((4,)), dma((4,)), dma((5,)), dma((5,)), dma((12,)),
    ]
    hbm = pl.BlockSpec(memory_space=pl.ANY)
    f32 = lambda *d: jax.ShapeDtypeStruct(d, F32)
    res = pl.pallas_call(
        block_kernel,
        out_shape=[jax.ShapeDtypeStruct((L, D), BF), f32(L, D), f32(10, 16), f32(8, 10), f32(10, 3 * D), f32(10, D), f32(10, D), f32(10, D)],
        in_specs=[hbm, hbm, pl.BlockSpec(memory_space=pltpu.VMEM)] + [hbm] * 8,
        out_specs=[hbm] * 8,
        scratch_shapes=scratch,
        compiler_params=pltpu.CompilerParams(collective_id=0, has_side_effects=True, vmem_limit_bytes=62 * 2**20),
        name="block",
    )(latents.reshape(L, D), cotangent.reshape(L, D), script_ids, gain_table, bias_one, gain_two, bias_two, w_qkv, w_out, w_up, w_down)
    o_lat, o_in, o_tab, o_b1, o_g2, o_b2, o_qkv, o_out, o_up, o_down = pl.pallas_call(
        results_kernel,
        out_shape=[jax.ShapeDtypeStruct((L, D), BF), f32(L, D), f32(10, 16), f32(10), f32(10), f32(10), f32(10, 3 * D), f32(10, D), f32(10, D), f32(10, D)],
        in_specs=[hbm] * 8,
        out_specs=[hbm] * 10,
        scratch_shapes=[V_((L, D), BF), V_((L, D), F32), V_((10, 16), F32), V_((8, 10), F32), V_((10, 3 * D), F32), V_((10, D), F32), V_((10, D), F32), V_((10, D), F32),
                        V_((10,), F32), V_((10,), F32), V_((10,), F32), dma((27,))],
        compiler_params=pltpu.CompilerParams(vmem_limit_bytes=62 * 2**20),
        name="results",
    )(*res)
    return (o_lat.reshape(1, L, D), o_in.reshape(1, L, D), o_tab, o_b1, o_qkv, o_out, o_g2, o_b2, o_up, o_down)


def solution(mesh):
    row = P(("dp", "fsdp"), None)
    vec = P(("dp", "fsdp"))
    item = P("dp", None, None)
    return jax.shard_map(
        per_device,
        mesh=mesh,
        in_specs=(item, P("dp"), row, vec, row, row, vec, vec, row, row, item),
        out_specs=(item, item, row, vec, row, row, vec, vec, row, row),
        check_vma=False,
    )
```

```python
import math

import jax
import jax.numpy as jnp
from jax import lax
from jax.experimental import pallas as pl
from jax.experimental.pallas import tpu as pltpu
from jax.sharding import PartitionSpec as P

HEADS = 8
HD = 160
D = 1280
L = 256
EPS = 1e-5
SCALE = 1.0 / math.sqrt(HD)
BF = jnp.bfloat16
F32 = jnp.float32

MESH = pl.DeviceIdType.MESH
CW = 640

class Pos:
    def __init__(s):
        dp = lax.axis_index("dp"); s.xh = lax.axis_index("fsdp")
        s.c = (dp & 1); s.y = (((dp >> 1)) & 3); s.xl = ((dp >> 3) & 1); s.z = dp >> 4
        s.x = s.xh * 2 + s.xl; s.h = (s.y >> 1); s.par = (s.y & 1)
        s.coords = [[(v + d) & 3 if d else v for d in range(4)] for v in (s.x, s.y, s.z)]
        s.rings = [[s.dev(**{n: s.coords[ax][d]}) for d in range(4)] for ax, n in enumerate('xyz')]
        s.sibling = s.dev(c=1 - s.c)
        s.pair = s.dev(x=s.xh * 2 + 1 - s.xl)
    def dev(s, x=None, y=None, z=None, c=None):
        x = s.x if x is None else x; y = s.y if y is None else y
        z = s.z if z is None else z; c = s.c if c is None else c
        return (((z * 2 + (x & 1)) * 4 + y) * 2 + c, (x >> 1))
    def ring(s, ax, d):
        return s.rings[ax][d & 3]
    def coord(s, ax, d):
        return s.coords[ax][d & 3]

def wait(ref, sem):
    pltpu.make_async_copy(ref, ref, sem).wait()

class AG:
    def __init__(s, p, W, stg, pieces, ssem, rsem, sib_r, s0s, s0r):
        s.p, s.W, s.stg, s.pieces = p, W, stg, pieces
        s.ssem, s.rsem, s.s0s, s.s0r = ssem, rsem, s0s, s0r
    def partners(s):
        p = s.p
        out = []
        for ax in range(3):
            for d in (1, 2, 3): out.append(p.ring(ax, d))
        for dy in (0, 1):
            for dx in (0, 1):
                for dc in (0, 1):
                    if (dy, dx, dc) == (0, 0, 0): continue
                    if (dy, dx, dc) == (0, 1, 0): continue
                    y = p.y ^ dy if dy else p.y
                    x = ((p.x + 2 * dx) & 3)
                    out.append(p.dev(x=x, y=y, c=((p.c + dc) & 1)))
        return out
    def s0_targets(s):
        p = s.p
        res = []
        for dy in (1, 0):
            for dx in (1, 0):
                y = p.y ^ dy if dy else p.y
                x = ((p.x + 2 * dx) & 3)
                res.append((dy, dx, y, x))
        return res
    def s0_src(s):
        p = s.p
        return (p.par * 2 + p.c) * 2 + p.xh
    def s0(s, ph):
        p = s.p; o = s.s0_src()
        for tc in (0, 1):
            cond = (o <= 4) if tc == 0 else (o >= 4)
            @pl.when(cond)
            def _(tc=tc):
                for dy, dx, y, x in s.s0_targets():
                    src = s.pieces.at[ph, ((x >> 1)) * 2 + (y & 1)]
                    dst = s.stg.at[ph, o - 4 * tc]
                    def send(sem):
                        pltpu.make_async_remote_copy(src, dst, s.s0s.at[sem], s.s0r.at[ph], device_id=p.dev(y=y, x=x, c=tc), device_id_type=MESH).start()
                    if dy == 0 and dx == 0:
                        @pl.when(p.c == tc)
                        def _():
                            pltpu.make_async_copy(src, dst, s.s0r.at[ph]).start()
                        @pl.when(p.c != tc)
                        def _():
                            send(2)
                    else:
                        send(tc)
    def s0_recv(s, ph):
        pl.when(s.p.c == 0)(lambda: wait(s.stg.at[ph], s.s0r.at[ph]))
        pl.when(s.p.c == 1)(lambda: wait(s.stg.at[ph, 0:4], s.s0r.at[ph]))
    def compact(s, ph):
        p = s.p
        i = lax.broadcasted_iota(jnp.int32, (48, 80), 0)
        k = lax.broadcasted_iota(jnp.int32, (48, 80), 1)
        r = 48 * p.c + i
        q = (r * 205) >> 11
        col = (q - 4 * p.c) * 16 + (r - q * 10)
        P = jnp.where(k == col, 1.0, 0.0).astype(jnp.bfloat16)
        res = jnp.dot(P, s.stg[ph].reshape(80, CW), preferred_element_type=jnp.float32).astype(jnp.bfloat16)
        def put(ts):
            s.W[ph, p.xh, p.par, p.z, p.xl, p.h, 3 * p.c + ts] = res[ts * 16:(ts + 1) * 16]
        put(0); put(1)
        pl.when(p.c == 0)(lambda: put(2))
    def order(s, ph, ts):
        a = (ph + ts) % 3
        return ((a + 1) % 3, (a + 2) % 3, a)
    def region(s, ph, t, full, over=None):
        p = s.p; o = over or {}
        x = o.get(0); y = o.get(1); z = o.get(2)
        xh, xl = (p.xh, p.xl) if x is None else ((x >> 1), (x & 1))
        h, par = (p.h, p.par) if y is None else ((y >> 1), (y & 1))
        zz = p.z if z is None else z
        if 0 in full: xh = xl = slice(None)
        if 1 in full: h = par = slice(None)
        if 2 in full: zz = slice(None)
        return [ph, xh, par, zz, xl, h, t]
    def ref(s, reg): return s.W.at[tuple(reg)]
    def cp(s, reg, ph, ts, kind, k, dev):
        r = s.ref(reg)
        return pltpu.make_async_remote_copy(r, r, s.ssem.at[kind + (4 if ts == 2 else 0)], s.rsem.at[ph * 3 + ts, k], device_id=dev, device_id_type=MESH)
    def half(s, reg, full, hf):
        reg = list(reg)
        i = 3 if 2 in full else (1 if 0 in full else 2)
        reg[i] = pl.ds(hf * 2, 2) if i == 3 else pl.ds(hf, 1)
        return reg
    def t(s, ts): return 3 * s.p.c + ts
    def direct(s, stage, ph, ts):
        a = s.order(ph, ts); full = a[:stage]; ax = a[stage]
        for d in (2, 1, 3):
            s.cp(s.region(ph, s.t(ts), full), ph, ts, stage, stage, s.p.ring(ax, d)).start()
    def got(s, ph, ts, k):
        r = s.W.at[ph]
        ref = (lambda: r.at[0, 0, 0:3, 0, 0, 0], lambda: r.at[0, 0, 0:3, :, :, 0], lambda: r.at[0, 0, :, :, :, 0],
               lambda: r.at[0, 0, :, :, :, 0], lambda: r.at[0, 0, :, :, :, 0], lambda: r.at[:, :, :, :, :, 0])[k]()
        wait(ref, s.rsem.at[ph * 3 + ts, k])
    def s3(s, ph, ts, what):
        a = s.order(ph, ts); full = a[:2]; ax = a[2]; tt = s.t(ts)
        R, L = s.p.ring(ax, 1), s.p.ring(ax, 3)
        reg = lambda d: s.region(ph, tt, full, {ax: s.p.coord(ax, d)})
        if what == 'own':
            s.cp(reg(0), ph, ts, 2, 2, R).start()
            s.cp(reg(0), ph, ts, 2, 3, L).start()
        elif what == 'fwdR': s.cp(s.half(reg(-1), full, 0), ph, ts, 2, 4, R).start()
        else: s.cp(s.half(reg(1), full, 1), ph, ts, 2, 4, L).start()
    def sib(s, ph, ts, piece):
        a = s.order(ph, ts); full = a[:2]; ax = a[2]
        d = (0, -1, 1, 2)[piece]
        s.cp(s.region(ph, s.t(ts), full, {ax: s.p.coord(ax, d)}), ph, ts, 3, 5, s.p.sibling).start()
    def go(s, ts, f, other=False):
        def h():
            f()
        if ts < 2: h()
        else: pl.when(s.p.c == (1 if other else 0))(h)
    def each(s, f, other=False):
        for ts in range(3): s.go(ts, lambda ts=ts: f(ts), other)
    def phase_a(s, ph):
        s.each(lambda ts: s.direct(0, ph, ts))
    def phase_b(s, ph):
        s.each(lambda ts: (s.got(ph, ts, 0), s.direct(1, ph, ts)))
    def phase_c(s, ph):
        s.each(lambda ts: (s.got(ph, ts, 1), s.s3(ph, ts, 'own'), s.sib(ph, ts, 0)))
    def phase_d(s, ph):
        s.each(lambda ts: (s.got(ph, ts, 2), s.s3(ph, ts, 'fwdR'), s.sib(ph, ts, 1), s.got(ph, ts, 3), s.s3(ph, ts, 'fwdL'), s.sib(ph, ts, 2)))
    def phase_e(s, ph):
        s.each(lambda ts: (s.got(ph, ts, 4), s.sib(ph, ts, 3)))
    def phase_f(s, ph):
        s.each(lambda ts: s.got(ph, ts, 5), other=True)
    def drain(s):
        W = s.W
        for ts, t in ((0, slice(0, 2)), (2, 0)):
            def w(ts=ts, t=t):
                k = 4 if ts == 2 else 0
                wait(W.at[:, 0, 0, 0:3, 0, 0, t], s.ssem.at[k])
                wait(W.at[:, 0, 0, 0:3, :, :, t], s.ssem.at[k + 1])
                wait(W.at[:, :, :, 0:3, :, :, t], s.ssem.at[k + 2])
                wait(W.at[:, :, :, :, :, :, t], s.ssem.at[k + 3])
            if ts == 0: w()
            else: pl.when(s.p.c == 0)(w)
        o = s.s0_src()
        for tc in (0, 1):
            cond = (o <= 4) if tc == 0 else (o >= 4)
            pl.when(cond)(lambda tc=tc: wait(s.pieces.at[:, 0:3], s.s0s.at[tc]))
            pl.when(jnp.logical_and(cond, s.p.c != tc))(lambda: wait(s.pieces.at[:, 0], s.s0s.at[2]))

def barrier(partners):
    b = pltpu.get_barrier_semaphore()
    for d in partners:
        pl.semaphore_signal(b, inc=1, device_id=d, device_id_type=MESH)
    pl.semaphore_wait(b, len(partners))

def fill_pieces(pieces, wqkv, wout, wup, wdown):
    mats = [(wqkv, 0), (wqkv, 1280), (wqkv, 2560), (wout, 0), (wup, 0), (wdown, 0)]
    for ph in range(3):
        for xh in range(2):
            r, off = mats[2 * ph + xh]
            for par in range(2):
                v = r[:, off + par * 640: off + (par + 1) * 640]
                pieces[ph, 2 * xh + par] = jnp.concatenate([v.astype(jnp.float32), jnp.zeros((6, 640), jnp.float32)], axis=0).astype(jnp.bfloat16)


def dot(a, b):
    return jnp.dot(a, b, preferred_element_type=F32)


def dot_nt(a, b):
    return lax.dot_general(a, b, (((1,), (1,)), ((), ())), preferred_element_type=F32)


def dot_tn(a, b):
    return lax.dot_general(a, b, (((0,), (0,)), ((), ())), preferred_element_type=F32)


def at128(v):
    return pl.multiple_of(v, 128)


def window(z, xl):
    return 320 * z - 64 * ((z & 1)) + 128 * xl


class Spread:
    def __init__(s, p, T, R0, R1, R2, T3, R3, out, ssem, rsem):
        s.p, s.T, s.T3, s.out, s.ssem, s.rsem = p, T, T3, out, ssem, rsem
        s.R = (R0, R1, R2, R3)

    def start(s, k):
        p = s.p
        src = s.T3 if k == 3 else s.T
        if k == 0: devs = [p.sibling]
        else: devs = [p.ring((1, 0, 2)[k - 1], d) for d in (1, 2, 3)]
        for i, dv in enumerate(devs):
            pltpu.make_async_remote_copy(src, s.R[k].at[i], s.ssem.at[k], s.rsem.at[k], device_id=dv, device_id_type=MESH).start()

    def finish(s, k):
        p = s.p
        R = s.R[k]
        wait(R, s.rsem.at[k])
        wait(R, s.ssem.at[k])
        if k < 2:
            acc = s.T[...].astype(F32)
            for i in range(R.shape[0]): acc = acc + R[i].astype(F32)
            s.T[...] = acc.astype(BF)
        elif k == 2:
            s.T3[...] = jnp.zeros((32, 384), BF)
            mine = pl.ds(at128(128 * p.xl), 256)
            other = pl.ds(at128(128 - 128 * p.xl), 256)
            s.T3[:, mine] = (s.T[...].astype(F32) + R[1].astype(F32)).astype(BF)
            s.T3[:, other] = (s.T3[:, other].astype(F32) + R[0].astype(F32) + R[2].astype(F32)).astype(BF)
        else:
            s.out[...] = jnp.zeros((32, D), BF)
            for i in range(4):
                lanes = pl.ds(at128(window(((p.z + 4 - i) & 3), 0)), 384)
                v = s.T3[...] if i == 0 else R[i - 1]
                s.out[:, lanes] = (s.out[:, lanes].astype(F32) + v.astype(F32)).astype(BF)


class Gather:
    def __init__(s, p, buf, R0, R1, S1, R2, S2, R3, R4, ssem, rsem):
        s.p, s.buf, s.R0, s.R1, s.S1, s.R2, s.S2, s.R3, s.R4 = p, buf, R0, R1, S1, R2, S2, R3, R4
        s.ssem, s.rsem = ssem, rsem
        s.active = (p.z >> 1) == p.c

    def send(s, k, src, dst, dv):
        pltpu.make_async_remote_copy(src, dst, s.ssem.at[k], s.rsem.at[k], device_id=dv, device_id_type=MESH).start()

    def start(s, k):
        p = s.p
        if k == 0:
            s.send(0, s.buf.at[1 - p.c], s.R0, p.sibling)
        elif k == 1:
            for d in (1, 2, 3):
                z = ((p.z + d) & 3)
                @pl.when((z >> 1) == p.c)
                def _(z=z, d=d):
                    s.send(1, s.buf.at[p.c, :, pl.ds(at128(256 * ((z & 1))), 384)], s.R1.at[d - 1], p.dev(z=z))
        else:
            @pl.when(s.active)
            def _():
                if k == 2:
                    s.send(2, s.S1.at[:, pl.ds(at128(128 - 128 * p.xl), 256)], s.R2, p.pair)
                elif k == 3:
                    for d in (1, 2, 3): s.send(3, s.S2, s.R3.at[d - 1], p.ring(1, d))
                else:
                    s.send(4, s.S2, s.R4, p.sibling)

    def finish(s, k):
        p = s.p
        if k == 0:
            wait(s.R0, s.rsem.at[0])
            wait(s.R0, s.ssem.at[0])
            s.buf[p.c] = s.buf[p.c] + s.R0[...]
            return
        if k == 1:
            pl.when(s.active)(lambda: wait(s.R1.at[0], s.ssem.at[1]))
            pl.when(jnp.logical_not(s.active))(lambda: wait(s.R1.at[0:2], s.ssem.at[1]))
        if k == 4:
            @pl.when(jnp.logical_not(s.active))
            def _():
                wait(s.R4, s.rsem.at[4])
                s.S2[...] = s.R4[...]
            pl.when(s.active)(lambda: wait(s.R4, s.ssem.at[4]))
            return
        @pl.when(s.active)
        def _():
            if k == 1:
                wait(s.R1, s.rsem.at[1])
                mine = pl.ds(at128(256 * ((p.z & 1))), 384)
                s.S1[...] = s.buf[p.c, :, mine] + s.R1[0] + s.R1[1] + s.R1[2]
            elif k == 2:
                wait(s.R2, s.rsem.at[2])
                wait(s.R2, s.ssem.at[2])
                s.S2[...] = s.S1[:, pl.ds(at128(128 * p.xl), 256)] + s.R2[...]
            else:
                wait(s.R3, s.rsem.at[3])
                wait(s.R3, s.ssem.at[3])
                s.S2[...] = s.S2[...] + s.R3[0] + s.R3[1] + s.R3[2]


class RS:
    def __init__(s, p, G, GW, RD, bufs, FR, EX, FIN, dss, drs, ss, rs, fs, fr):
        s.p, s.G, s.GW, s.RD, s.bufs, s.FR, s.EX, s.FIN = p, G, GW, RD, bufs, FR, EX, FIN
        s.dss, s.drs, s.ss, s.rs, s.fs, s.fr = dss, drs, ss, rs, fs, fr

    def gref(s, ph):
        return s.G[ph]

    def go(s, ts, f, other=False):
        def h():
            f()
        if ts < 2: h()
        else: pl.when(s.p.c == (1 if other else 0))(h)

    def d2d(s, ph, ts, act, par):
        p = s.p
        g = s.gref(ph)
        t = 3 * (1 - p.c) + ts if act != 'recv' else 3 * p.c + ts
        cp = pltpu.make_async_remote_copy(g.at[par, :, :, :, t], s.RD.at[ph, ts, par], s.dss.at[(ts >> 1)], s.drs.at[ph * 3 + ts, par], device_id=p.sibling, device_id_type=MESH)
        if act == 'start': cp.start()
        else: cp.wait_recv()

    def d2d_start(s, ph, par):
        for ts in range(3): s.go(ts, lambda ts=ts: s.d2d(ph, ts, 'start', par), other=True)

    def d2d_add(s, ph, ts, par):
        g = s.gref(ph)
        t = 3 * s.p.c + ts
        s.d2d(ph, ts, 'recv', par)
        def body(z, _):
            g[par, z, :, :, t] = (g[par, z, :, :, t].astype(F32) + s.RD[ph, ts, par, z].astype(F32)).astype(BF)
            return 0
        lax.fori_loop(0, 4, body, 0)

    def order(s, ph, ts):
        return ((1, 0, 2), (2, 0, 1), (0, 2, 1))[ts]

    def fidx(s, ph, ts):
        return (1, 2, 0)[ts]

    def piece(s, ph, ts, st, k):
        p = s.p
        o = s.order(ph, ts)
        ax = o[st]
        done = o[:st]
        par = h = zz = xl = slice(None)
        if 0 in done: xl = p.xl
        if 1 in done: h, par = p.h, p.par
        if 2 in done: zz = p.z
        if ax == 0: xl = k
        if ax == 1: h, par = (k >> 1), (k & 1)
        if ax == 2: zz = k
        return s.gref(ph).at[par, zz, xl, h, 3 * p.c + ts]

    def half(s, ph, ts, st, k, hf):
        p = s.p
        o = s.order(ph, ts)
        ax = o[st]
        assert st == 0
        t = 3 * p.c + ts
        if ax == 1: return s.gref(ph).at[(k & 1), pl.ds(2 * hf, 2), :, (k >> 1), t]
        return s.gref(ph).at[hf, k, :, :, t]

    def bhalf(s, ph, ts, hf):
        f = s.fidx(ph, ts)
        b = s.bufs[f][0]
        if f == 1: return b.at[ph, 2, pl.ds(2 * hf, 2)]
        return b.at[ph, 2, hf]

    def cp(s, src, dst, sk, sl, k, dev):
        return pltpu.make_async_remote_copy(src, dst, s.ss.at[sk], s.rs.at[sl, k], device_id=dev, device_id_type=MESH)

    def add(s, dst, srcs):
        lead = dst.shape[:-2]
        if len(lead) >= 1 and lead[0] > 1:
            def body(i, _):
                acc = dst[i].astype(F32)
                for r in srcs: acc = acc + r[i].astype(F32)
                dst[i] = acc.astype(BF)
                return 0
            lax.fori_loop(0, lead[0], body, 0)
        else:
            acc = dst[...].astype(F32)
            for r in srcs: acc = acc + r[...].astype(F32)
            dst[...] = acc.astype(BF)

    def ring_cps(s, ph, ts, st):
        p = s.p
        o = s.order(ph, ts)
        ax = o[st]
        f = s.fidx(ph, ts)
        sl = ph * 3 + ts
        b = s.bufs[f][st]
        sk = st + (3 if ts == 2 else 0)
        if ax == 0:
            k = 1 - p.xl
            src, dv = s.piece(ph, ts, st, k), p.pair
            if st == 0: return [s.cp(src.at[par], b.at[ph, 0, par], sk, sl, par, dv) for par in range(2)]
            return [s.cp(src, b.at[ph, 0], sk, sl, 2 + st, dv)]
        res = []
        for i, d in enumerate((2, 1, 3)):
            res.append(s.cp(s.piece(ph, ts, st, p.coord(ax, d)), b.at[ph, i], sk, sl, 2 + st, p.ring(ax, d)))
        return res

    def first_a(s, ph, ts, par):
        ax = s.order(ph, ts)[0]
        if ax == 0:
            s.ring_cps(ph, ts, 0)[par].start()
        elif ax == 2:
            s.sf_half(ph, ts)[1 - par].start()
        else:
            @pl.when(s.p.par == par)
            def _():
                for c in s.sf_half(ph, ts): c.start()

    def sf_half(s, ph, ts):
        p = s.p
        ax = s.order(ph, ts)[0]
        sl = ph * 3 + ts
        k = p.coord(ax, 2)
        return [s.cp(s.half(ph, ts, 0, k, 1), s.bhalf(ph, ts, 1), 0, sl, 0, p.ring(ax, 1)),
                s.cp(s.half(ph, ts, 0, k, 0), s.bhalf(ph, ts, 0), 0, sl, 1, p.ring(ax, 3))]

    def sf_full(s, ph, ts):
        p = s.p
        ax = s.order(ph, ts)[0]
        sl = ph * 3 + ts
        b = s.bufs[s.fidx(ph, ts)][0]
        return [s.cp(s.piece(ph, ts, 0, p.coord(ax, 1)), b.at[ph, 0], 0, sl, 2, p.ring(ax, 1)),
                s.cp(s.piece(ph, ts, 0, p.coord(ax, 3)), b.at[ph, 1], 0, sl, 2, p.ring(ax, 3))]

    def first_b(s, ph, ts):
        p = s.p
        o = s.order(ph, ts)
        ax = o[0]
        if ax == 0: return
        hb = s.sf_half(ph, ts)
        full = s.sf_full(ph, ts)
        hb[0].wait_recv()
        s.add(s.half(ph, ts, 0, p.coord(ax, 1), 1), [s.bhalf(ph, ts, 1)])
        full[0].start()
        hb[1].wait_recv()
        s.add(s.half(ph, ts, 0, p.coord(ax, 3), 0), [s.bhalf(ph, ts, 0)])
        full[1].start()

    def first_c(s, ph, ts):
        p = s.p
        o = s.order(ph, ts)
        ax = o[0]
        me = (p.xl, p.y, p.z)[ax]
        b = s.bufs[s.fidx(ph, ts)][0]
        if ax == 0:
            for par, c in enumerate(s.ring_cps(ph, ts, 0)):
                c.wait_recv()
                s.add(s.piece(ph, ts, 0, me).at[par], [b.at[ph, 0, par]])
            return
        wait(b.at[ph, 0:2], s.rs.at[ph * 3 + ts, 2])
        s.add(s.piece(ph, ts, 0, me), [b.at[ph, i] for i in range(2)])

    def next_start(s, ph, ts, st):
        for c in s.ring_cps(ph, ts, st): c.start()

    def next_finish(s, ph, ts, st):
        p = s.p
        ax = s.order(ph, ts)[st]
        me = (p.xl, p.y, p.z)[ax]
        b = s.bufs[s.fidx(ph, ts)][st]
        wait(b.at[ph], s.rs.at[ph * 3 + ts, 2 + st])
        s.add(s.piece(ph, ts, st, me), [b.at[ph, i] for i in range(1 if ax == 0 else 3)])

    def each(s, f):
        for ts in range(3): s.go(ts, lambda ts=ts: f(ts))

    def first(s, ph, par):
        s.each(lambda ts: (s.d2d_add(ph, ts, par), s.first_a(ph, ts, par)))

    def step(s, ph, k):
        if k == 2: s.each(lambda ts: s.first_b(ph, ts))
        elif k == 3: s.each(lambda ts: (s.first_c(ph, ts), s.next_start(ph, ts, 1)))
        elif k == 4: s.each(lambda ts: (s.next_finish(ph, ts, 1), s.next_start(ph, ts, 2)))
        elif k == 5:
            s.each(lambda ts: s.next_finish(ph, ts, 2))
            s.final_start(ph)

    def fin_cps(s, ph, k):
        p = s.p
        o = 4 * p.c + k
        chunk = 2 * p.xh + p.par
        dev = p.dev(x=((o & 1)) * 2 + p.xl, y=2 * p.h + (o >> 2), c=(((o >> 1)) & 1))
        return pltpu.make_async_remote_copy(s.EX.at[ph, k], s.FIN.at[ph, chunk, p.c], s.fs.at[0], s.fr.at[ph, p.c], device_id=dev, device_id_type=MESH)

    def myo(s):
        p = s.p
        return (p.par * 2 + p.c) * 2 + p.xh

    def final_start(s, ph):
        p = s.p
        g = s.gref(ph)
        def put(ts):
            s.FR[ts] = g[p.par, p.z, p.xl, p.h, 3 * p.c + ts]
        put(0); put(1)
        pl.when(p.c == 0)(lambda: put(2))
        i = lax.broadcasted_iota(jnp.int32, (80, 48), 1)
        k = lax.broadcasted_iota(jnp.int32, (80, 48), 0)
        r = 48 * p.c + i
        q = (r * 205) >> 11
        col = (q - 4 * p.c) * 16 + (r - q * 10)
        pt = jnp.where(k == col, 1.0, 0.0).astype(BF)
        s.EX[ph] = dot(pt, s.FR[...].reshape(48, CW)).astype(BF).reshape(5, 16, CW)
        for k in range(5):
            def send(k=k):
                me = 4 * p.c + k == s.myo()
                @pl.when(me)
                def _():
                    s.FIN[ph, 2 * p.xh + p.par, p.c] = s.EX[ph, k]
                @pl.when(jnp.logical_not(me))
                def _():
                    s.fin_cps(ph, k).start()
            if k < 4: send()
            else: pl.when(p.c == 0)(send)

    def final_wait(s, ph):
        p = s.p
        o = s.myo()
        for sc in range(2):
            used = (o <= 4) if sc == 0 else (o >= 4)
            pl.when(jnp.logical_and(used, p.c == sc))(lambda: wait(s.FIN.at[ph, 0:3, 0], s.fr.at[ph, sc]))
            pl.when(jnp.logical_and(used, p.c != sc))(lambda: wait(s.FIN.at[ph, :, 0], s.fr.at[ph, sc]))

    def drain(s):
        p = s.p
        G = s.GW
        wait(G.at[:, :, :, :, :, 0:2], s.dss.at[0])
        pl.when(p.c == 1)(lambda: wait(G.at[:, :, :, :, :, 0], s.dss.at[1]))
        wait(G.at[:, :, 0:3, :, :, 0:2], s.ss.at[0])
        wait(G.at[:, 0, :, 0, 0, 0:2], s.ss.at[1])
        wait(G.at[:, 0, 0:3, 0, 0, 0:2], s.ss.at[2])
        @pl.when(p.c == 0)
        def _():
            wait(G.at[:, :, :, :, 0, 0], s.ss.at[3])
            wait(G.at[:, 0, 0:3, :, :, 0], s.ss.at[4])
            wait(G.at[:, 0, 0:3, 0, 0, 0], s.ss.at[5])
        o = s.myo()
        n = jnp.where(p.c == 0, jnp.where(o <= 4, 4, 5), jnp.where(o >= 4, 3, 4))
        for k in (3, 4, 5):
            pl.when(n == k)(lambda k=k: wait(s.EX.at[:, 0:k], s.fs.at[0]))


def clear_last(stg, FR):
    stg[:, 4] = jnp.zeros((3, 16, CW), BF)
    FR[2] = jnp.zeros((16, CW), BF)


FIRST, Q, K, V, MIXED, SECOND, ACTIVE, GU, GAO, GMX, GQ, GK, GV = range(13)
RB = 32
UNROLL = 4


def block_kernel(lat_in, cot_in, sid, *refs):
    small_in, (o_lat, o_in), small_out = refs[0:8], refs[8:10], refs[10:16]
    block_body(lat_in, cot_in, sid, small_in, o_lat, o_in, small_out, *refs[16:])


def block_body(lat_in, cot_in, sid, small_in, o_lat, o_in, small_out,
                 W, stg, pieces, A, N1, N2, MID, DG, PR, I1, I2, VEC, CS, GW, RD, b00, b01, b02, b10, b11, b12, b20, b21, b22,
                 FR, EX, FIN, SB, SBT, SB0, SB1, SB2, SBT3, SB3, SG, SG0, SG1, SGS1, SG2, SGS2, SG3, SG4,
                 lat, cot, gt, b1, g2, b2, wq, wo, wu, wd, o_tab, o_vec, o_qkv, o_out, o_up, o_down, ssem, rsem, s0s, s0r, dss, drs, gss, grs, fs, fr, sbs, sbr, sgs, sgr, io):
    p = Pos()
    ag = AG(p, W, stg, pieces, ssem, rsem, None, s0s, s0r)
    G = [GW.at[0], GW.at[1], GW.at[2]]
    rs = RS(p, G, GW, RD, [[b00, b01, b02], [b10, b11, b12], [b20, b21, b22]], FR, EX, FIN, dss, drs, gss, grs, fs, fr)
    sb = Spread(p, SBT, SB0, SB1, SB2, SBT3, SB3, SB, sbs, sbr)
    sg = Gather(p, SG, SG0, SG1, SGS1, SG2, SGS2, SG3, SG4, sgs, sgr)
    idx = lax.axis_index("dp") * 2 + p.xh

    parts = ag.partners()
    bar = pltpu.get_barrier_semaphore()
    for d in parts:
        pl.semaphore_signal(bar, inc=1, device_id=d, device_id_type=MESH)
    in_lat = pltpu.make_async_copy(lat_in, lat, io.at[0])
    in_cot = pltpu.make_async_copy(cot_in, cot, io.at[1])
    ins = [pltpu.make_async_copy(a, v, io.at[4 + i]) for i, (a, v) in enumerate(zip(small_in, (gt, b1, g2, b2, wq, wo, wu, wd)))]
    for c in ins: c.start()
    in_lat.start(); in_cot.start()
    for c in ins: c.wait()
    fill_pieces(pieces, wq, wo, wu, wd)
    pl.when(p.c == 1)(lambda: clear_last(stg, FR))
    j = lax.broadcasted_iota(jnp.int32, (16, 256), 0)
    lane = lax.broadcasted_iota(jnp.int32, (16, 256), 1) + window(p.z, p.xl)
    own = jnp.where(jnp.logical_and(lane == idx * 10 + j, j < 10), 1.0, 0.0)
    own16 = own[0:10].astype(BF)
    spread = [dot_tn(gt[...], own16)] + [dot(jnp.broadcast_to(b[...].reshape(1, 10), (8, 10)), own16)[0:1] for b in (b1, g2, b2)] + [jnp.zeros((13, 256), F32)]
    SBT[...] = jnp.concatenate(spread, axis=0).astype(BF)
    pl.semaphore_wait(bar, len(parts))

    sb.start(0)
    for ph in range(3): ag.s0(ph)

    def ln1(r, _):
        rows = pl.ds(pl.multiple_of(r * RB, RB), RB)
        x = lat[rows, :].astype(F32)
        mu = jnp.mean(x, axis=-1, keepdims=True)
        xc = x - mu
        inv = lax.rsqrt(jnp.mean(xc * xc, axis=-1, keepdims=True) + EPS)
        N1[rows, :] = xc * inv
        I1[rows, :] = jnp.broadcast_to(inv, (RB, 128))
        return 0
    in_lat.wait(); in_cot.wait()
    lax.fori_loop(0, L // RB, ln1, 0, unroll=UNROLL)
    ag.s0_recv(0); ag.compact(0); ag.phase_a(0)
    sb.finish(0); sb.start(1)
    ag.s0_recv(1); ag.compact(1); ag.phase_a(1)
    ag.phase_b(0)
    sb.finish(1); sb.start(2)
    ag.s0_recv(2); ag.compact(2); ag.phase_a(2)
    ag.phase_b(1)
    ag.phase_c(0)
    sb.finish(2); sb.start(3)
    ag.phase_b(2)
    ag.phase_c(1)
    A[MIXED] = jnp.zeros((L, D), BF)
    for k in (GQ, GK, GV): A[k] = jnp.zeros((L, D), BF)
    CS[...] = jnp.zeros_like(CS)
    ag.phase_d(0)
    ag.phase_c(2)
    sb.finish(3)
    lane32 = lax.broadcasted_iota(jnp.int32, (8, 32), 1)
    sub8 = lax.broadcasted_iota(jnp.int32, (8, 32), 0)
    script = jnp.broadcast_to(sid[...].reshape(1, 1), (1, 640))
    tgt = jnp.where(sub8 == 0, script[:, 0:32], jnp.where(sub8 < 4, 15 + sub8, -1))
    pick = jnp.where(lane32 == tgt, 1.0, 0.0).astype(BF)
    VEC[...] = dot(pick, SB[...])

    def mk_first(r, _):
        rows = pl.ds(pl.multiple_of(r * RB, RB), RB)
        A[FIRST, rows, :] = (N1[rows, :] * VEC[0:1, :] + VEC[1:2, :]).astype(BF)
        return 0
    lax.fori_loop(0, L // RB, mk_first, 0, unroll=UNROLL)
    ag.phase_d(1)
    ag.phase_e(0)
    ag.phase_f(0)

    def wpan(ph, xh, par): return W[ph, xh, par].reshape(D, CW)
    def cols(par): return pl.ds(par * CW, CW)

    for par in range(2):
        A[Q, :, cols(par)] = dot(A[FIRST], wpan(0, 0, par)).astype(BF)
    ag.phase_d(2)
    for par in range(2):
        A[K, :, cols(par)] = dot(A[FIRST], wpan(0, 1, par)).astype(BF)
    ag.phase_e(1)
    ag.phase_f(1)
    for par in range(2):
        A[V, :, cols(par)] = dot(A[FIRST], wpan(1, 0, par)).astype(BF)

    lane256 = lax.broadcasted_iota(jnp.int32, (1, 256), 1)
    def masks(w):
        m = jnp.where(jnp.logical_and(lane256 >= 32 * w, lane256 < 32 * w + HD), 1.0, 0.0)
        return m, m.astype(BF)
    def win(pn, w):
        return pl.ds(pl.multiple_of(pn * CW + w * 128, 128), 256)

    for pn in range(2):
        def att(w, _, pn=pn):
            cw = win(pn, w)
            m32, m16 = masks(w)
            sc = dot_nt(A[Q, :, cw] * m16, A[K, :, cw]) * SCALE
            e = jnp.exp(sc - jnp.max(sc, axis=-1, keepdims=True))
            pr = e * (1.0 / jnp.sum(e, axis=-1, keepdims=True))
            PR[pn * 4 + w] = pr
            mx = dot(pr.astype(BF), A[V, :, cw]) * m32
            A[MIXED, :, cw] = A[MIXED, :, cw] + mx.astype(BF)
            return 0
        lax.fori_loop(0, 4, att, 0, unroll=True)
    ag.phase_e(2)
    for par in range(2):
        MID[:, cols(par)] = lat[:, cols(par)].astype(F32) + dot(A[MIXED], wpan(1, 1, par))

    def ln2(r, _):
        rows = pl.ds(pl.multiple_of(r * RB, RB), RB)
        x = MID[rows, :]
        mu = jnp.mean(x, axis=-1, keepdims=True)
        xc = x - mu
        inv = lax.rsqrt(jnp.mean(xc * xc, axis=-1, keepdims=True) + EPS)
        n = xc * inv
        N2[rows, :] = n
        I2[rows, :] = jnp.broadcast_to(inv, (RB, 128))
        A[SECOND, rows, :] = (n * VEC[2:3, :] + VEC[3:4, :]).astype(BF)
        return 0
    lax.fori_loop(0, L // RB, ln2, 0, unroll=UNROLL)
    ag.phase_f(2)
    for par in range(2):
        DG[:, cols(par)] = dot(A[SECOND], wpan(2, 0, par))

    def gelu(r, _):
        rows = pl.ds(pl.multiple_of(r * RB, RB), RB)
        u = DG[rows, :]
        c0 = math.sqrt(2.0 / math.pi)
        u2 = u * u
        th = jnp.tanh(c0 * (u + 0.044715 * u2 * u))
        hp = 0.5 * (1.0 + th)
        A[ACTIVE, rows, :] = (u * hp).astype(BF)
        DG[rows, :] = hp + 0.5 * u * (1.0 - th * th) * (c0 * (1.0 + 3 * 0.044715 * u2))
        return 0
    lax.fori_loop(0, L // RB, gelu, 0, unroll=UNROLL)

    def back(src, ph, xh, n):
        acc = None
        for par in range(2):
            t = dot_nt(src(par), W[ph, xh, par, 2 * n:2 * n + 2].reshape(CW, CW))
            acc = t if acc is None else acc + t
        return acc

    half = pl.ds(pl.multiple_of(p.xh * CW, 128), CW)

    def wgrad(ph, par, left, right):
        for n in range(2):
            v = dot_tn(A[left, :, cols(n)], right[:, half])
            G[ph][par, 2 * n:2 * n + 2] = v.astype(BF).reshape(2, 2, 2, 5, 16, CW)
        rs.d2d_start(ph, par)

    wgrad(2, 1, ACTIVE, cot)
    for n in range(2):
        A[GU, :, cols(n)] = (back(lambda par: cot[:, cols(par)], 2, 1, n) * DG[:, cols(n)]).astype(BF)
    wgrad(2, 0, SECOND, A.at[GU])
    for n in range(2):
        DG[:, cols(n)] = back(lambda par: A[GU, :, cols(par)], 2, 0, n)

    rs.first(2, 1)

    def ln2b(r, _):
        rows = pl.ds(pl.multiple_of(r * RB, RB), RB)
        gs = DG[rows, :]
        n = N2[rows, :]
        CS[1] += jnp.sum((gs * n).reshape(RB // 8, 8, D), axis=0)
        CS[2] += jnp.sum(gs.reshape(RB // 8, 8, D), axis=0)
        dn = gs * VEC[2:3, :]
        m1 = jnp.mean(dn, axis=-1, keepdims=True)
        m2 = jnp.mean(dn * n, axis=-1, keepdims=True)
        gm = cot[rows, :].astype(F32) + I2[rows, 0:1] * (dn - m1 - n * m2)
        N2[rows, :] = gm
        A[GAO, rows, :] = gm.astype(BF)
        return 0
    lax.fori_loop(0, L // RB, ln2b, 0, unroll=UNROLL)
    wgrad(1, 1, MIXED, A.at[GAO])
    for n in range(2):
        A[GMX, :, cols(n)] = back(lambda par: A[GAO, :, cols(par)], 1, 1, n).astype(BF)
        if n == 0: rs.first(2, 0)

    for i in range(2):
        pn = p.xh if i == 0 else 1 - p.xh
        def attb(w, _, pn=pn):
            cw = win(pn, w)
            m32, m16 = masks(w)
            gm = A[GMX, :, cw] * m16
            qm = A[Q, :, cw] * m16
            pr = PR[pn * 4 + w]
            gp = dot_nt(gm, A[V, :, cw])
            rt = jnp.sum(gp * pr, axis=-1, keepdims=True)
            gsc = (pr * (gp - rt)).astype(BF)
            A[GV, :, cw] = A[GV, :, cw] + dot_tn(pr.astype(BF), gm).astype(BF)
            A[GQ, :, cw] = A[GQ, :, cw] + (dot(gsc, A[K, :, cw]) * SCALE * m32).astype(BF)
            A[GK, :, cw] = A[GK, :, cw] + (dot_tn(gsc, qm) * SCALE).astype(BF)
            return 0
        lax.fori_loop(0, 2, attb, 0, unroll=True)
        if i == 0:
            rs.first(1, 1)
            rs.step(2, 2)
        else:
            rs.first(1, 0)
            rs.first(0, 0)
            rs.first(0, 1)
            rs.step(2, 3)
        lax.fori_loop(2, 4, attb, 0, unroll=True)
        if i == 0:
            wgrad(1, 0, FIRST, A.at[GV])
            wgrad(0, 0, FIRST, A.at[GQ])
            wgrad(0, 1, FIRST, A.at[GK])
    rs.step(1, 2)
    rs.step(0, 2)
    for n in range(2):
        acc = None
        for g, (ph, xh) in ((GQ, (0, 0)), (GK, (0, 1)), (GV, (1, 0))):
            t = back(lambda par: A[g, :, cols(par)], ph, xh, n)
            acc = t if acc is None else acc + t
        DG[:, cols(n)] = acc
    rs.step(2, 4)

    def ln1b(r, _):
        rows = pl.ds(pl.multiple_of(r * RB, RB), RB)
        gf = DG[rows, :]
        n = N1[rows, :]
        CS[3] += jnp.sum((gf * n).reshape(RB // 8, 8, D), axis=0)
        CS[0] += jnp.sum(gf.reshape(RB // 8, 8, D), axis=0)
        dn = gf * VEC[0:1, :]
        m1 = jnp.mean(dn, axis=-1, keepdims=True)
        m2 = jnp.mean(dn * n, axis=-1, keepdims=True)
        DG[rows, :] = N2[rows, :] + I1[rows, 0:1] * (dn - m1 - n * m2)
        return 0
    lax.fori_loop(0, L // RB, ln1b, 0, unroll=UNROLL)
    out_in = pltpu.make_async_copy(DG, o_in, io.at[3])
    out_in.start()
    sub24 = lax.broadcasted_iota(jnp.int32, (24, 640), 0)
    for k in range(2):
        v = [jnp.sum(CS[i, :, k * 640:(k + 1) * 640], axis=0, keepdims=True) for i in range(4)]
        SG[k] = (jnp.where(sub24 == script, v[3], 0.0) + jnp.where(sub24 == 16, v[0], 0.0)
                 + jnp.where(sub24 == 17, v[1], 0.0) + jnp.where(sub24 == 18, v[2], 0.0))
    sg.start(0)
    rs.step(1, 3)
    rs.step(0, 3)
    for par in range(2):
        A[SECOND, :, cols(par)] = (MID[:, cols(par)] + dot(A[ACTIVE], wpan(2, 1, par))).astype(BF)
    out_lat = pltpu.make_async_copy(A.at[SECOND], o_lat, io.at[2])
    out_lat.start()
    sg.finish(0); sg.start(1)
    rs.step(2, 5)
    rs.step(1, 4)
    rs.step(0, 4)
    sg.finish(1); sg.start(2)
    ag.drain()
    rs.step(1, 5)
    rs.step(0, 5)
    sg.finish(2); sg.start(3)

    outs = [(o_qkv, 0), (o_qkv, 1280), (o_qkv, 2560), (o_out, 0), (o_up, 0), (o_down, 0)]
    def emit(ph):
        rs.final_wait(ph)
        o_id = rs.myo()
        sel = jnp.where(o_id > 4, 1, 0)
        @pl.when(o_id == 4)
        def _():
            FIN[ph, :, 0] = FIN[ph, :, 0] + FIN[ph, :, 1]
        for xh in range(2):
            for par in range(2):
                o, off = outs[2 * ph + par]
                v = FIN[ph, 2 * xh + par, sel].astype(F32)
                o[:, off + xh * 640: off + (xh + 1) * 640] = v[0:10]
    emit(2)
    sg.finish(3); sg.start(4)
    emit(1)
    sg.finish(4)
    hi = lax.Precision.HIGHEST
    tab = lax.dot_general(own, SGS2[...], (((1,), (1,)), ((), ())), precision=hi, preferred_element_type=F32)
    vec = lax.dot_general(SGS2[16:24], own, (((1,), (1,)), ((), ())), precision=hi, preferred_element_type=F32)
    o_tab[...] = tab[0:10, 0:16]
    o_vec[...] = vec[:, 0:10]
    emit(0)
    outs = [pltpu.make_async_copy(v, o, io.at[4 + i]) for i, (v, o) in enumerate(zip((o_tab, o_vec, o_qkv, o_out, o_up, o_down), small_out))]
    for c in outs: c.start()
    rs.drain()
    out_lat.wait(); out_in.wait()
    for c in outs: c.wait()


def results_kernel(lat, inp, tab, vec, qkv, out, up, down, o_lat, o_in, o_tab, o_b1, o_g2, o_b2, o_qkv, o_out, o_up, o_down,
                   v_lat, v_in, v_tab, v_vec, v_qkv, v_out, v_up, v_down, v_b1, v_g2, v_b2, sem):
    first = pltpu.make_async_copy(vec, v_vec, sem.at[0])
    first.start()
    moves = []
    for a, v, o, n in ((inp, v_in, o_in, 4), (lat, v_lat, o_lat, 2), (qkv, v_qkv, o_qkv, 1), (out, v_out, o_out, 1), (up, v_up, o_up, 1), (down, v_down, o_down, 1), (tab, v_tab, o_tab, 1)):
        for k in range(n):
            c = a.shape[0] // n
            cut = (lambda r: r.at[pl.ds(k * c, c)]) if n > 1 else (lambda r: r)
            i = 2 + 2 * len(moves)
            moves.append((pltpu.make_async_copy(cut(a), cut(v), sem.at[i]), pltpu.make_async_copy(cut(v), cut(o), sem.at[i + 1])))
    for a, _ in moves: a.start()
    first.wait()
    small = []
    for i, (v, o) in enumerate(((v_b1, o_b1), (v_g2, o_g2), (v_b2, o_b2))):
        v[...] = v_vec[i]
        small.append(pltpu.make_async_copy(v, o, sem.at[24 + i]))
        small[-1].start()
    for a, b in moves:
        a.wait()
        b.start()
    for _, b in moves: b.wait()
    for c in small: c.wait()


def per_device(latents, script_ids, gain_table, bias_one, w_qkv, w_out, gain_two, bias_two, w_up, w_down, cotangent):
    V_ = pltpu.VMEM
    dma = pltpu.SemaphoreType.DMA
    blk = (16, CW)
    scratch = [
        V_((3, 2, 2, 4, 2, 2, 5, 16, CW), BF), V_((3, 5) + blk, BF), V_((3, 4) + blk, BF),
        V_((13, L, D), BF), V_((L, D), F32), V_((L, D), F32), V_((L, D), F32), V_((L, D), F32),
        V_((8, 256, 256), F32), V_((L, 128), F32), V_((L, 128), F32), V_((8, D), F32), V_((4, 8, D), F32),
        V_((3, 2, 4, 2, 2, 5) + blk, BF), V_((3, 3, 2, 4, 2, 2) + blk, BF),
        V_((3, 1, 2, 4, 2) + blk, BF), V_((3, 3, 2, 2) + blk, BF), V_((3, 3) + blk, BF),
        V_((3, 3, 4, 2) + blk, BF), V_((3, 1, 4) + blk, BF), V_((3, 3) + blk, BF),
        V_((3, 3, 2, 2, 2) + blk, BF), V_((3, 1, 2, 2) + blk, BF), V_((3, 3) + blk, BF),
        V_((3,) + blk, BF), V_((3, 5) + blk, BF), V_((3, 4, 2) + blk, BF),
        V_((32, D), BF), V_((32, 256), BF), V_((1, 32, 256), BF), V_((3, 32, 256), BF), V_((3, 32, 256), BF), V_((32, 384), BF), V_((3, 32, 384), BF),
        V_((2, 24, 640), F32), V_((24, 640), F32), V_((3, 24, 384), F32), V_((24, 384), F32), V_((24, 256), F32), V_((24, 256), F32), V_((3, 24, 256), F32), V_((24, 256), F32), V_((L, D), BF), V_((L, D), BF),
        V_((10, 16), BF), V_((10,), BF), V_((10,), BF), V_((10,), BF), V_((10, 3 * D), BF), V_((10, D), BF), V_((10, D), BF), V_((10, D), BF),
        V_((10, 16), F32), V_((8, 10), F32), V_((10, 3 * D), F32), V_((10, D), F32), V_((10, D), F32), V_((10, D), F32),
        dma((8,)), dma((9, 6)), dma((3,)), dma((3,)),
        dma((2,)), dma((9, 2)), dma((6,)), dma((9, 5)), dma((1,)), dma((3, 2)),
        dma((4,)), dma((4,)), dma((5,)), dma((5,)), dma((12,)),
    ]
    hbm = pl.BlockSpec(memory_space=pl.ANY)
    f32 = lambda *d: jax.ShapeDtypeStruct(d, F32)
    res = pl.pallas_call(
        block_kernel,
        out_shape=[jax.ShapeDtypeStruct((L, D), BF), f32(L, D), f32(10, 16), f32(8, 10), f32(10, 3 * D), f32(10, D), f32(10, D), f32(10, D)],
        in_specs=[hbm, hbm, pl.BlockSpec(memory_space=pltpu.VMEM)] + [hbm] * 8,
        out_specs=[hbm] * 8,
        scratch_shapes=scratch,
        compiler_params=pltpu.CompilerParams(collective_id=0, has_side_effects=True, vmem_limit_bytes=62 * 2**20),
        name="block",
    )(latents.reshape(L, D), cotangent.reshape(L, D), script_ids, gain_table, bias_one, gain_two, bias_two, w_qkv, w_out, w_up, w_down)
    o_lat, o_in, o_tab, o_b1, o_g2, o_b2, o_qkv, o_out, o_up, o_down = pl.pallas_call(
        results_kernel,
        out_shape=[jax.ShapeDtypeStruct((L, D), BF), f32(L, D), f32(10, 16), f32(10), f32(10), f32(10), f32(10, 3 * D), f32(10, D), f32(10, D), f32(10, D)],
        in_specs=[hbm] * 8,
        out_specs=[hbm] * 10,
        scratch_shapes=[V_((L, D), BF), V_((L, D), F32), V_((10, 16), F32), V_((8, 10), F32), V_((10, 3 * D), F32), V_((10, D), F32), V_((10, D), F32), V_((10, D), F32),
                        V_((10,), F32), V_((10,), F32), V_((10,), F32), dma((27,))],
        compiler_params=pltpu.CompilerParams(vmem_limit_bytes=62 * 2**20),
        name="results",
    )(*res)
    return (o_lat.reshape(1, L, D), o_in.reshape(1, L, D), o_tab, o_b1, o_qkv, o_out, o_g2, o_b2, o_up, o_down)


def solution(mesh):
    row = P(("dp", "fsdp"), None)
    vec = P(("dp", "fsdp"))
    item = P("dp", None, None)
    return jax.shard_map(
        per_device,
        mesh=mesh,
        in_specs=(item, P("dp"), row, vec, row, row, vec, vec, row, row, item),
        out_specs=(item, item, row, vec, row, row, vec, vec, row, row),
        check_vma=False,
    )
```
